32 devices in a mesh: fsdp: 4 (over z), seq: 8 (over y, x, core).
Axes of the slice: x: 2, y: 2, z: 4, core: 2. Of those that a mesh axis runs over, the one named last changes fastest.
Arguments:
- block_in: bfloat16 [3, 16384, 1280], P(None, ('fsdp', 'seq')), may hold values from -6 to 6
- cotangent: bfloat16 [3, 16384, 1280], P(None, ('fsdp', 'seq')), may hold values from -6 to 6
- lengths: int32 [3, 4, 8], P(None, 'fsdp'), may hold values from 1 to 4089, as said below
- item_weights: int32 [3, 4, 8], P(None, 'fsdp'), may hold values from 1 to 4
- first_gain: bfloat16 [1280], P('fsdp'), may hold values from 0.5 to 1.5
- first_shift: bfloat16 [1280], P('fsdp'), may hold values from -3 to 3
- entry_weight: bfloat16 [1280, 1280], P('fsdp'), may hold values from -0.15625 to 0.15625
- entry_bias: bfloat16 [1280], P('fsdp'), may hold values from -3 to 3
- middle_gain: bfloat16 [1280], P('fsdp'), may hold values from 0.5 to 1.5
- middle_shift: bfloat16 [1280], P('fsdp'), may hold values from -3 to 3
- conv_weight: bfloat16 [5, 1280, 1280], P(None, 'fsdp'), may hold values from -0.078125 to 0.078125
- conv_bias: bfloat16 [1280], P('fsdp'), may hold values from -3 to 3
- final_gain: bfloat16 [1280], P('fsdp'), may hold values from 0.5 to 1.5
- final_shift: bfloat16 [1280], P('fsdp'), may hold values from -3 to 3
- exit_weight: bfloat16 [1280, 1280], P(None, 'fsdp'), may hold values from -0.15625 to 0.15625
- exit_bias: bfloat16 [1280], P('fsdp'), may hold values from -3 to 3
Outputs:
- block_out: bfloat16 [3, 16384, 1280], P(None, ('fsdp', 'seq'))
- input_grad: bfloat16 [3, 16384, 1280], P(None, ('fsdp', 'seq'))
- first_gain_grad: float32 [1280], P('fsdp')
- first_shift_grad: float32 [1280], P('fsdp')
- entry_weight_grad: float32 [1280, 1280], P('fsdp')
- entry_bias_grad: float32 [1280], P('fsdp')
- middle_gain_grad: float32 [1280], P('fsdp')
- middle_shift_grad: float32 [1280], P('fsdp')
- conv_weight_grad: float32 [5, 1280, 1280], P(None, 'fsdp')
- conv_bias_grad: float32 [1280], P('fsdp')
- final_gain_grad: float32 [1280], P('fsdp')
- final_shift_grad: float32 [1280], P('fsdp')
- exit_weight_grad: float32 [1280, 1280], P(None, 'fsdp')
- exit_bias_grad: float32 [1280], P('fsdp')
The draws below stay inside these ranges and needn't reach their ends.
Inputs may be any that keep to these rules, and one draw needn't show every extreme that they name: For each micro-batch and group the 8 lengths sum to at most 4096, the residues past their sum being padding; one item of each group, at a place drawn from the seed, is longer than 3584 and starts within the first 512 residues; in some group the other items have length 1 and there is no padding.
All inputs are finite; a program needn't handle non-finite values.
Results may differ from the reference program's by a relative error of at most 0.0072.
Values may be sent and summed in bfloat16 or wider, within the bound.
A program may use at most 256 MiB of HBM per device.

```python
import jax
import jax.numpy as jnp
from jax import lax

D = 1280
INNER = 1280
KERNEL_TAPS = 5
DILATION_STEP = 128
MB = 3
ITEMS = 8
TOK_DEV = 512
GROUP_RESIDUES = 4096
GROUPS = 4
TOKENS = 16384


def draw_lengths(key, part):
    key = jax.random.fold_in(key, 11)
    key_short, key_pad, key_pick, key_full = jax.random.split(key, 4)
    short_most = TOK_DEV // (2 * ITEMS)
    shorts = jax.random.randint(key_short, (MB, GROUPS, ITEMS), 1, short_most + 1)
    padding = jax.random.randint(key_pad, (MB, GROUPS, 1), 0, TOK_DEV // 2)
    full_index = jax.random.randint(key_full, (), 0, MB * GROUPS)
    full_mask = jnp.arange(MB * GROUPS).reshape(MB, GROUPS, 1) == full_index
    shorts = jnp.where(full_mask, 1, shorts)
    padding = jnp.where(full_mask, 0, padding)
    chosen = jax.random.randint(key_pick, (MB, GROUPS, 1), 0, ITEMS)
    slot_mask = jnp.arange(ITEMS)[None, None, :] == chosen
    others = jnp.sum(jnp.where(slot_mask, 0, shorts), axis=2, keepdims=True)
    longest = GROUP_RESIDUES - others - padding
    return jnp.where(slot_mask, longest, shorts).astype(jnp.int32)


def place_ends(drawn, key, low, largest):
    longest = drawn.shape.index(max(drawn.shape))
    spots = []
    for shift in (0, 1):
        where = [jax.random.randint(jax.random.fold_in(key, axis), (), 0, length) for axis, length in enumerate(drawn.shape)]
        where[longest] = (where[longest] + shift) % drawn.shape[longest]
        spots.append(tuple(where))
    return drawn.at[spots[0]].set(low).at[spots[1]].set(largest)


def shard_levels(own_key, dims, cuts, least, largest):
    def one(position, blocks):
        draws = jax.random.uniform(jax.random.fold_in(jax.random.fold_in(own_key, 6), position), (blocks,), jnp.float32, least / len(cuts), largest / len(cuts))
        return jnp.repeat(jnp.exp(draws), dims[position] // blocks).reshape((-1,) + (1,) * (len(dims) - position - 1))

    level = one(*cuts[0])
    for cut in cuts[1:]:
        level = level * one(*cut)
    return level


def noise(stream_key, shape, scale, limit, shards=(), kind=jnp.bfloat16):
    array = jax.random.normal(stream_key, shape, jnp.float32) * scale
    if len(shards) > 0:
        array = shard_levels(stream_key, shape, shards, -0.22, 0.18) * array
    return jnp.clip(array, min=-limit, max=limit).astype(kind)


def setup_inputs(seed: int = 0) -> dict:
    splits = jax.random.split(jax.random.key(seed), 17)
    return {
        "block_in": noise(splits[0], (MB, TOKENS, D), 1.0, 6.0, ((1, 32),)),
        "cotangent": noise(splits[1], (MB, TOKENS, D), 1.0, 6.0, ((1, 32),)),
        "lengths": draw_lengths(jax.random.fold_in(splits[16], 71), 0),
        "item_weights": place_ends(jax.random.randint(splits[3], (MB, GROUPS, ITEMS), 1, 5), jax.random.fold_in(splits[3], 1), 1, 4).astype(jnp.int32),
        "first_gain": jnp.clip(1.0 + 0.1 * jax.random.normal(splits[4], (D,), jnp.float32), 0.5, 1.5).astype(jnp.bfloat16),
        "first_shift": noise(splits[5], (D,), 0.3, 3.0, ((0, 4),)),
        "entry_weight": noise(splits[6], (D, INNER), D ** -0.5, 0.15625, ((0, 4),)),
        "entry_bias": noise(splits[7], (INNER,), 0.3, 3.0, ((0, 4),)),
        "middle_gain": jnp.clip(1.0 + 0.1 * jax.random.normal(splits[8], (INNER,), jnp.float32), 0.5, 1.5).astype(jnp.bfloat16),
        "middle_shift": noise(splits[9], (INNER,), 0.3, 3.0, ((0, 4),)),
        "conv_weight": noise(splits[10], (KERNEL_TAPS, INNER, INNER), (KERNEL_TAPS * INNER) ** -0.5, 0.078125, ((1, 4),)),
        "conv_bias": noise(splits[11], (INNER,), 0.3, 3.0, ((0, 4),)),
        "final_gain": jnp.clip(1.0 + 0.1 * jax.random.normal(splits[12], (INNER,), jnp.float32), 0.5, 1.5).astype(jnp.bfloat16),
        "final_shift": noise(splits[13], (INNER,), 0.3, 3.0, ((0, 4),)),
        "exit_weight": noise(splits[14], (INNER, D), INNER ** -0.5, 0.15625, ((1, 4),)),
        "exit_bias": noise(splits[15], (D,), 0.3, 3.0, ((0, 4),)),
    }


@jax.custom_vjp
def low(v):
    return lax.optimization_barrier(v.astype(jnp.bfloat16)).astype(jnp.float32)

@jax.custom_vjp
def low_back(v):
    return v

def low_keep(v):
    return (low(v), None)

def low_pass(kept, grad):
    return (grad,)

def back_keep(v):
    return (v, None)

def back_low(kept, grad):
    return (low(grad),)
low.defvjp(low_keep, low_pass)
low_back.defvjp(back_keep, back_low)
eps_norm = 1e-05

def norm_act(values, scale_vec, shift_vec):
    row_mean = lax.optimization_barrier(jnp.mean(values, axis=-1, keepdims=True))
    centred = values - row_mean
    spread = lax.optimization_barrier(jnp.mean(centred * centred, axis=-1, keepdims=True))
    return jax.nn.gelu(centred * lax.rsqrt(spread + eps_norm) * scale_vec + shift_vec, approximate=False)

def product(left, right):
    return jnp.dot(left, right, precision=lax.Precision.HIGHEST, preferred_element_type=jnp.float32)

def item_of(item_lengths):
    half_reach = KERNEL_TAPS // 2
    ends = jnp.cumsum(item_lengths).astype(jnp.int32)
    residue_position = jnp.arange(GROUP_RESIDUES + 2 * half_reach * DILATION_STEP, dtype=jnp.int32) - half_reach * DILATION_STEP
    inside = (residue_position >= 0) & (residue_position < GROUP_RESIDUES)
    seg_all = lax.optimization_barrier(jnp.sum((residue_position[:, None] >= ends[None, :]).astype(jnp.int32), axis=1)).astype(jnp.int32)
    return jnp.where(inside, seg_all, -1).astype(jnp.int32)

def tap_masks(segment_extended):
    half_reach = KERNEL_TAPS // 2
    middle_tap = segment_extended[half_reach * DILATION_STEP:half_reach * DILATION_STEP + GROUP_RESIDUES]
    mask_list = []
    for kernel_tap_index in range(KERNEL_TAPS):
        segment_tapped = segment_extended[kernel_tap_index * DILATION_STEP:kernel_tap_index * DILATION_STEP + GROUP_RESIDUES]
        keep_mask = (segment_tapped == middle_tap) & (segment_tapped >= 0) & (segment_tapped < ITEMS)
        mask_list.append(keep_mask.astype(jnp.float32))
    return mask_list

def block(params, stream_in, mask_list):
    gain_one, shift_one, weight_in, bias_in, gain_two, shift_two, weight_conv, bias_conv, gain_three, shift_three, weight_out, bias_out = params
    half_reach = KERNEL_TAPS // 2
    act_one = low(norm_act(stream_in, gain_one, shift_one))
    inner_one = low_back(product(act_one, weight_in) + bias_in)
    second_activation = low(norm_act(inner_one, gain_two, shift_two))
    padded_rows = jnp.pad(second_activation, ((half_reach * DILATION_STEP, half_reach * DILATION_STEP), (0, 0)))
    shifted_tap_rows = jnp.concatenate([padded_rows[kernel_tap_index * DILATION_STEP:kernel_tap_index * DILATION_STEP + GROUP_RESIDUES] * mask_list[kernel_tap_index][:, None] for kernel_tap_index in range(KERNEL_TAPS)], axis=1)
    inner_two = low(low_back(product(shifted_tap_rows, weight_conv.reshape(KERNEL_TAPS * INNER, INNER)) + bias_conv))
    act_three = low(norm_act(inner_two, gain_three, shift_three))
    branch = low_back(product(act_three, weight_out) + bias_out)
    return stream_in + branch

def reference(block_in, cotangent, lengths, item_weights, first_gain, first_shift, entry_weight, entry_bias, middle_gain, middle_shift, conv_weight, conv_bias, final_gain, final_shift, exit_weight, exit_bias):
    params = tuple((value.astype(jnp.float32) for value in (first_gain, first_shift, entry_weight, entry_bias, middle_gain, middle_shift, conv_weight, conv_bias, final_gain, final_shift, exit_weight, exit_bias)))
    half_reach = KERNEL_TAPS // 2
    inputs = block_in.astype(jnp.float32).reshape(MB * GROUPS, GROUP_RESIDUES, D)
    pulls = cotangent.astype(jnp.float32).reshape(MB * GROUPS, GROUP_RESIDUES, D)
    all_lengths = lengths.reshape(MB * GROUPS, ITEMS)
    all_weights = item_weights.reshape(MB * GROUPS, ITEMS)

    def one_stream(grads, packed):
        stream_in, stream_pull, item_lengths, weight_row = packed
        segment_extended = item_of(item_lengths)
        mask_list = tap_masks(segment_extended)
        middle_tap = segment_extended[half_reach * DILATION_STEP:half_reach * DILATION_STEP + GROUP_RESIDUES]
        match = middle_tap[:, None] == jnp.arange(ITEMS, dtype=jnp.int32)[None, :]
        row_scale = lax.optimization_barrier(jnp.sum(jnp.where(match, weight_row[None, :], 0), axis=1)).astype(jnp.float32)
        result, pullback = jax.vjp(lambda prm, value: block(prm, value, mask_list), params, stream_in)
        grad_params, grad_input = pullback(stream_pull * row_scale[:, None])
        grads = jax.tree.map(lambda left, right: left + right, grads, grad_params)
        return (grads, (result.astype(jnp.bfloat16), grad_input.astype(jnp.bfloat16)))
    zeros = tuple((jnp.zeros(value.shape, jnp.float32) for value in params))
    grads, (outputs, input_grads) = lax.scan(one_stream, zeros, (inputs, pulls, all_lengths, all_weights))
    return (outputs.reshape(MB, TOKENS, D), input_grads.reshape(MB, TOKENS, D), grads[0], grads[1], grads[2], grads[3], grads[4], grads[5], grads[6], grads[7], grads[8], grads[9], grads[10], grads[11])
```

```python
import functools
import math

import jax
import jax.numpy as jnp
from jax import lax
from jax.experimental import pallas as pl
from jax.experimental.pallas import tpu as pltpu
from jax.sharding import PartitionSpec as P

KERNEL_TAPS = 5
DILATION_STEP = 128


eps_norm = 1e-05

MESH = pl.DeviceIdType.MESH
BF = jnp.bfloat16
F32 = jnp.float32
LANES = 128
VMEM_MOST = 60 << 20
NN = (((1,), (0,)), ((), ()))
NT = (((1,), (1,)), ((), ()))
TN = (((0,), (0,)), ((), ()))
ROOT_HALF = math.sqrt(0.5)
PHI_SCALE = 1.0 / math.sqrt(2.0 * math.pi)
EXP2_SCALE = -0.5 * math.log2(math.e)
G1, S1, BE, G2, S2, BC, G3, S3, BX = range(9)
VECTORS = 16


def mm(left, right, dims):
    return lax.dot_general(left, right, dims, preferred_element_type=F32)


def normed(v):
    centred = v - jnp.mean(v, axis=-1, keepdims=True)
    inverse = lax.rsqrt(jnp.mean(centred * centred, axis=-1, keepdims=True) + eps_norm)
    return centred * inverse, inverse


def phi(u):
    return 0.5 + 0.5 * lax.erf(u * ROOT_HALF)


def slope(u, big_phi):
    return big_phi + u * (PHI_SCALE * jnp.exp2(u * u * EXP2_SCALE))


def fold(tile):
    return jnp.sum(tile.reshape(tile.shape[0] // 8, 8, tile.shape[1]), axis=0)


def pull_back(t, n, inverse, gain):
    at = t * gain
    return (
        at - jnp.mean(at, axis=-1, keepdims=True) - n * jnp.mean(at * n, axis=-1, keepdims=True)
    ) * inverse


def span(i, size):
    return pl.ds(pl.multiple_of(i * size, size), size)


def for_each(count, step):
    lax.fori_loop(0, count, lambda i, carry: (step(i), carry)[1], 0)


def wide(mask, width):
    return jnp.concatenate([mask] * (width // LANES), axis=1)


class Place:
    def __init__(self):
        self.z = lax.axis_index("fsdp")
        self.s = lax.axis_index("seq")
        self.nz = lax.axis_size("fsdp")
        self.ns = lax.axis_size("seq")
        s = self.s
        self.c = lax.rem(s, 2)
        self.x = lax.rem(s // 2, 2)
        self.y = s // 4
        self.q = s // 2
        self.core = (self.z, s + 1 - 2 * self.c)
        self.px = (self.z, s + 2 - 4 * self.x)
        self.py = (self.z, s + 4 - 8 * self.y)
        self.left = (self.z, lax.rem(s + self.ns - 1, self.ns))
        self.right = (self.z, lax.rem(s + 1, self.ns))

    def up(self, j):
        return lax.rem(self.z + j, self.nz)

    def down(self, j):
        return lax.rem(self.z + self.nz - j, self.nz)

    def above(self, j):
        return (self.up(j), self.s)

    def greet(self):
        peers = [self.core, self.px, self.py, self.left, self.right]
        peers += [self.above(j) for j in range(1, self.nz)]
        barrier = pltpu.get_barrier_semaphore()
        for peer in peers:
            pl.semaphore_signal(barrier, inc=1, device_id=peer, device_id_type=MESH)
        pl.semaphore_wait(barrier, len(peers))


def send(src, dst, send_sem, recv_sem, peer):
    return pltpu.make_async_remote_copy(
        src_ref=src,
        dst_ref=dst,
        send_sem=send_sem,
        recv_sem=recv_sem,
        device_id=peer,
        device_id_type=MESH,
    )


def find_items(place, lengths, weights, item, scale, micro, rows, halo):
    extent = rows + 2 * halo
    count = lengths.shape[1]
    for m in range(micro):
        position = lax.broadcasted_iota(jnp.int32, (extent, LANES), 0) + (place.s * rows - halo)
        found = jnp.zeros((extent, LANES), jnp.int32)
        end = jnp.int32(0)
        ends = []
        for j in range(count):
            end = end + lengths[m, j]
            ends.append(end)
            found = found + jnp.where(position >= end, 1, 0)
        found = jnp.where(
            (position >= 0) & (position < place.ns * rows) & (found < count), found, -1
        )
        item[m] = found
        if scale is not None:
            own = found[halo : halo + rows]
            total = jnp.zeros((rows, LANES), jnp.int32)
            for j in range(count):
                total = total + jnp.where(own == j, weights[m, j], 0)
            scale[m] = total.astype(F32)


def keep(item, m, tap, rows, halo):
    own = item[m, halo : halo + rows]
    first = pl.multiple_of(halo + (tap - KERNEL_TAPS // 2) * DILATION_STEP, DILATION_STEP)
    other = item[m, pl.ds(first, rows)]
    return jnp.where((own == other) & (own >= 0), 1.0, 0.0).astype(F32)


TAP_ORDER = (2, 1, 3, 0, 4)


def forward_kernel(
    block_in, cotangent, lengths, weights, vectors, entry, conv, exit_t,
    gathered, act_one, inner_one, ext_two, act_three, grad_two, grad_branch, params, sums,
    held, total, grad_three, tap_w, one, pulled, item, scale, parts,
    vec_send, vec_recv, z_send, z_recv, a_send, a_recv, b_send, b_recv, c_send, c_recv,
    halo_send, halo_recv, load_sem, store_sem, tap_sem,
):
    place = Place()
    micro, rows, width = block_in.shape
    halo = (KERNEL_TAPS // 2) * DILATION_STEP
    z, c, q, x, y, nz = place.z, place.c, place.q, place.x, place.y, place.nz
    shard = entry.shape[0]
    piece = shard // 4
    half = width // 2
    taps = conv.shape[0] + 2
    order = [0, 1] + [2 + k for k in TAP_ORDER]
    tile_n = 256
    tile_r = 64
    others = range(1, nz)

    loads = []
    for m in range(micro):
        loads.append(pltpu.make_async_copy(block_in.at[m], one.at[m], load_sem.at[0, m]))
        loads.append(pltpu.make_async_copy(cotangent.at[m], pulled.at[m], load_sem.at[1, m]))
    for load in loads:
        load.start()
    own = []
    for t in range(taps):
        src = entry if t == 0 else exit_t if t == 1 else conv.at[t - 2]
        own.append((src, pltpu.make_async_copy(src, gathered.at[t, pl.ds(z * shard, shard)], tap_sem.at[2, t])))
    place.greet()

    cols = pl.ds(pl.multiple_of(c * half, LANES), half)

    def at(t, zz, first, count):
        return gathered.at[t, pl.ds(zz * shard + first * piece, count * piece), cols]

    vec_copies = [
        send(vectors, parts.at[z], vec_send.at[j - 1], vec_recv.at[j - 1], place.above(j))
        for j in others
    ]
    for copy in vec_copies:
        copy.start()
    parts[z] = vectors[...]

    z_copies, a_copies, b_copies, c_copies = {}, {}, {}, {}

    def spread_z(i):
        t = order[i]
        src = own[t][0]
        for j in others:
            copy = send(src.at[pl.ds(q * piece, piece), cols], at(t, z, q, 1), z_send.at[t, j - 1], z_recv.at[t, j - 1], place.above(j))
            copy.start()
            z_copies[t, j] = copy
        own[t][1].start()

    def first_axis(i):
        return place.px if i % 2 == 0 else place.py

    def spread_a(i):
        t = order[i]
        for j in others:
            z_copies[t, j].wait_recv()
            block = at(t, place.down(j), q, 1)
            copy = send(block, block, a_send.at[t, j - 1], a_recv.at[t, j - 1], first_axis(i))
            copy.start()
            a_copies[t, j] = copy

    def spread_b(i):
        t = order[i]
        for j in others:
            a_copies[t, j].wait_recv()
            zz = place.down(j)
            if i % 2 == 0:
                blocks = [at(t, zz, 2 * y, 2)]
                peer = place.py
            else:
                blocks = [at(t, zz, x, 1), at(t, zz, x + 2, 1)]
                peer = place.px
            copies = []
            for n, block in enumerate(blocks):
                copy = send(block, block, b_send.at[t, j - 1, n], b_recv.at[t, j - 1, n], peer)
                copy.start()
                copies.append(copy)
            b_copies[t, j] = copies

    def spread_c(i):
        t = order[i]
        for j in others:
            for copy in b_copies[t, j]:
                copy.wait_recv()
            block = at(t, place.down(j), 0, 4)
            copy = send(block, block, c_send.at[t, j - 1], c_recv.at[t, j - 1], place.core)
            copy.start()
            c_copies[t, j] = copy

    tap_loads = {}

    def arrived(i):
        t = order[i]
        for j in others:
            c_copies[t, j].wait_recv()
        own[t][1].wait()
        tap_loads[i] = pltpu.make_async_copy(gathered.at[t], tap_w.at[i % 2], tap_sem.at[i % 2, 0])
        tap_loads[i].start()

    def tick(i):
        if i + 3 < taps:
            spread_z(i + 3)
        if i < taps:
            spread_a(i)
        if 0 <= i - 1 < taps:
            spread_b(i - 1)
        if 0 <= i - 2 < taps:
            spread_c(i - 2)
        if 0 <= i - 3 < taps:
            arrived(i - 3)

    for i in range(3):
        spread_z(i)

    find_items(place, lengths, weights, item, scale, micro, rows, halo)
    for copy in vec_copies:
        copy.wait_recv()
    stacked_parts = [parts[zz].astype(F32)[:, :shard] for zz in range(nz)]
    params[...] = jnp.concatenate(stacked_parts, axis=1)

    def vec(r):
        return params[r : r + 1, :]

    sums[...] = jnp.zeros_like(sums)

    def norm_one(m):
        def step(i):
            rs = span(i, tile_r)
            n, _ = normed(one[m, rs, :].astype(F32))
            u = n * vec(G1) + vec(S1)
            one[m, rs, :] = (u * phi(u)).astype(BF)

        for_each(rows // tile_r, step)

    stores = []

    def store(src, dst):
        copy = pltpu.make_async_copy(src, dst, store_sem.at[len(stores)])
        copy.start()
        stores.append(copy)
        return copy

    one_out = []
    for m in range(micro):
        loads[2 * m].wait()
        norm_one(m)
        one_out.append(store(one.at[m], act_one.at[m]))
    tick(0)

    def pull(m):
        def step(i):
            rs = span(i, tile_r)
            value = (pulled[m, rs, :].astype(F32) * wide(scale[m, rs, :], width)).astype(BF)
            pulled[m, rs, :] = value
            sums[3] += fold(value.astype(F32))

        for_each(rows // tile_r, step)

    branch_out = []
    for m in range(micro):
        loads[2 * m + 1].wait()
        pull(m)
        branch_out.append(store(pulled.at[m], grad_branch.at[m]))
    tick(1)
    tick(2)
    tick(3)

    def halo_right(m):
        return send(held.at[m, pl.ds(rows, halo)], held.at[m, pl.ds(0, halo)], halo_send.at[0, m], halo_recv.at[0, m], place.right)

    def halo_left(m):
        return send(held.at[m, pl.ds(halo, halo)], held.at[m, pl.ds(rows + halo, halo)], halo_send.at[1, m], halo_recv.at[1, m], place.left)

    at_start, at_end = place.s == 0, place.s == place.ns - 1

    @pl.when(at_start)
    def _():
        held[:, 0:halo, :] = jnp.zeros((micro, halo, width), BF)

    @pl.when(at_end)
    def _():
        held[:, rows + halo :, :] = jnp.zeros((micro, halo, width), BF)

    tap_loads[0].wait()
    inner_out = []
    for m in range(micro):

        def entry_step(i, m=m):
            ns = span(i, tile_n)
            total[m, :, ns] = mm(one[m], tap_w[0, :, ns], NN) + params[BE : BE + 1, ns]

        for_each(width // tile_n, entry_step)
        inner_out.append(store(total.at[m], inner_one.at[m]))

        def norm_two(i, m=m):
            rs = span(i, tile_r)
            n, _ = normed(total[m, rs, :])
            u = n * vec(G2) + vec(S2)
            held[m, pl.ds(pl.multiple_of(halo + i * tile_r, tile_r), tile_r), :] = (u * phi(u)).astype(BF)

        for_each(rows // tile_r, norm_two)

        @pl.when(jnp.logical_not(at_end))
        def _(m=m):
            halo_right(m).start()

        @pl.when(jnp.logical_not(at_start))
        def _(m=m):
            halo_left(m).start()

        if m == 0:
            tick(4)

    tap_loads[1].wait()

    def exit_step(i):
        m, ns = i // (width // tile_n), span(lax.rem(i, width // tile_n), tile_n)
        grad_three[m, :, ns] = mm(pulled[m], tap_w[1, :, ns], NN)

    for_each(micro * (width // tile_n), exit_step)
    tick(5)

    for copy in inner_out:
        copy.wait()

    def conv_tap(i, first):
        tap = TAP_ORDER[i - 2]
        slot = i % 2
        tap_loads[i].wait()
        start = halo + (tap - KERNEL_TAPS // 2) * DILATION_STEP

        def step(n):
            m, ns = n // (width // tile_n), span(lax.rem(n, width // tile_n), tile_n)
            got = mm(held[m, pl.ds(start, rows), :], tap_w[slot, :, ns], NN)
            got = got * wide(keep(item, m, tap, rows, halo), tile_n)
            if first:
                total[m, :, ns] = got
            else:
                total[m, :, ns] += got

        for_each(micro * (width // tile_n), step)

    ext_out = []
    for i in range(2, taps):
        if i == 3:
            for m in range(micro):

                @pl.when(jnp.logical_not(at_start))
                def _(m=m):
                    halo_right(m).wait_recv()

                @pl.when(jnp.logical_not(at_end))
                def _(m=m):
                    halo_left(m).wait_recv()

                ext_out.append(store(held.at[m], ext_two.at[m]))
        conv_tap(i, i == 2)
        if i + 4 <= taps + 2:
            tick(i + 4)

    for copy in one_out + branch_out:
        copy.wait()
    for m in range(micro):

        def norm_three(i, m=m):
            rs = span(i, tile_r)
            v = (total[m, rs, :] + vec(BC)).astype(BF).astype(F32)
            n, inverse = normed(v)
            u = n * vec(G3) + vec(S3)
            big_phi = phi(u)
            one[m, rs, :] = (u * big_phi).astype(BF)
            t = grad_three[m, rs, :] * slope(u, big_phi)
            sums[1] += fold(t * n)
            sums[2] += fold(t)
            grad = pull_back(t, n, inverse, vec(G3)).astype(BF)
            pulled[m, rs, :] = grad
            sums[0] += fold(grad.astype(F32))

        for_each(rows // tile_r, norm_three)
        store(one.at[m], act_three.at[m])
        store(pulled.at[m], grad_two.at[m])

    for copy in stores:
        if not any(copy is done for done in one_out + branch_out + inner_out):
            copy.wait()
    for m in range(micro):

        @pl.when(jnp.logical_not(at_end))
        def _(m=m):
            halo_right(m).wait_send()

        @pl.when(jnp.logical_not(at_start))
        def _(m=m):
            halo_left(m).wait_send()

    for copy in vec_copies:
        copy.wait_send()
    for copies in (z_copies, a_copies, c_copies):
        for copy in copies.values():
            copy.wait_send()
    for copies in b_copies.values():
        for copy in copies:
            copy.wait_send()


def forward(block_in, cotangent, lengths, weights, vectors, entry, conv, exit_t):
    micro, rows, width = block_in.shape
    halo = (KERNEL_TAPS // 2) * DILATION_STEP
    taps = conv.shape[0] + 2
    nz = lax.axis_size("fsdp")
    extent = rows + 2 * halo
    shape = jax.ShapeDtypeStruct
    anywhere = pl.BlockSpec(memory_space=pl.ANY)
    near = pl.BlockSpec(memory_space=pltpu.VMEM)
    scalars = pl.BlockSpec(memory_space=pltpu.SMEM)
    dma = pltpu.SemaphoreType.DMA
    flops = 2 * micro * rows * width * width * taps
    return pl.pallas_call(
        forward_kernel,
        out_shape=(
            shape((taps, width, width), BF),
            shape((micro, rows, width), BF),
            shape((micro, rows, width), F32),
            shape((micro, extent, width), BF),
            shape((micro, rows, width), BF),
            shape((micro, rows, width), BF),
            shape((micro, rows, width), BF),
            shape((VECTORS, width), F32),
            shape((4, 8, width), F32),
        ),
        in_specs=[anywhere, anywhere, scalars, scalars, near, anywhere, anywhere, anywhere],
        out_specs=(anywhere,) * 7 + (near, near),
        scratch_shapes=[
            pltpu.VMEM((micro, extent, width), BF),
            pltpu.VMEM((micro, rows, width), F32),
            pltpu.VMEM((micro, rows, width), F32),
            pltpu.VMEM((2, width, width), BF),
            pltpu.VMEM((micro, rows, width), BF),
            pltpu.VMEM((micro, rows, width), BF),
            pltpu.VMEM((micro, extent, LANES), jnp.int32),
            pltpu.VMEM((micro, rows, LANES), F32),
            pltpu.VMEM((nz,) + vectors.shape, BF),
            dma((nz - 1,)),
            dma((nz - 1,)),
            dma((taps, nz - 1)),
            dma((taps, nz - 1)),
            dma((taps, nz - 1)),
            dma((taps, nz - 1)),
            dma((taps, nz - 1, 2)),
            dma((taps, nz - 1, 2)),
            dma((taps, nz - 1)),
            dma((taps, nz - 1)),
            dma((2, micro)),
            dma((2, micro)),
            dma((2, micro)),
            dma((6 * micro,)),
            dma((3, taps)),
        ],
        compiler_params=pltpu.CompilerParams(
            collective_id=1, has_side_effects=True, vmem_limit_bytes=VMEM_MOST
        ),
        cost_estimate=pl.CostEstimate(flops=flops, bytes_accessed=80 << 20, transcendentals=0),
        name="gather_and_forward",
    )(block_in, cotangent, lengths, weights, vectors, entry, conv, exit_t)


BACK_ORDER = (2, 1, 3, 0, 4)


def backward_kernel(
    block_in, cotangent, lengths, weights, params, sums_in, gathered, act_one, inner_one, ext_two, act_three, grad_two, grad_branch,
    block_out, input_grad, shares, vec_out,
    held, grads, total, buf, inner, item, scale, sums,
    out_core, own, in_core, in_a, out_a, keep_a, in_b, out_b, keep_b, in_z, out_z, keep_z, final,
    vec_part, vec_in,
    core_send, core_recv, a_send, a_recv, b_send, b_recv, z_send, z_recv, f_own, f_send, f_recv, g_send, g_recv, h_send, h_recv,
    halo_send, halo_recv, vec_send, vec_recv, load_sem, inner_sem, store_sem, credit,
):
    place = Place()
    micro, rows, width = block_in.shape
    halo = (KERNEL_TAPS // 2) * DILATION_STEP
    z, c, q, x, y, nz = place.z, place.c, place.q, place.x, place.y, place.nz
    taps, shard, _ = shares.shape
    piece = shard // 4
    half = width // 2
    order = [1] + [2 + k for k in BACK_ORDER] + [0]
    tile_n = 256
    tile_m = 256
    tile_r = 64
    chunk = inner.shape[1]
    across = width // tile_n
    others = range(1, nz)
    at_start, at_end = place.s == 0, place.s == place.ns - 1
    low, high = pl.ds(0, micro * rows), pl.ds(micro * rows, micro * rows)
    tap_rows = pl.ds(micro * rows, width)

    def load(src, dst, n):
        copy = pltpu.make_async_copy(src, dst, load_sem.at[n])
        copy.start()
        return copy

    branch_in = [load(grad_branch.at[m], buf.at[pl.ds(m * rows, rows)], m) for m in range(micro)]
    three_in = [load(act_three.at[m], buf.at[pl.ds((micro + m) * rows, rows)], micro + m) for m in range(micro)]
    two_in = load(ext_two, held, 2 * micro)
    grads_in = load(grad_two, grads.at[:, pl.ds(halo, rows)], 2 * micro + 1)
    place.greet()

    halo_right = send(grad_two.at[:, pl.ds(rows - halo, halo)], grads.at[:, pl.ds(0, halo)], halo_send.at[0], halo_recv.at[0], place.right)
    halo_left = send(grad_two.at[:, pl.ds(0, halo)], grads.at[:, pl.ds(rows + halo, halo)], halo_send.at[1], halo_recv.at[1], place.left)

    @pl.when(jnp.logical_not(at_end))
    def _():
        halo_right.start()

    @pl.when(jnp.logical_not(at_start))
    def _():
        halo_left.start()

    @pl.when(at_start)
    def _():
        grads[:, 0:halo, :] = jnp.zeros((micro, halo, width), BF)

    @pl.when(at_end)
    def _():
        grads[:, rows + halo :, :] = jnp.zeros((micro, halo, width), BF)

    find_items(place, lengths, weights, item, scale, micro, rows, halo)
    sums[...] = jnp.zeros_like(sums)
    for n, r in enumerate((BC, G3, S3, BX)):
        sums[r] = sums_in[n]

    def vec(r):
        return params[r : r + 1, :]

    my_cols = pl.ds(pl.multiple_of(c * half, LANES), half)
    core_cols = pl.ds(pl.multiple_of(half - c * half, LANES), half)
    sent = {}

    def axes(i):
        if i % 2 == 0:
            return x, y, place.px, place.py
        return y, x, place.py, place.px

    def block_rows(i, zz, other, mine):
        step_mine, step_other = (piece, 2 * piece) if i % 2 == 0 else (2 * piece, piece)
        return pl.ds(pl.multiple_of(zz * shard + other * step_other + mine * step_mine, 16), piece)

    def stage_core(i):
        copy = send(out_core, in_core, core_send.at[i], core_recv.at[i], place.core)
        if i > 0:
            pl.semaphore_wait(credit, 1)
        copy.start()
        sent["core", i] = copy

    def stage_a(i):
        mine, _, peer, _ = axes(i)
        slot = i % 2
        sent["core", i].wait_recv()
        if i >= 2:
            sent["a", i - 2].wait_send()

        def step(n):
            zz, other = n // 2, lax.rem(n, 2)
            kept = block_rows(i, zz, other, mine)
            gone = block_rows(i, zz, other, 1 - mine)
            out_a[slot, n] = (own[gone, :].astype(F32) + in_core[gone, :].astype(F32)).astype(BF)
            keep_a[slot, n] = (own[kept, :].astype(F32) + in_core[kept, :].astype(F32)).astype(keep_a.dtype)

        for_each(2 * nz, step)
        copy = send(out_a.at[slot], in_a.at[i], a_send.at[i], a_recv.at[i], peer)
        copy.start()
        sent["a", i] = copy
        if i < taps - 1:
            pl.semaphore_signal(credit, inc=1, device_id=place.core, device_id_type=MESH)

    def stage_b(i):
        _, mine, _, peer = axes(i)
        slot = i % 2
        sent["a", i].wait_recv()
        if i >= 2:
            sent["b", i - 2].wait_send()

        def step(zz):
            kept, gone = 2 * zz + mine, 2 * zz + 1 - mine
            out_b[slot, zz] = (keep_a[slot, gone].astype(F32) + in_a[i, gone].astype(F32)).astype(BF)
            keep_b[slot, zz] = keep_a[slot, kept].astype(F32) + in_a[i, kept].astype(F32)

        for_each(nz, step)
        copy = send(out_b.at[slot], in_b.at[i], b_send.at[i], b_recv.at[i], peer)
        copy.start()
        sent["b", i] = copy

    def stage_z(i):
        slot = i % 2
        sent["b", i].wait_recv()
        for j in range(nz):
            if j > 0 and i >= 2:
                sent["z", i - 2, j].wait_send()
            zz = place.up(j)
            value = keep_b[slot, zz] + in_b[i, zz].astype(F32)
            if j == 0:
                keep_z[slot] = value
                continue
            out_z[slot, j - 1] = value.astype(BF)
            copy = send(out_z.at[slot, j - 1], in_z.at[i, j - 1], z_send.at[i, j - 1], z_recv.at[i, j - 1], place.above(j))
            copy.start()
            sent["z", i, j] = copy

    def share_at(i, first, count):
        return shares.at[order[i], pl.ds(pl.multiple_of(first * piece, 16), count * piece), my_cols]

    def stage_final(i):
        slot = i % 2
        value = keep_z[slot]
        for j in others:
            sent["z", i, j].wait_recv()
            value = value + in_z[i, j - 1].astype(F32)
        if i >= 2:
            sent["f", i - 2].wait_send()
        final[slot] = value.astype(BF)
        here = pltpu.make_async_copy(final.at[slot], share_at(i, q, 1), f_own.at[i])
        here.start()
        copy = send(final.at[slot], share_at(i, q, 1), f_send.at[i], f_recv.at[i], axes(i)[2])
        copy.start()
        sent["f", i] = copy
        sent["own", i] = here

    def stage_g(i):
        sent["own", i].wait()
        sent["f", i].wait_recv()
        if i % 2 == 0:
            blocks = [share_at(i, 2 * y, 2)]
        else:
            blocks = [share_at(i, x, 1), share_at(i, x + 2, 1)]
        for n, block in enumerate(blocks):
            copy = send(block, block, g_send.at[i, n], g_recv.at[i, n], axes(i)[3])
            copy.start()
            sent["g", i, n] = copy

    def stage_h(i):
        for n in range(1 + i % 2):
            sent["g", i, n].wait_recv()
        block = share_at(i, 0, 4)
        copy = send(block, block, h_send.at[i], h_recv.at[i], place.core)
        copy.start()
        sent["h", i] = copy

    def tick(i):
        for back, stage in ((4, stage_h), (3, stage_g), (2, stage_final), (1, stage_z), (0, stage_b)):
            if 0 <= i - back < taps:
                stage(i - back)

    def weight_grad(i, product):
        if i > 0:
            sent["core", i - 1].wait_send()

        def far(n):
            ms = span(n, tile_m)
            out_core[ms, :] = product(ms, core_cols).astype(BF)

        for_each(width // tile_m, far)
        stage_core(i)

        def near(n):
            ms = span(n, tile_m)
            own[ms, :] = product(ms, my_cols).astype(own.dtype)

        for_each(width // tile_m, near)
        stage_a(i)

    for copy in branch_in + three_in:
        copy.wait()
    weight_grad(0, lambda ms, ns: mm(buf[low, ms], buf[high, ns], TN))

    def load_tap(k):
        return load(gathered.at[2 + k], buf.at[tap_rows], 2 * micro + 2)

    tap_in = load_tap(BACK_ORDER[0])
    two_in.wait()
    grads_in.wait()

    def back_tap(n, k, first):
        start = halo - (k - KERNEL_TAPS // 2) * DILATION_STEP

        def step(i):
            m, j = i // across, lax.rem(i, across)
            ns = span(j, tile_n)
            rs = pl.ds(pl.multiple_of(micro * rows + j * tile_n, tile_n), tile_n)
            got = mm(grads[m, pl.ds(start, rows), :], buf[rs, :], NT)
            got = got * wide(keep(item, m, KERNEL_TAPS - 1 - k, rows, halo), tile_n)
            if first:
                total[m, :, ns] = got
            else:
                total[m, :, ns] += got

        for_each(micro * across, step)

    for n, k in enumerate(BACK_ORDER):

        def masked(i, k=k):
            m, r = i // (rows // 128), lax.rem(i, rows // 128)
            first = pl.multiple_of(halo + r * 128, 128)
            tap_first = pl.multiple_of(first + (k - KERNEL_TAPS // 2) * DILATION_STEP, 128)
            mine = item[m, pl.ds(first, 128)]
            mask = jnp.where((mine == item[m, pl.ds(tap_first, 128)]) & (mine >= 0), 1.0, 0.0)
            value = grads[m, pl.ds(first, 128), :].astype(F32) * wide(mask, width)
            buf[span(i, 128), :] = value.astype(BF)

        for_each(micro * rows // 128, masked)
        start = halo + (k - KERNEL_TAPS // 2) * DILATION_STEP

        def product(ms, ns, start=start):
            got = None
            for m in range(micro):
                part = mm(held[m, pl.ds(start, rows), ms], buf[pl.ds(m * rows, rows), ns], TN)
                got = part if got is None else got + part
            return got

        weight_grad(n + 1, product)
        if n == 1:

            @pl.when(jnp.logical_not(at_start))
            def _():
                halo_right.wait_recv()

            @pl.when(jnp.logical_not(at_end))
            def _():
                halo_left.wait_recv()

        tap_in.wait()
        back_tap(n, k, n == 0)
        if n + 1 < len(BACK_ORDER):
            tap_in = load_tap(BACK_ORDER[n + 1])
        tick(n)

    entry_in = load(gathered.at[0], buf.at[tap_rows], 2 * micro + 2)
    one_in = [load(act_one.at[m], held.at[m, pl.ds(0, rows)], m) for m in range(micro)]
    block_load = [load(block_in.at[m], held.at[m, pl.ds(rows, rows)], micro + m) for m in range(micro)]
    pull_in = load(cotangent, grads.at[:, pl.ds(0, rows)], 2 * micro)
    chunks = micro * rows // chunk
    per_block = rows // chunk

    def fetch(n):
        m, r = n // per_block, lax.rem(n, per_block)
        slot = lax.rem(n, 2)
        return pltpu.make_async_copy(inner_one.at[m, span(r, chunk)], inner.at[slot], inner_sem.at[slot])

    fetch(0).start()

    def norm_two(n):
        m, r = n // per_block, lax.rem(n, per_block)
        slot = lax.rem(n, 2)

        @pl.when(n + 1 < chunks)
        def _():
            fetch(n + 1).start()

        fetch(n).wait()
        for part in range(chunk // tile_r):
            rs = pl.ds(pl.multiple_of(r * chunk + part * tile_r, tile_r), tile_r)
            norm, inverse = normed(inner[slot, part * tile_r : (part + 1) * tile_r, :])
            u = norm * vec(G2) + vec(S2)
            t = total[m, rs, :] * slope(u, phi(u))
            sums[G2] += fold(t * norm)
            sums[S2] += fold(t)
            grad = pull_back(t, norm, inverse, vec(G2)).astype(BF)
            buf[pl.ds(pl.multiple_of(n * chunk + part * tile_r, tile_r), tile_r), :] = grad
            sums[BE] += fold(grad.astype(F32))

    for_each(chunks, norm_two)
    tick(5)

    for copy in one_in:
        copy.wait()

    def entry_product(ms, ns):
        got = None
        for m in range(micro):
            part = mm(held[m, pl.ds(0, rows), ms], buf[pl.ds(m * rows, rows), ns], TN)
            got = part if got is None else got + part
        return got

    weight_grad(taps - 1, entry_product)
    three_again = [load(act_three.at[m], held.at[m, pl.ds(0, rows)], m) for m in range(micro)]

    entry_in.wait()

    def entry_step(i):
        m, j = i // across, lax.rem(i, across)
        rs = pl.ds(pl.multiple_of(micro * rows + j * tile_n, tile_n), tile_n)
        total[m, :, span(j, tile_n)] = mm(buf[span(m, rows), :], buf[rs, :], NT)

    for_each(micro * across, entry_step)
    exit_in = load(gathered.at[1], buf.at[tap_rows], 2 * micro + 2)
    tick(6)
    pull_in.wait()
    stores = []
    for m in range(micro):
        block_load[m].wait()

        def norm_one(i, m=m):
            rs = span(i, tile_r)
            norm, inverse = normed(held[m, pl.ds(pl.multiple_of(rows + i * tile_r, tile_r), tile_r), :].astype(F32))
            u = norm * vec(G1) + vec(S1)
            t = total[m, rs, :] * slope(u, phi(u))
            sums[G1] += fold(t * norm)
            sums[S1] += fold(t)
            grad = pull_back(t, norm, inverse, vec(G1))
            pulled = grads[m, rs, :].astype(F32) * wide(scale[m, rs, :], width)
            grads[m, rs, :] = (pulled + grad).astype(BF)

        for_each(rows // tile_r, norm_one)
        copy = pltpu.make_async_copy(grads.at[m, pl.ds(0, rows)], input_grad.at[m], store_sem.at[0, m])
        copy.start()
        stores.append(copy)
    tick(7)

    vec_part[0] = jnp.zeros_like(vec_part[0])
    for r in range(sums.shape[0]):
        vec_part[0, r : r + 1, :] = jnp.sum(sums[r], axis=0, keepdims=True)

    def vec_stage(n, peer):
        copy = send(vec_part.at[n], vec_in.at[n], vec_send.at[n], vec_recv.at[n], peer)
        copy.start()
        sent["v", n] = copy

    def vec_add(n):
        sent["v", n].wait_recv()
        vec_part[n + 1] = vec_part[n] + vec_in[n]

    vec_stage(0, place.core)

    exit_in.wait()
    for m in range(micro):
        three_again[m].wait()

        def exit_step(j, m=m):
            ns = span(j, tile_n)
            rs = pl.ds(pl.multiple_of(micro * rows + j * tile_n, tile_n), tile_n)
            got = mm(held[m, pl.ds(0, rows), :], buf[rs, :], NT) + params[BX : BX + 1, ns]
            out = held[m, pl.ds(rows, rows), ns].astype(F32) + got
            held[m, pl.ds(rows, rows), ns] = out.astype(BF)

        for_each(across, exit_step)
        copy = pltpu.make_async_copy(held.at[m, pl.ds(rows, rows)], block_out.at[m], store_sem.at[1, m])
        copy.start()
        stores.append(copy)
        vec_add(m)
        if m == 0:
            vec_stage(1, place.px)
        elif m == 1:
            vec_stage(2, place.py)
    tick(8)
    for j in others:
        copy = send(vec_part.at[3], vec_in.at[2 + j], vec_send.at[2 + j], vec_recv.at[2 + j], place.above(j))
        copy.start()
        sent["v", 2 + j] = copy
    tick(9)
    value = vec_part[3]
    for j in others:
        sent["v", 2 + j].wait_recv()
        value = value + vec_in[2 + j]
    vec_out[...] = value
    tick(10)
    for i in range(taps):
        sent["h", i].wait_recv()
    for copy in stores:
        copy.wait()

    @pl.when(jnp.logical_not(at_end))
    def _():
        halo_right.wait_send()

    @pl.when(jnp.logical_not(at_start))
    def _():
        halo_left.wait_send()

    sent["core", taps - 1].wait_send()
    for key, copy in sent.items():
        if key[0] in ("a", "b", "z", "f") and key[1] >= taps - 2 or key[0] in ("g", "h", "v"):
            copy.wait_send()


def backward(block_in, cotangent, lengths, weights, shard, kept):
    gathered, act_one, inner_one, ext_two, act_three, grad_two, grad_branch, params, sums = kept
    micro, rows, width = block_in.shape
    halo = (KERNEL_TAPS // 2) * DILATION_STEP
    taps = gathered.shape[0]
    nz = lax.axis_size("fsdp")
    extent = rows + 2 * halo
    piece = shard // 4
    half = width // 2
    shape = jax.ShapeDtypeStruct
    anywhere = pl.BlockSpec(memory_space=pl.ANY)
    near = pl.BlockSpec(memory_space=pltpu.VMEM)
    scalars = pl.BlockSpec(memory_space=pltpu.SMEM)
    dma = pltpu.SemaphoreType.DMA
    vmem = pltpu.VMEM
    flops = 2 * micro * rows * width * width * (2 * taps)
    return pl.pallas_call(
        backward_kernel,
        out_shape=(
            shape((micro, rows, width), BF),
            shape((micro, rows, width), BF),
            shape((taps, shard, width), BF),
            shape((VECTORS, width), F32),
        ),
        in_specs=[anywhere, anywhere, scalars, scalars, near, near] + [anywhere] * 7,
        out_specs=(anywhere, anywhere, anywhere, near),
        scratch_shapes=[
            vmem((micro, extent, width), BF),
            vmem((micro, extent, width), BF),
            vmem((micro, rows, width), F32),
            vmem((2 * micro * rows, width), BF),
            vmem((2, 128, width), F32),
            vmem((micro, extent, LANES), jnp.int32),
            vmem((micro, rows, LANES), F32),
            vmem((9, 8, width), F32),
            vmem((width, half), BF),
            vmem((width, half), BF),
            vmem((width, half), BF),
            vmem((taps, 2 * nz, piece, half), BF),
            vmem((2, 2 * nz, piece, half), BF),
            vmem((2, 2 * nz, piece, half), BF),
            vmem((taps, nz, piece, half), BF),
            vmem((2, nz, piece, half), BF),
            vmem((2, nz, piece, half), F32),
            vmem((taps, nz - 1, piece, half), BF),
            vmem((2, nz - 1, piece, half), BF),
            vmem((2, piece, half), F32),
            vmem((2, piece, half), BF),
            vmem((4, VECTORS, width), F32),
            vmem((2 + nz, VECTORS, width), F32),
            dma((taps,)),
            dma((taps,)),
            dma((taps,)),
            dma((taps,)),
            dma((taps,)),
            dma((taps,)),
            dma((taps, nz - 1)),
            dma((taps, nz - 1)),
            dma((taps,)),
            dma((taps,)),
            dma((taps,)),
            dma((taps, 2)),
            dma((taps, 2)),
            dma((taps,)),
            dma((taps,)),
            dma((2,)),
            dma((2,)),
            dma((2 + nz,)),
            dma((2 + nz,)),
            dma((2 * micro + 3,)),
            dma((2,)),
            dma((2, micro)),
            pltpu.SemaphoreType.REGULAR,
        ],
        compiler_params=pltpu.CompilerParams(
            collective_id=2, has_side_effects=True, vmem_limit_bytes=VMEM_MOST
        ),
        cost_estimate=pl.CostEstimate(flops=flops, bytes_accessed=80 << 20, transcendentals=0),
        name="backward_and_reduce",
    )(block_in, cotangent, lengths, weights, params, sums, gathered, act_one, inner_one, ext_two, act_three, grad_two, grad_branch)


def kernels_on_device(
    block_in,
    cotangent,
    lengths,
    item_weights,
    first_gain,
    first_shift,
    entry_weight,
    entry_bias,
    middle_gain,
    middle_shift,
    conv_weight,
    conv_bias,
    final_gain,
    final_shift,
    exit_weight,
    exit_bias,
):
    shard = entry_weight.shape[0]
    rows = [
        first_gain,
        first_shift,
        entry_bias,
        middle_gain,
        middle_shift,
        conv_bias,
        final_gain,
        final_shift,
        exit_bias,
    ]
    padded = -(-shard // LANES) * LANES
    vectors = jnp.pad(jnp.stack(rows), ((0, VECTORS - len(rows)), (0, padded - shard)))
    own_lengths, own_weights = lengths[:, 0], item_weights[:, 0]
    kept = forward(
        block_in, cotangent, own_lengths, own_weights, vectors, entry_weight, conv_weight, exit_weight.T
    )
    outputs, input_grads, shares, sums = backward(
        block_in, cotangent, own_lengths, own_weights, shard, kept
    )
    own_sums = lax.dynamic_slice_in_dim(sums, lax.axis_index("fsdp") * shard, shard, axis=1)
    vec = [own_sums[r] for r in range(len(rows))]
    return (
        outputs,
        input_grads,
        vec[G1],
        vec[S1],
        shares[0].astype(F32),
        vec[BE],
        vec[G2],
        vec[S2],
        shares[2:].astype(F32),
        vec[BC],
        vec[G3],
        vec[S3],
        shares[1].astype(F32).T,
        vec[BX],
    )


def fits(mesh):
    return mesh.shape["seq"] == 8


def norm_act(values, scale_vec, shift_vec):
    row_mean = jnp.mean(values, axis=-1, keepdims=True)
    centred = values - row_mean
    spread = jnp.mean(centred * centred, axis=-1, keepdims=True)
    return jax.nn.gelu(
        centred * lax.rsqrt(spread + eps_norm) * scale_vec + shift_vec, approximate=False
    )


def column_product(left, right):
    return lax.dot_general(
        left, right, (((0,), (0,)), ((), ())), preferred_element_type=jnp.float32
    )


def row_product(left, right):
    return lax.dot_general(
        left, right, (((1,), (1,)), ((), ())), preferred_element_type=jnp.float32
    )


def items_at(residue_position, item_lengths, stream_len):
    item_places = jnp.arange(item_lengths.shape[0], dtype=jnp.int32)
    ends = jnp.sum(
        jnp.where(item_places[:, None] <= item_places[None, :], item_lengths[:, None], 0), axis=0
    )
    inside = (residue_position >= 0) & (residue_position < stream_len)
    seg_all = jnp.sum((residue_position[:, None] >= ends[None, :]).astype(jnp.int32), axis=1)
    return jnp.where(inside, seg_all, -1)


def stacked(extended, segment_extended, tap_offset, row_count, item_count):
    half_reach = KERNEL_TAPS // 2
    middle_tap = segment_extended[half_reach * tap_offset : half_reach * tap_offset + row_count]
    tap_parts = []
    for kernel_tap_index in range(KERNEL_TAPS):
        segment_tapped = segment_extended[
            kernel_tap_index * tap_offset : kernel_tap_index * tap_offset + row_count
        ]
        keep_mask = (
            (segment_tapped == middle_tap) & (segment_tapped >= 0) & (segment_tapped < item_count)
        )
        tap_parts.append(
            extended[kernel_tap_index * tap_offset : kernel_tap_index * tap_offset + row_count]
            * keep_mask[:, None].astype(extended.dtype)
        )
    return jnp.concatenate(tap_parts, axis=1)


def on_device(
    block_in,
    cotangent,
    lengths,
    item_weights,
    first_gain,
    first_shift,
    entry_weight,
    entry_bias,
    middle_gain,
    middle_shift,
    conv_weight,
    conv_bias,
    final_gain,
    final_shift,
    exit_weight,
    exit_bias,
):
    micro_count = block_in.shape[0]
    row_count = block_in.shape[1]
    model_width = block_in.shape[2]
    inner_width = entry_weight.shape[1]
    item_count = lengths.shape[2]
    sequence_count = lax.axis_size("seq")
    seq_place = lax.axis_index("seq")
    stream_len = row_count * sequence_count
    half_reach = KERNEL_TAPS // 2
    totals = [
        jnp.zeros((model_width,), jnp.float32),
        jnp.zeros((model_width,), jnp.float32),
        jnp.zeros((model_width, inner_width), jnp.float32),
        jnp.zeros((inner_width,), jnp.float32),
        jnp.zeros((inner_width,), jnp.float32),
        jnp.zeros((inner_width,), jnp.float32),
        jnp.zeros((KERNEL_TAPS, inner_width, inner_width), jnp.float32),
        jnp.zeros((inner_width,), jnp.float32),
        jnp.zeros((inner_width,), jnp.float32),
        jnp.zeros((inner_width,), jnp.float32),
        jnp.zeros((inner_width, model_width), jnp.float32),
        jnp.zeros((model_width,), jnp.float32),
    ]
    outputs = []
    input_grads = []
    for micro_index in range(micro_count):
        params = (
            lax.all_gather(first_gain, "fsdp", axis=0, tiled=True),
            lax.all_gather(first_shift, "fsdp", axis=0, tiled=True),
            lax.all_gather(entry_weight, "fsdp", axis=0, tiled=True),
            lax.all_gather(entry_bias, "fsdp", axis=0, tiled=True),
            lax.all_gather(middle_gain, "fsdp", axis=0, tiled=True),
            lax.all_gather(middle_shift, "fsdp", axis=0, tiled=True),
            lax.all_gather(conv_weight, "fsdp", axis=1, tiled=True),
            lax.all_gather(conv_bias, "fsdp", axis=0, tiled=True),
            lax.all_gather(final_gain, "fsdp", axis=0, tiled=True),
            lax.all_gather(final_shift, "fsdp", axis=0, tiled=True),
            lax.all_gather(exit_weight, "fsdp", axis=1, tiled=True),
            lax.all_gather(exit_bias, "fsdp", axis=0, tiled=True),
        )
        (
            gain_one,
            shift_one,
            weight_in,
            bias_in,
            gain_two,
            shift_two,
            weight_conv,
            bias_conv,
            gain_three,
            shift_three,
            weight_out,
            bias_out,
        ) = params
        item_lengths = lengths[micro_index, 0]
        weight_row = item_weights[micro_index, 0]
        own_position = seq_place * row_count + jnp.arange(row_count, dtype=jnp.int32)
        seg_own = items_at(own_position, item_lengths, stream_len)
        match = seg_own[:, None] == jnp.arange(item_count, dtype=jnp.int32)[None, :]
        row_scale = jnp.sum(jnp.where(match, weight_row[None, :], 0), axis=1).astype(jnp.float32)
        inputs = block_in[micro_index].astype(jnp.float32)
        normed_one, back_one = jax.vjp(
            norm_act, inputs, gain_one.astype(jnp.float32), shift_one.astype(jnp.float32)
        )
        act_one = normed_one.astype(jnp.bfloat16)
        inner_one = jnp.dot(
            act_one, weight_in, preferred_element_type=jnp.float32
        ) + bias_in.astype(jnp.float32)
        normed_two, back_two = jax.vjp(
            norm_act, inner_one, gain_two.astype(jnp.float32), shift_two.astype(jnp.float32)
        )
        second_activation = normed_two.astype(jnp.bfloat16)
        flat_conv = weight_conv.reshape(KERNEL_TAPS * inner_width, inner_width)
        flip_conv = (
            jnp.flip(weight_conv, 0)
            .transpose(0, 2, 1)
            .reshape(KERNEL_TAPS * inner_width, inner_width)
        )
        tap_offset = DILATION_STEP // sequence_count
        residue_position = (
            sequence_count
            * (
                jnp.arange(row_count + 2 * half_reach * tap_offset, dtype=jnp.int32)
                - half_reach * tap_offset
            )
            + seq_place
        )
        segment_extended = items_at(residue_position, item_lengths, stream_len)
        dealt = lax.all_to_all(
            second_activation.reshape(row_count // sequence_count, sequence_count, inner_width),
            "seq",
            split_axis=1,
            concat_axis=0,
            tiled=True,
        ).reshape(row_count, inner_width)
        extended = jnp.pad(dealt, ((half_reach * tap_offset, half_reach * tap_offset), (0, 0)))
        shifted_tap_rows = stacked(extended, segment_extended, tap_offset, row_count, item_count)
        dealt_out = (
            jnp.dot(shifted_tap_rows, flat_conv, preferred_element_type=jnp.float32)
            + bias_conv.astype(jnp.float32)
        ).astype(jnp.bfloat16)
        inner_two = lax.all_to_all(
            dealt_out.reshape(sequence_count, row_count // sequence_count, 1, inner_width),
            "seq",
            split_axis=0,
            concat_axis=2,
            tiled=True,
        ).reshape(row_count, inner_width)
        normed_three, back_three = jax.vjp(
            norm_act,
            inner_two.astype(jnp.float32),
            gain_three.astype(jnp.float32),
            shift_three.astype(jnp.float32),
        )
        act_three = normed_three.astype(jnp.bfloat16)
        branch = jnp.dot(
            act_three, weight_out, preferred_element_type=jnp.float32
        ) + bias_out.astype(jnp.float32)
        outputs.append((inputs + branch).astype(jnp.bfloat16))
        pulled = cotangent[micro_index].astype(jnp.float32) * row_scale[:, None]
        grad_branch = pulled.astype(jnp.bfloat16)
        sum_exit_weight = column_product(act_three, grad_branch)
        sum_exit_bias = jnp.sum(grad_branch.astype(jnp.float32), axis=0)
        grad_act_three = row_product(grad_branch, weight_out)
        grad_inner_two, sum_final_gain, sum_final_shift = back_three(grad_act_three)
        low_inner_two = grad_inner_two.astype(jnp.bfloat16)
        sum_conv_bias = jnp.sum(low_inner_two.astype(jnp.float32), axis=0)
        grad_dealt = lax.all_to_all(
            low_inner_two.reshape(row_count // sequence_count, sequence_count, inner_width),
            "seq",
            split_axis=1,
            concat_axis=0,
            tiled=True,
        ).reshape(row_count, inner_width)
        sum_conv_weight = column_product(shifted_tap_rows, grad_dealt)
        grad_ext = jnp.pad(grad_dealt, ((half_reach * tap_offset, half_reach * tap_offset), (0, 0)))
        dealt_back = jnp.dot(
            stacked(grad_ext, segment_extended, tap_offset, row_count, item_count),
            flip_conv,
            preferred_element_type=jnp.float32,
        )
        grad_act_two = lax.all_to_all(
            dealt_back.reshape(sequence_count, row_count // sequence_count, 1, inner_width),
            "seq",
            split_axis=0,
            concat_axis=2,
            tiled=True,
        ).reshape(row_count, inner_width)
        grad_inner_one, sum_middle_gain, sum_middle_shift = back_two(grad_act_two)
        low_inner_one = grad_inner_one.astype(jnp.bfloat16)
        sum_entry_weight = column_product(act_one, low_inner_one)
        sum_entry_bias = jnp.sum(low_inner_one.astype(jnp.float32), axis=0)
        grad_act_one = row_product(low_inner_one, weight_in)
        grad_inputs, sum_first_gain, sum_first_shift = back_one(grad_act_one)
        input_grads.append((pulled + grad_inputs).astype(jnp.bfloat16))
        fresh = (
            sum_first_gain,
            sum_first_shift,
            sum_entry_weight,
            sum_entry_bias,
            sum_middle_gain,
            sum_middle_shift,
            sum_conv_weight.reshape(KERNEL_TAPS, inner_width, inner_width),
            sum_conv_bias,
            sum_final_gain,
            sum_final_shift,
            sum_exit_weight,
            sum_exit_bias,
        )
        totals = [left + right for left, right in zip(totals, fresh)]
    shares = (
        lax.psum_scatter(totals[0], "fsdp", scatter_dimension=0, tiled=True),
        lax.psum_scatter(totals[1], "fsdp", scatter_dimension=0, tiled=True),
        lax.psum_scatter(totals[2], "fsdp", scatter_dimension=0, tiled=True),
        lax.psum_scatter(totals[3], "fsdp", scatter_dimension=0, tiled=True),
        lax.psum_scatter(totals[4], "fsdp", scatter_dimension=0, tiled=True),
        lax.psum_scatter(totals[5], "fsdp", scatter_dimension=0, tiled=True),
        lax.psum_scatter(totals[6], "fsdp", scatter_dimension=1, tiled=True),
        lax.psum_scatter(totals[7], "fsdp", scatter_dimension=0, tiled=True),
        lax.psum_scatter(totals[8], "fsdp", scatter_dimension=0, tiled=True),
        lax.psum_scatter(totals[9], "fsdp", scatter_dimension=0, tiled=True),
        lax.psum_scatter(totals[10], "fsdp", scatter_dimension=1, tiled=True),
        lax.psum_scatter(totals[11], "fsdp", scatter_dimension=0, tiled=True),
    )
    result = lax.psum(
        (
            shares[0],
            shares[1],
            shares[2],
            shares[3],
            shares[4],
            shares[5],
            shares[6],
            shares[7],
            shares[8],
            shares[9],
            shares[10],
            shares[11],
        ),
        "seq",
    )
    return (
        jnp.stack(outputs),
        jnp.stack(input_grads),
        result[0],
        result[1],
        result[2],
        result[3],
        result[4],
        result[5],
        result[6],
        result[7],
        result[8],
        result[9],
        result[10],
        result[11],
    )


def solution(mesh):
    in_specs = (
        P(None, ("fsdp", "seq"), None),
        P(None, ("fsdp", "seq"), None),
        P(None, "fsdp", None),
        P(None, "fsdp", None),
        P("fsdp"),
        P("fsdp"),
        P("fsdp", None),
        P("fsdp"),
        P("fsdp"),
        P("fsdp"),
        P(None, "fsdp", None),
        P("fsdp"),
        P("fsdp"),
        P("fsdp"),
        P(None, "fsdp"),
        P("fsdp"),
    )
    out_specs = (
        P(None, ("fsdp", "seq"), None),
        P(None, ("fsdp", "seq"), None),
        P("fsdp"),
        P("fsdp"),
        P("fsdp", None),
        P("fsdp"),
        P("fsdp"),
        P("fsdp"),
        P(None, "fsdp", None),
        P("fsdp"),
        P("fsdp"),
        P("fsdp"),
        P(None, "fsdp"),
        P("fsdp"),
    )
    body = kernels_on_device if fits(mesh) else on_device
    return jax.shard_map(
        body, mesh=mesh, in_specs=in_specs, out_specs=out_specs, check_vma=False
    )
```

```python
import functools
import math

import jax
import jax.numpy as jnp
from jax import lax
from jax.experimental import pallas as pl
from jax.experimental.pallas import tpu as pltpu
from jax.sharding import PartitionSpec as P

KERNEL_TAPS = 5
DILATION_STEP = 128


eps_norm = 1e-05

MESH = pl.DeviceIdType.MESH
BF = jnp.bfloat16
F32 = jnp.float32
LANES = 128
VMEM_MOST = 60 << 20
NN = (((1,), (0,)), ((), ()))
NT = (((1,), (1,)), ((), ()))
TN = (((0,), (0,)), ((), ()))
ROOT_HALF = math.sqrt(0.5)
PHI_SCALE = 1.0 / math.sqrt(2.0 * math.pi)
EXP2_SCALE = -0.5 * math.log2(math.e)
G1, S1, BE, G2, S2, BC, G3, S3, BX = range(9)
VECTORS = 16


def mm(left, right, dims):
    return lax.dot_general(left, right, dims, preferred_element_type=F32)


def normed(v):
    centred = v - jnp.mean(v, axis=-1, keepdims=True)
    inverse = lax.rsqrt(jnp.mean(centred * centred, axis=-1, keepdims=True) + eps_norm)
    return centred * inverse, inverse


def phi(u):
    return 0.5 + 0.5 * lax.erf(u * ROOT_HALF)


def slope(u, big_phi):
    return big_phi + u * (PHI_SCALE * jnp.exp2(u * u * EXP2_SCALE))


def fold(tile):
    return jnp.sum(tile.reshape(tile.shape[0] // 8, 8, tile.shape[1]), axis=0)


def pull_back(t, n, inverse, gain):
    at = t * gain
    return (
        at - jnp.mean(at, axis=-1, keepdims=True) - n * jnp.mean(at * n, axis=-1, keepdims=True)
    ) * inverse


def span(i, size):
    return pl.ds(pl.multiple_of(i * size, size), size)


def for_each(count, step):
    lax.fori_loop(0, count, lambda i, carry: (step(i), carry)[1], 0)


def wide(mask, width):
    return jnp.concatenate([mask] * (width // LANES), axis=1)


class Place:
    def __init__(self):
        self.z = lax.axis_index("fsdp")
        self.s = lax.axis_index("seq")
        self.nz = lax.axis_size("fsdp")
        self.ns = lax.axis_size("seq")
        s = self.s
        self.c = lax.rem(s, 2)
        self.x = lax.rem(s // 2, 2)
        self.y = s // 4
        self.q = s // 2
        self.core = (self.z, s + 1 - 2 * self.c)
        self.px = (self.z, s + 2 - 4 * self.x)
        self.py = (self.z, s + 4 - 8 * self.y)
        self.left = (self.z, lax.rem(s + self.ns - 1, self.ns))
        self.right = (self.z, lax.rem(s + 1, self.ns))

    def up(self, j):
        return lax.rem(self.z + j, self.nz)

    def down(self, j):
        return lax.rem(self.z + self.nz - j, self.nz)

    def above(self, j):
        return (self.up(j), self.s)

    def peers(self, turn):
        along_x, along_y = 2 - 4 * self.x, 4 - 8 * self.y
        return (
            (self.z, self.s + (1 - turn) * along_x + turn * along_y),
            (self.z, self.s + turn * along_x + (1 - turn) * along_y),
        )

    def partner(self, turn):
        return self.q + (1 - turn) * (1 - 2 * self.x) + turn * (2 - 4 * self.y)

    def greet(self):
        peers = [self.core, self.px, self.py, self.left, self.right]
        peers += [self.above(j) for j in range(1, self.nz)]
        barrier = pltpu.get_barrier_semaphore()
        for peer in peers:
            pl.semaphore_signal(barrier, inc=1, device_id=peer, device_id_type=MESH)
        pl.semaphore_wait(barrier, len(peers))


def send(src, dst, send_sem, recv_sem, peer):
    return pltpu.make_async_remote_copy(
        src_ref=src,
        dst_ref=dst,
        send_sem=send_sem,
        recv_sem=recv_sem,
        device_id=peer,
        device_id_type=MESH,
    )


def load_tap(place, own, gathered, dst, sems):
    shard = own.shape[0]
    copies = []
    for j in range(place.nz):
        rows = pl.ds(pl.multiple_of(place.down(j) * shard, 16), shard)
        src = own if j == 0 else gathered.at[rows]
        copies.append(pltpu.make_async_copy(src, dst.at[rows], sems.at[j]))
    for copy in copies:
        copy.start()
    return copies


def wait_all(copies):
    for copy in copies:
        copy.wait()


def wait_all_recv(copies):
    for copy in copies:
        copy.wait_recv()


def find_items(place, lengths, item, micro, rows, halo):
    extent = rows + 2 * halo
    count = lengths.shape[2]
    for m in range(micro):
        position = lax.broadcasted_iota(jnp.int32, (extent, LANES), 0) + (place.s * rows - halo)
        found = jnp.zeros((extent, LANES), jnp.int32)
        end = jnp.int32(0)
        for j in range(count):
            end = end + lengths[m, 0, j]
            found = found + jnp.where(position >= end, 1, 0)
        inside = (position >= 0) & (position < place.ns * rows) & (found < count)
        item[m] = jnp.where(inside, found, -1)


def row_scale(item, weights, m, first, size):
    own = item[m, pl.ds(first, size)]
    total = jnp.zeros((size, LANES), jnp.int32)
    for j in range(weights.shape[2]):
        total = total + jnp.where(own == j, weights[m, 0, j], 0)
    return total.astype(F32)


def keep(item, m, tap, first, size):
    own = item[m, pl.ds(first, size)]
    there = pl.multiple_of(first + (tap - KERNEL_TAPS // 2) * DILATION_STEP, DILATION_STEP)
    other = item[m, pl.ds(there, size)]
    return jnp.where((own == other) & (own >= 0), 1.0, 0.0).astype(F32)


TAP_ORDER = (2, 1, 3, 0, 4)
WHOLE = ()
DEPTH = 3


def block_kernel(
    block_in, cotangent, lengths, weights, vectors, entry, conv, exit_t,
    block_out, input_grad, shares, vec_out, gathered, act_one, inner_one, act_three, grad_three, grad_branch,
    held, total, grads, buf, chunk, item, params, parts, sums,
    out_core, own, in_core, in_a, out_a, keep_a, in_b, out_b, keep_b, in_z, out_z, keep_z, final, in_w, out_w, keep_w, out_p, in_p, keep_p, vec_part, vec_in,
    pv_send, pv_recv, zg_send, zg_recv, ag_send, ag_recv, bg_send, bg_recv, cg_send, cg_recv, halo_send, halo_recv,
    core_send, core_recv, a_send, a_recv, b_send, b_recv, z_send, z_recv, f_own, f_send, f_recv, g_send, g_recv, h_send, h_recv, w_send, w_recv,
    vec_send, vec_recv, load_sem, store_sem, tap_sem, chunk_sem, ready, credit,
):
    place = Place()
    micro, rows, width = block_in.shape
    halo = (KERNEL_TAPS // 2) * DILATION_STEP
    extent = rows + 2 * halo
    z, c, q, x, y, nz = place.z, place.c, place.q, place.x, place.y, place.nz
    taps, shard, _ = shares.shape
    piece = shard // 4
    half = width // 2
    tile_a = 256
    tile_m = half
    tile_r = 128
    down = rows // tile_a
    part = chunk.shape[1]
    per_block = rows // part
    others = range(1, nz)
    at_start, at_end = place.s == 0, place.s == place.ns - 1
    low, high = pl.ds(0, micro * rows), pl.ds(micro * rows, micro * rows)
    tap_rows = pl.ds(micro * rows, width)
    cols = pl.ds(pl.multiple_of(c * half, LANES), half)
    core_cols = pl.ds(pl.multiple_of(half - c * half, LANES), half)
    shards = [entry, exit_t] + [conv.at[k] for k in range(taps - 2)]

    def vec(r):
        return params[r : r + 1, :]

    def at_rows(m, first, count):
        return pl.ds(pl.multiple_of(m * extent + first, 16), count)

    def load(src, dst, n):
        copy = pltpu.make_async_copy(src, dst, load_sem.at[n])
        copy.start()
        return copy

    def store(src, dst, n):
        copy = pltpu.make_async_copy(src, dst, store_sem.at[n])
        copy.start()
        return copy

    def with_left(step):
        pl.when(jnp.logical_not(at_start))(step)

    def with_right(step):
        pl.when(jnp.logical_not(at_end))(step)

    block_load = [load(block_in.at[m], buf.at[at_rows(m, halo, rows)], m) for m in range(micro)]
    pull_load = [load(cotangent.at[m], held.at[m, pl.ds(0, rows)], micro + m) for m in range(micro)]
    place.greet()

    order = [0, 1] + [2 + k for k in TAP_ORDER]
    zg, ag, bg, cg, tap_loads = {}, {}, {}, {}, {}

    def at(t, zz, first, count):
        start = pl.multiple_of(zz * shard + first * piece, 16)
        return gathered.at[t, pl.ds(start, count * piece), cols]

    def spread_z(i):
        t = order[i]
        first, count = (0, 4) if i in WHOLE else (q, 1)
        start = pl.multiple_of(first * piece, 16)
        for j in others:
            copy = send(shards[t].at[pl.ds(start, count * piece), cols], at(t, z, first, count), zg_send.at[t, j - 1], zg_recv.at[t, j - 1], place.above(j))
            copy.start()
            zg[t, j] = copy

    def spread_a(i):
        t = order[i]
        for j in others:
            if i in WHOLE:
                continue
            zg[t, j].wait_recv()
            block = at(t, place.down(j), q, 1)
            copy = send(block, block, ag_send.at[t, j - 1], ag_recv.at[t, j - 1], place.peers(c)[0])
            copy.start()
            ag[t, j] = copy

    def spread_b(i):
        t = order[i]
        for j in others:
            if i in WHOLE:
                bg[t, j] = [zg[t, j]]
                continue
            ag[t, j].wait_recv()
            copies = []
            for n, which in enumerate((q, place.partner(c))):
                block = at(t, place.down(j), which, 1)
                copy = send(block, block, bg_send.at[t, j - 1, n], bg_recv.at[t, j - 1, n], place.peers(c)[1])
                copy.start()
                copies.append(copy)
            bg[t, j] = copies

    def spread_c(i):
        t = order[i]
        for j in others:
            wait_all_recv(bg[t, j])
            block = at(t, place.down(j), 0, 4)
            copy = send(block, block, cg_send.at[t, j - 1], cg_recv.at[t, j - 1], place.core)
            copy.start()
            cg[t, j] = copy

    def slot_rows(i):
        return pl.ds((i % 2) * width, width)

    def arrived(i):
        t = order[i]
        for j in others:
            cg[t, j].wait_recv()
        tap_loads[i] = load_tap(place, shards[t], gathered.at[t], grads.at[slot_rows(i)], tap_sem.at[i % 2])

    def tick(i):
        for back, stage in ((-3, spread_z), (0, spread_a), (1, spread_b), (2, spread_c)):
            if 0 <= i - back < taps:
                stage(i - back)

    spread_z(0)
    pv = [
        send(vectors, parts.at[z], pv_send.at[j - 1], pv_recv.at[j - 1], place.above(j))
        for j in others
    ]
    for copy in pv:
        copy.start()
    parts[z] = vectors[...]

    def block_right(m):
        return send(block_in.at[m, pl.ds(rows - halo, halo)], buf.at[at_rows(m, 0, halo)], halo_send.at[0, m], halo_recv.at[0, m], place.right)

    def block_left(m):
        return send(block_in.at[m, pl.ds(0, halo)], buf.at[at_rows(m, rows + halo, halo)], halo_send.at[1, m], halo_recv.at[1, m], place.left)

    def block_sides(m):
        with_right(lambda: block_right(m).start())
        with_left(lambda: block_left(m).start())

    block_sides(0)

    def edges(array):
        for m in range(micro):

            @pl.when(at_start)
            def _(m=m):
                array[at_rows(m, 0, halo), :] = jnp.zeros((halo, width), BF)

            @pl.when(at_end)
            def _(m=m):
                array[at_rows(m, rows + halo, halo), :] = jnp.zeros((halo, width), BF)

    edges(buf)
    spread_z(1)
    find_items(place, lengths, item, micro, rows, halo)
    sums[...] = jnp.zeros_like(sums)
    wait_all_recv(pv)
    params[...] = jnp.concatenate([parts[zz].astype(F32)[:, :shard] for zz in range(nz)], axis=1)
    spread_z(2)

    def norm_one(first, count):
        def step(i):
            rs = pl.ds(pl.multiple_of(first + i * tile_r, tile_r), tile_r)
            n, _ = normed(buf[rs, :].astype(F32))
            u = n * vec(G1) + vec(S1)
            buf[rs, :] = (u * phi(u)).astype(BF)

        for_each(count // tile_r, step)

    one_out = []
    for m in range(micro):
        block_load[m].wait()
        norm_one(m * extent + halo, rows)
        one_out.append(store(buf.at[at_rows(m, halo, rows)], act_one.at[m], m))

    branch_out = []
    for m in range(micro):
        pull_load[m].wait()

        def pull(i, m=m):
            rs = span(i, tile_r)
            weight = row_scale(item, weights, m, pl.multiple_of(halo + i * tile_r, tile_r), tile_r)
            value = (held[m, rs, :].astype(F32) * wide(weight, width)).astype(BF)
            held[m, rs, :] = value
            sums[BX] += fold(value.astype(F32))

        for_each(rows // tile_r, pull)
        branch_out.append(store(held.at[m, pl.ds(0, rows)], grad_branch.at[m], micro + m))
    tick(0)

    def norm_sides(m):
        with_left(lambda: block_right(m).wait_recv())
        with_right(lambda: block_left(m).wait_recv())
        norm_one(m * extent, halo)
        norm_one(m * extent + halo + rows, halo)

    norm_sides(0)
    tick(1)
    block_sides(1)
    block_sides(2)
    tick(2)
    norm_sides(1)
    tick(3)
    arrived(0)

    wait_all(tap_loads[0])
    wait_all(branch_out)
    inner_out = []

    def norm_two(m, source, first, count):
        def step(i):
            n, _ = normed(total[m, pl.ds(pl.multiple_of(source + i * tile_r, tile_r), tile_r), :])
            u = n * vec(G2) + vec(S2)
            rs = pl.ds(pl.multiple_of(first + i * tile_r, tile_r), tile_r)
            held[m, rs, :] = (u * phi(u)).astype(BF)

        for_each(count // tile_r, step)

    def entry_tile(m, i, first):
        got = mm(buf[at_rows(m, first, tile_a), :], grads[pl.ds(0, width), :], NN)
        total[m, span(i, tile_a), :] = got + vec(BE)

    for m in range(micro):
        for_each(down, lambda i, m=m: entry_tile(m, i, halo + i * tile_a))
        inner_out.append(store(total.at[m], inner_one.at[m], 2 * micro + m))
        norm_two(m, 0, halo, rows)
        if m == 1:
            tick(4)
            arrived(1)
    norm_sides(2)
    for m in range(micro):
        inner_out[m].wait()
        for_each(halo // tile_a, lambda i, m=m: entry_tile(m, i, i * tile_a))
        for_each(halo // tile_a, lambda i, m=m: entry_tile(m, halo // tile_a + i, halo + rows + i * tile_a))
        norm_two(m, 0, 0, halo)
        norm_two(m, halo, halo + rows, halo)
        if m == 1:
            tick(5)
    arrived(2)
    wait_all(one_out)
    branch_in = [load(grad_branch.at[m], buf.at[pl.ds(m * rows, rows)], m) for m in range(micro)]

    wait_all(tap_loads[1])
    three_out = []
    for m in range(micro):
        branch_in[m].wait()

        def exit_back(i, m=m):
            left = buf[pl.ds(pl.multiple_of(m * rows + i * tile_a, tile_a), tile_a), :]
            total[m, span(i, tile_a), :] = mm(left, grads[pl.ds(width, width), :], NN)

        for_each(down, exit_back)
        three_out.append(store(total.at[m], grad_three.at[m], 2 * micro + m))
    tick(6)
    arrived(3)
    wait_all(three_out)

    def conv_tap(i):
        tap = TAP_ORDER[i - 2]
        wait_all(tap_loads[i])
        offset = (tap - KERNEL_TAPS // 2) * DILATION_STEP

        def step(n):
            m, r = n // down, pl.multiple_of(lax.rem(n, down) * tile_a, tile_a)
            rs = pl.ds(r, tile_a)
            left = held[m, pl.ds(pl.multiple_of(halo + offset + r, DILATION_STEP), tile_a), :]
            got = mm(left, grads[slot_rows(i), :], NN)
            got = got * wide(keep(item, m, tap, halo + r, tile_a), width)
            if i == 2:
                total[m, rs, :] = got
            else:
                total[m, rs, :] += got

        for_each(micro * down, step)

    for i in range(2, taps):
        conv_tap(i)
        if i + 2 < taps:
            tick(i + 5)
            arrived(i + 2)

    with_left(lambda: pl.semaphore_signal(ready.at[1], inc=1, device_id=place.left, device_id_type=MESH))
    with_right(lambda: pl.semaphore_signal(ready.at[0], inc=1, device_id=place.right, device_id_type=MESH))
    edges(grads)

    def fetch(source, n):
        m, r = n // per_block, lax.rem(n, per_block)
        slot = lax.rem(n, 2)
        return pltpu.make_async_copy(source.at[m, span(r, part)], chunk.at[slot], chunk_sem.at[slot])

    def chunked(source, m, work):
        def step(n, carry):
            @pl.when(n + 1 < micro * per_block)
            def _():
                fetch(source, n + 1).start()

            fetch(source, n).wait()
            for p in range(part // tile_r):
                r = pl.multiple_of((n - m * per_block) * part + p * tile_r, tile_r)
                work(m, r, chunk[lax.rem(n, 2), p * tile_r : (p + 1) * tile_r, :])
            return carry

        lax.fori_loop(m * per_block, (m + 1) * per_block, step, 0)

    def norm_three(m, r, grad_in):
        v = (total[m, pl.ds(r, tile_r), :] + vec(BC)).astype(BF).astype(F32)
        n, inverse = normed(v)
        u = n * vec(G3) + vec(S3)
        big_phi = phi(u)
        buf[pl.ds(pl.multiple_of((micro + m) * rows + r, tile_r), tile_r), :] = (u * big_phi).astype(BF)
        t = grad_in * slope(u, big_phi)
        sums[G3] += fold(t * n)
        sums[S3] += fold(t)
        grad = pull_back(t, n, inverse, vec(G3)).astype(BF)
        grads[at_rows(m, halo + r, tile_r), :] = grad
        sums[BC] += fold(grad.astype(F32))

    def grad_right(m):
        return send(grads.at[at_rows(m, rows, halo)], grads.at[at_rows(m, 0, halo)], halo_send.at[2, m], halo_recv.at[2, m], place.right)

    def grad_left(m):
        return send(grads.at[at_rows(m, halo, halo)], grads.at[at_rows(m, rows + halo, halo)], halo_send.at[3, m], halo_recv.at[3, m], place.left)

    fetch(grad_three, 0).start()
    act_out = []
    for m in range(micro):
        chunked(grad_three, m, norm_three)
        if m == 0:
            with_left(lambda: pl.semaphore_wait(ready.at[0], 1))
            with_right(lambda: pl.semaphore_wait(ready.at[1], 1))
        with_right(lambda m=m: grad_right(m).start())
        with_left(lambda m=m: grad_left(m).start())
        act_out.append(store(buf.at[pl.ds((micro + m) * rows, rows)], act_three.at[m], m))

    back = [1] + [2 + k for k in TAP_ORDER] + [0]
    last = taps - 1
    mine_a, mine_b = (1 - c) * x + c * y, c * x + (1 - c) * y
    sent = {}

    def block_at(other, mine):
        return (other * (2 - c) + mine * (1 + c)) * piece

    def stage_core(i):
        copy = send(out_core, in_core, core_send.at[i], core_recv.at[i], place.core)
        if i > 0:
            pl.semaphore_wait(credit.at[0], 1)
        copy.start()
        sent["core", i] = copy

    def used_core(i):
        if i < last:
            pl.semaphore_signal(credit.at[0], inc=1, device_id=place.core, device_id_type=MESH)

    def stage_w():
        sent["core", 0].wait_recv()
        for j in range(nz):
            rs = pl.ds(pl.multiple_of(place.up(j) * shard, 16), shard)
            value = own[rs, :].astype(F32) + in_core[rs, :].astype(F32)
            if j == 0:
                keep_w[...] = value
                continue
            out_w[j - 1] = value.astype(BF)
            copy = send(out_w.at[j - 1], in_w.at[j - 1], w_send.at[j - 1], w_recv.at[j - 1], place.above(j))
            copy.start()
            sent["w", j] = copy
        used_core(0)

    def stage_wa():
        value = keep_w[...]
        for j in others:
            sent["w", j].wait_recv()
            value = value + in_w[j - 1].astype(F32)
        keep_w[...] = value
        for other in range(2):
            gone = pl.ds(pl.multiple_of(block_at(other, 1 - mine_a), 16), piece)
            out_p[other] = keep_w[gone, :].astype(BF)
        copy = send(out_p.at[pl.ds(0, 2)], in_p.at[pl.ds(0, 2)], a_send.at[0], a_recv.at[0], place.peers(c)[0])
        copy.start()
        sent["a", 0] = copy

    def stage_wb():
        sent["a", 0].wait_recv()

        def total_of(other):
            rs = pl.ds(pl.multiple_of(block_at(other, mine_a), 16), piece)
            return keep_w[rs, :] + in_p[other].astype(F32)

        out_p[2] = total_of(1 - mine_b).astype(BF)
        keep_p[...] = total_of(mine_b)
        copy = send(out_p.at[2], in_p.at[2], b_send.at[0], b_recv.at[0], place.peers(c)[1])
        copy.start()
        sent["b", 0] = copy

    def stage_a(i):
        slot = i % 2
        sent["core", i].wait_recv()
        if i >= 3:
            sent["a", i - 2].wait_send()

        def step(n):
            base, other = (n // 2) * shard, lax.rem(n, 2)
            kept = pl.ds(pl.multiple_of(base + block_at(other, mine_a), 16), piece)
            gone = pl.ds(pl.multiple_of(base + block_at(other, 1 - mine_a), 16), piece)
            out_a[slot, n] = (own[gone, :].astype(F32) + in_core[gone, :].astype(F32)).astype(BF)
            keep_a[slot, n] = (own[kept, :].astype(F32) + in_core[kept, :].astype(F32)).astype(keep_a.dtype)

        for_each(2 * nz, step)
        if i > DEPTH:
            pl.semaphore_wait(credit.at[1], 1)
        copy = send(out_a.at[slot], in_a.at[i % DEPTH], a_send.at[i], a_recv.at[i], place.peers(c)[0])
        copy.start()
        sent["a", i] = copy
        used_core(i)

    def stage_b(i):
        slot = i % 2
        sent["a", i].wait_recv()
        if i >= 3:
            sent["b", i - 2].wait_send()

        def step(zz):
            kept, gone = 2 * zz + mine_b, 2 * zz + 1 - mine_b
            out_b[slot, zz] = (keep_a[slot, gone].astype(F32) + in_a[i % DEPTH, gone].astype(F32)).astype(BF)
            keep_b[slot, zz] = (keep_a[slot, kept].astype(F32) + in_a[i % DEPTH, kept].astype(F32)).astype(keep_b.dtype)

        for_each(nz, step)
        if i + DEPTH <= last:
            pl.semaphore_signal(credit.at[1], inc=1, device_id=place.peers(c)[0], device_id_type=MESH)
        if i > DEPTH:
            pl.semaphore_wait(credit.at[2], 1)
        copy = send(out_b.at[slot], in_b.at[i % DEPTH], b_send.at[i], b_recv.at[i], place.peers(c)[1])
        copy.start()
        sent["b", i] = copy

    def stage_z(i):
        slot = i % 2
        sent["b", i].wait_recv()
        for j in range(nz):
            if j > 0 and i >= 3:
                sent["z", i - 2, j].wait_send()
            zz = place.up(j)
            value = keep_b[slot, zz].astype(F32) + in_b[i % DEPTH, zz].astype(F32)
            if j == 0:
                keep_z[slot] = value
                continue
            out_z[slot, j - 1] = value.astype(BF)
            copy = send(out_z.at[slot, j - 1], in_z.at[i - 1, j - 1], z_send.at[i, j - 1], z_recv.at[i, j - 1], place.above(j))
            copy.start()
            sent["z", i, j] = copy
        used_b(i)

    def used_b(i):
        if i + DEPTH <= last:
            pl.semaphore_signal(credit.at[2], inc=1, device_id=place.peers(c)[1], device_id_type=MESH)

    def share_at(i, first, count):
        return shares.at[back[i], pl.ds(pl.multiple_of(first * piece, 16), count * piece), cols]

    def stage_f(i):
        slot = i % 2
        if i == 0:
            sent["b", 0].wait_recv()
            value = keep_p[...] + in_p[2].astype(F32)
        else:
            value = keep_z[slot]
            for j in others:
                sent["z", i, j].wait_recv()
                value = value + in_z[i - 1, j - 1].astype(F32)
        if i >= 2:
            sent["f", i - 2].wait_send()
        final[slot] = value.astype(BF)
        here = pltpu.make_async_copy(final.at[slot], share_at(i, q, 1), f_own.at[i])
        here.start()
        copy = send(final.at[slot], share_at(i, q, 1), f_send.at[i], f_recv.at[i], place.peers(c)[0])
        copy.start()
        sent["f", i] = copy
        sent["own", i] = here

    def stage_g(i):
        sent["own", i].wait()
        sent["f", i].wait_recv()
        for n, which in enumerate((q, place.partner(c))):
            block = share_at(i, which, 1)
            copy = send(block, block, g_send.at[i, n], g_recv.at[i, n], place.peers(c)[1])
            copy.start()
            sent["g", i, n] = copy

    def stage_h(i):
        for n in range(2):
            sent["g", i, n].wait_recv()
        block = share_at(i, 0, 4)
        copy = send(block, block, h_send.at[i], h_recv.at[i], place.core)
        copy.start()
        sent["h", i] = copy

    def weight_grad(i, product):
        if i > 0:
            sent["core", i - 1].wait_send()

        def far(n):
            ms = span(n, tile_m)
            out_core[ms, :] = product(ms, core_cols).astype(BF)

        for_each(width // tile_m, far)
        stage_core(i)

        def near(n):
            ms = span(n, tile_m)
            own[ms, :] = product(ms, cols).astype(own.dtype)

        for_each(width // tile_m, near)
        if i == 0:
            stage_w()
        else:
            stage_a(i)

    weight_grad(0, lambda ms, ns: mm(buf[low, ms], buf[high, ns], TN))
    wait_all(act_out)

    def fetch_tap(t):
        return load_tap(place, shards[t], gathered.at[t], buf.at[tap_rows], tap_sem.at[0])

    def back_tap(n, k):
        offset = (k - KERNEL_TAPS // 2) * DILATION_STEP

        def step(i):
            m, r = i // down, pl.multiple_of(lax.rem(i, down) * tile_a, tile_a)
            rs = pl.ds(r, tile_a)
            first = pl.multiple_of(m * extent + halo - offset + r, DILATION_STEP)
            got = mm(grads[pl.ds(first, tile_a), :], buf[tap_rows, :], NT)
            got = got * wide(keep(item, m, KERNEL_TAPS - 1 - k, halo + r, tile_a), width)
            if n == 0:
                total[m, rs, :] = got
            else:
                total[m, rs, :] += got

        for_each(micro * down, step)

    tap_in = fetch_tap(2 + TAP_ORDER[0])
    for n, k in enumerate(TAP_ORDER):

        def masked(i, k=k):
            m, r = i // (rows // 128), lax.rem(i, rows // 128)
            first = pl.multiple_of(halo + r * 128, 128)
            mask = keep(item, m, k, first, 128)
            value = grads[at_rows(m, first, 128), :].astype(F32) * wide(mask, width)
            buf[span(i, 128), :] = value.astype(BF)

        for_each(micro * rows // 128, masked)
        start = halo + (k - KERNEL_TAPS // 2) * DILATION_STEP

        def product(ms, ns, start=start):
            got = None
            for m in range(micro):
                one = mm(held[m, pl.ds(start, rows), ms], buf[pl.ds(m * rows, rows), ns], TN)
                got = one if got is None else got + one
            return got

        weight_grad(n + 1, product)
        if n >= 2:
            stage_z(n - 1)
        if n >= 1:
            stage_b(n)
        if n == 1:
            for m in range(micro):
                with_left(lambda m=m: grad_right(m).wait_recv())
                with_right(lambda m=m: grad_left(m).wait_recv())
        if n == 2:
            stage_wa()
        elif n == 3:
            stage_wb()
        elif n == 4:
            stage_f(0)
        wait_all(tap_in)
        back_tap(n, k)
        if n + 1 < len(TAP_ORDER):
            tap_in = fetch_tap(2 + TAP_ORDER[n + 1])
        if n == 3:
            stage_f(1)
        elif n == 4:
            stage_g(0)
            stage_g(1)
            stage_f(2)

    entry_in = fetch_tap(0)
    one_in = [load(act_one.at[m], held.at[m, pl.ds(0, rows)], m) for m in range(micro)]
    block_load = [load(block_in.at[m], held.at[m, pl.ds(rows, rows)], micro + m) for m in range(micro)]
    for m in range(micro):
        with_right(lambda m=m: grad_right(m).wait_send())
        with_left(lambda m=m: grad_left(m).wait_send())
    pull_in = [load(cotangent.at[m], grads.at[at_rows(m, 0, rows)], 2 * micro + m) for m in range(micro)]

    def norm_two_back(m, r, inner):
        n, inverse = normed(inner)
        u = n * vec(G2) + vec(S2)
        t = total[m, pl.ds(r, tile_r), :] * slope(u, phi(u))
        sums[G2] += fold(t * n)
        sums[S2] += fold(t)
        grad = pull_back(t, n, inverse, vec(G2)).astype(BF)
        buf[pl.ds(pl.multiple_of(m * rows + r, tile_r), tile_r), :] = grad
        sums[BE] += fold(grad.astype(F32))

    fetch(inner_one, 0).start()
    for m in range(micro):
        chunked(inner_one, m, norm_two_back)
        if m == 0:
            stage_z(4)
            stage_b(5)
        elif m == 1:
            stage_h(0)
            stage_h(1)
            stage_g(2)
            stage_f(3)
        else:
            stage_f(4)

    wait_all(one_in)

    def entry_product(ms, ns):
        got = None
        for m in range(micro):
            one = mm(held[m, pl.ds(0, rows), ms], buf[pl.ds(m * rows, rows), ns], TN)
            got = one if got is None else got + one
        return got

    weight_grad(last, entry_product)
    stage_h(2)
    stage_g(3)
    stage_z(5)
    three_again = [load(act_three.at[m], held.at[m, pl.ds(0, rows)], m) for m in range(micro)]

    wait_all(entry_in)

    def entry_back(i):
        m, r = i // down, lax.rem(i, down)
        total[m, span(r, tile_a), :] = mm(buf[span(i, tile_a), :], buf[tap_rows, :], NT)

    for_each(micro * down, entry_back)
    exit_in = fetch_tap(1)
    stage_h(3)
    stage_g(4)
    stage_f(5)
    stage_b(6)
    stores = []
    for m in range(micro):
        block_load[m].wait()
        pull_in[m].wait()

        def norm_one_back(i, m=m):
            rs = span(i, tile_r)
            n, inverse = normed(held[m, pl.ds(pl.multiple_of(rows + i * tile_r, tile_r), tile_r), :].astype(F32))
            u = n * vec(G1) + vec(S1)
            t = total[m, rs, :] * slope(u, phi(u))
            sums[G1] += fold(t * n)
            sums[S1] += fold(t)
            grad = pull_back(t, n, inverse, vec(G1))
            there = at_rows(m, i * tile_r, tile_r)
            weight = row_scale(item, weights, m, pl.multiple_of(halo + i * tile_r, tile_r), tile_r)
            pulled = grads[there, :].astype(F32) * wide(weight, width)
            grads[there, :] = (pulled + grad).astype(BF)

        for_each(rows // tile_r, norm_one_back)
        stores.append(store(grads.at[at_rows(m, 0, rows)], input_grad.at[m], micro + m))
        if m == 0:
            stage_h(4)
            stage_g(5)
            stage_z(6)
    stage_h(5)
    stage_f(6)

    vec_part[0] = jnp.zeros_like(vec_part[0])
    for r in range(sums.shape[0]):
        vec_part[0, r : r + 1, :] = jnp.sum(sums[r], axis=0, keepdims=True)

    def vec_stage(n, peer):
        copy = send(vec_part.at[n], vec_in.at[n], vec_send.at[n], vec_recv.at[n], peer)
        copy.start()
        sent["v", n] = copy

    def vec_add(n):
        sent["v", n].wait_recv()
        vec_part[n + 1] = vec_part[n] + vec_in[n]

    vec_stage(0, place.core)

    wait_all(exit_in)
    for m in range(micro):
        three_again[m].wait()

        def exit_step(i, m=m):
            got = mm(held[m, span(i, tile_a), :], buf[tap_rows, :], NT) + vec(BX)
            rs = pl.ds(pl.multiple_of(rows + i * tile_a, tile_a), tile_a)
            held[m, rs, :] = (held[m, rs, :].astype(F32) + got).astype(BF)

        for_each(down, exit_step)
        stores.append(store(held.at[m, pl.ds(rows, rows)], block_out.at[m], 2 * micro + m))
        vec_add(m)
        if m == 0:
            vec_stage(1, place.px)
        elif m == 1:
            vec_stage(2, place.py)
    stage_g(6)
    for j in others:
        copy = send(vec_part.at[3], vec_in.at[2 + j], vec_send.at[2 + j], vec_recv.at[2 + j], place.above(j))
        copy.start()
        sent["v", 2 + j] = copy
    stage_h(6)
    value = vec_part[3]
    for j in others:
        sent["v", 2 + j].wait_recv()
        value = value + vec_in[2 + j]
    vec_out[...] = value
    for i in range(taps):
        sent["h", i].wait_recv()
    wait_all(stores)

    for m in range(micro):
        with_right(lambda m=m: block_right(m).wait_send())
        with_left(lambda m=m: block_left(m).wait_send())
    for copy in pv + list(zg.values()) + list(ag.values()) + list(cg.values()):
        copy.wait_send()
    for (t, j), copies in bg.items():
        for copy in copies:
            if copy is not zg[t, j]:
                copy.wait_send()
    sent["core", last].wait_send()
    for key, copy in sent.items():
        late = key[0] in ("a", "b", "z", "f") and key[1] >= last - 1
        if late or key in (("a", 0), ("b", 0)) or key[0] in ("g", "h", "v", "w"):
            copy.wait_send()


def run_block(block_in, cotangent, lengths, weights, vectors, entry, conv, exit_t):
    micro, rows, width = block_in.shape
    halo = (KERNEL_TAPS // 2) * DILATION_STEP
    taps = conv.shape[0] + 2
    nz = lax.axis_size("fsdp")
    extent = rows + 2 * halo
    shard = entry.shape[0]
    piece = shard // 4
    half = width // 2
    shape = jax.ShapeDtypeStruct
    anywhere = pl.BlockSpec(memory_space=pl.ANY)
    near = pl.BlockSpec(memory_space=pltpu.VMEM)
    scalars = pl.BlockSpec(memory_space=pltpu.SMEM)
    dma = pltpu.SemaphoreType.DMA
    vmem = pltpu.VMEM
    flops = 2 * micro * rows * width * width * (3 * taps)
    return pl.pallas_call(
        block_kernel,
        out_shape=(
            shape((micro, rows, width), BF),
            shape((micro, rows, width), BF),
            shape((taps, shard, width), BF),
            shape((VECTORS, width), F32),
            shape((taps, width, width), BF),
            shape((micro, rows, width), BF),
            shape((micro, rows, width), F32),
            shape((micro, rows, width), BF),
            shape((micro, rows, width), F32),
            shape((micro, rows, width), BF),
        ),
        in_specs=[anywhere, anywhere, scalars, scalars, near, anywhere, anywhere, anywhere],
        out_specs=(anywhere, anywhere, anywhere, near) + (anywhere,) * 6,
        scratch_shapes=[
            vmem((micro, extent, width), BF),
            vmem((micro, rows, width), F32),
            vmem((micro * extent, width), BF),
            vmem((micro * extent, width), BF),
            vmem((2, 128, width), F32),
            vmem((micro, extent, LANES), jnp.int32),
            vmem((VECTORS, width), F32),
            vmem((nz,) + vectors.shape, BF),
            vmem((9, 8, width), F32),
            vmem((width, half), BF),
            vmem((width, half), BF),
            vmem((width, half), BF),
            vmem((DEPTH, 2 * nz, piece, half), BF),
            vmem((2, 2 * nz, piece, half), BF),
            vmem((2, 2 * nz, piece, half), BF),
            vmem((DEPTH, nz, piece, half), BF),
            vmem((2, nz, piece, half), BF),
            vmem((2, nz, piece, half), BF),
            vmem((taps - 1, nz - 1, piece, half), BF),
            vmem((2, nz - 1, piece, half), BF),
            vmem((2, piece, half), F32),
            vmem((2, piece, half), BF),
            vmem((nz - 1, shard, half), BF),
            vmem((nz - 1, shard, half), BF),
            vmem((shard, half), F32),
            vmem((3, piece, half), BF),
            vmem((3, piece, half), BF),
            vmem((piece, half), F32),
            vmem((4, VECTORS, width), F32),
            vmem((2 + nz, VECTORS, width), F32),
            dma((nz - 1,)),
            dma((nz - 1,)),
            dma((taps, nz - 1)),
            dma((taps, nz - 1)),
            dma((taps, nz - 1)),
            dma((taps, nz - 1)),
            dma((taps, nz - 1, 2)),
            dma((taps, nz - 1, 2)),
            dma((taps, nz - 1)),
            dma((taps, nz - 1)),
            dma((4, micro)),
            dma((4, micro)),
            dma((taps,)),
            dma((taps,)),
            dma((taps,)),
            dma((taps,)),
            dma((taps,)),
            dma((taps,)),
            dma((taps, nz - 1)),
            dma((taps, nz - 1)),
            dma((taps,)),
            dma((taps,)),
            dma((taps,)),
            dma((taps, 2)),
            dma((taps, 2)),
            dma((taps,)),
            dma((taps,)),
            dma((nz - 1,)),
            dma((nz - 1,)),
            dma((2 + nz,)),
            dma((2 + nz,)),
            dma((3 * micro,)),
            dma((3 * micro,)),
            dma((2, nz)),
            dma((2,)),
            pltpu.SemaphoreType.REGULAR((2,)),
            pltpu.SemaphoreType.REGULAR((3,)),
        ],
        compiler_params=pltpu.CompilerParams(
            collective_id=1, has_side_effects=True, vmem_limit_bytes=VMEM_MOST
        ),
        cost_estimate=pl.CostEstimate(flops=flops, bytes_accessed=160 << 20, transcendentals=0),
        name="residual_block",
    )(block_in, cotangent, lengths, weights, vectors, entry, conv, exit_t)


def kernels_on_device(
    block_in,
    cotangent,
    lengths,
    item_weights,
    first_gain,
    first_shift,
    entry_weight,
    entry_bias,
    middle_gain,
    middle_shift,
    conv_weight,
    conv_bias,
    final_gain,
    final_shift,
    exit_weight,
    exit_bias,
):
    shard = entry_weight.shape[0]
    rows = [
        first_gain,
        first_shift,
        entry_bias,
        middle_gain,
        middle_shift,
        conv_bias,
        final_gain,
        final_shift,
        exit_bias,
    ]
    padded = -(-shard // LANES) * LANES
    place = lax.broadcasted_iota(jnp.int32, (VECTORS, padded), 0)
    vectors = jnp.zeros((VECTORS, padded), BF)
    for r, row in enumerate(rows):
        vectors = jnp.where(place == r, jnp.pad(row, (0, padded - shard))[None, :], vectors)
    outputs, input_grads, shares, sums = run_block(
        block_in, cotangent, lengths, item_weights, vectors, entry_weight, conv_weight, exit_weight.T
    )[:4]
    own_sums = lax.dynamic_slice_in_dim(sums, lax.axis_index("fsdp") * shard, shard, axis=1)
    vec = [own_sums[r] for r in range(len(rows))]
    return (
        outputs,
        input_grads,
        vec[G1],
        vec[S1],
        shares[0].astype(F32),
        vec[BE],
        vec[G2],
        vec[S2],
        shares[2:].astype(F32),
        vec[BC],
        vec[G3],
        vec[S3],
        shares[1].astype(F32).T,
        vec[BX],
    )


def fits(mesh):
    return mesh.shape["seq"] == 8


def norm_act(values, scale_vec, shift_vec):
    row_mean = jnp.mean(values, axis=-1, keepdims=True)
    centred = values - row_mean
    spread = jnp.mean(centred * centred, axis=-1, keepdims=True)
    return jax.nn.gelu(
        centred * lax.rsqrt(spread + eps_norm) * scale_vec + shift_vec, approximate=False
    )


def column_product(left, right):
    return lax.dot_general(
        left, right, (((0,), (0,)), ((), ())), preferred_element_type=jnp.float32
    )


def row_product(left, right):
    return lax.dot_general(
        left, right, (((1,), (1,)), ((), ())), preferred_element_type=jnp.float32
    )


def items_at(residue_position, item_lengths, stream_len):
    item_places = jnp.arange(item_lengths.shape[0], dtype=jnp.int32)
    ends = jnp.sum(
        jnp.where(item_places[:, None] <= item_places[None, :], item_lengths[:, None], 0), axis=0
    )
    inside = (residue_position >= 0) & (residue_position < stream_len)
    seg_all = jnp.sum((residue_position[:, None] >= ends[None, :]).astype(jnp.int32), axis=1)
    return jnp.where(inside, seg_all, -1)


def stacked(extended, segment_extended, tap_offset, row_count, item_count):
    half_reach = KERNEL_TAPS // 2
    middle_tap = segment_extended[half_reach * tap_offset : half_reach * tap_offset + row_count]
    tap_parts = []
    for kernel_tap_index in range(KERNEL_TAPS):
        segment_tapped = segment_extended[
            kernel_tap_index * tap_offset : kernel_tap_index * tap_offset + row_count
        ]
        keep_mask = (
            (segment_tapped == middle_tap) & (segment_tapped >= 0) & (segment_tapped < item_count)
        )
        tap_parts.append(
            extended[kernel_tap_index * tap_offset : kernel_tap_index * tap_offset + row_count]
            * keep_mask[:, None].astype(extended.dtype)
        )
    return jnp.concatenate(tap_parts, axis=1)


def on_device(
    block_in,
    cotangent,
    lengths,
    item_weights,
    first_gain,
    first_shift,
    entry_weight,
    entry_bias,
    middle_gain,
    middle_shift,
    conv_weight,
    conv_bias,
    final_gain,
    final_shift,
    exit_weight,
    exit_bias,
):
    micro_count = block_in.shape[0]
    row_count = block_in.shape[1]
    model_width = block_in.shape[2]
    inner_width = entry_weight.shape[1]
    item_count = lengths.shape[2]
    sequence_count = lax.axis_size("seq")
    seq_place = lax.axis_index("seq")
    stream_len = row_count * sequence_count
    half_reach = KERNEL_TAPS // 2
    totals = [
        jnp.zeros((model_width,), jnp.float32),
        jnp.zeros((model_width,), jnp.float32),
        jnp.zeros((model_width, inner_width), jnp.float32),
        jnp.zeros((inner_width,), jnp.float32),
        jnp.zeros((inner_width,), jnp.float32),
        jnp.zeros((inner_width,), jnp.float32),
        jnp.zeros((KERNEL_TAPS, inner_width, inner_width), jnp.float32),
        jnp.zeros((inner_width,), jnp.float32),
        jnp.zeros((inner_width,), jnp.float32),
        jnp.zeros((inner_width,), jnp.float32),
        jnp.zeros((inner_width, model_width), jnp.float32),
        jnp.zeros((model_width,), jnp.float32),
    ]
    outputs = []
    input_grads = []
    for micro_index in range(micro_count):
        params = (
            lax.all_gather(first_gain, "fsdp", axis=0, tiled=True),
            lax.all_gather(first_shift, "fsdp", axis=0, tiled=True),
            lax.all_gather(entry_weight, "fsdp", axis=0, tiled=True),
            lax.all_gather(entry_bias, "fsdp", axis=0, tiled=True),
            lax.all_gather(middle_gain, "fsdp", axis=0, tiled=True),
            lax.all_gather(middle_shift, "fsdp", axis=0, tiled=True),
            lax.all_gather(conv_weight, "fsdp", axis=1, tiled=True),
            lax.all_gather(conv_bias, "fsdp", axis=0, tiled=True),
            lax.all_gather(final_gain, "fsdp", axis=0, tiled=True),
            lax.all_gather(final_shift, "fsdp", axis=0, tiled=True),
            lax.all_gather(exit_weight, "fsdp", axis=1, tiled=True),
            lax.all_gather(exit_bias, "fsdp", axis=0, tiled=True),
        )
        (
            gain_one,
            shift_one,
            weight_in,
            bias_in,
            gain_two,
            shift_two,
            weight_conv,
            bias_conv,
            gain_three,
            shift_three,
            weight_out,
            bias_out,
        ) = params
        item_lengths = lengths[micro_index, 0]
        weight_row = item_weights[micro_index, 0]
        own_position = seq_place * row_count + jnp.arange(row_count, dtype=jnp.int32)
        seg_own = items_at(own_position, item_lengths, stream_len)
        match = seg_own[:, None] == jnp.arange(item_count, dtype=jnp.int32)[None, :]
        row_scale = jnp.sum(jnp.where(match, weight_row[None, :], 0), axis=1).astype(jnp.float32)
        inputs = block_in[micro_index].astype(jnp.float32)
        normed_one, back_one = jax.vjp(
            norm_act, inputs, gain_one.astype(jnp.float32), shift_one.astype(jnp.float32)
        )
        act_one = normed_one.astype(jnp.bfloat16)
        inner_one = jnp.dot(
            act_one, weight_in, preferred_element_type=jnp.float32
        ) + bias_in.astype(jnp.float32)
        normed_two, back_two = jax.vjp(
            norm_act, inner_one, gain_two.astype(jnp.float32), shift_two.astype(jnp.float32)
        )
        second_activation = normed_two.astype(jnp.bfloat16)
        flat_conv = weight_conv.reshape(KERNEL_TAPS * inner_width, inner_width)
        flip_conv = (
            jnp.flip(weight_conv, 0)
            .transpose(0, 2, 1)
            .reshape(KERNEL_TAPS * inner_width, inner_width)
        )
        tap_offset = DILATION_STEP // sequence_count
        residue_position = (
            sequence_count
            * (
                jnp.arange(row_count + 2 * half_reach * tap_offset, dtype=jnp.int32)
                - half_reach * tap_offset
            )
            + seq_place
        )
        segment_extended = items_at(residue_position, item_lengths, stream_len)
        dealt = lax.all_to_all(
            second_activation.reshape(row_count // sequence_count, sequence_count, inner_width),
            "seq",
            split_axis=1,
            concat_axis=0,
            tiled=True,
        ).reshape(row_count, inner_width)
        extended = jnp.pad(dealt, ((half_reach * tap_offset, half_reach * tap_offset), (0, 0)))
        shifted_tap_rows = stacked(extended, segment_extended, tap_offset, row_count, item_count)
        dealt_out = (
            jnp.dot(shifted_tap_rows, flat_conv, preferred_element_type=jnp.float32)
            + bias_conv.astype(jnp.float32)
        ).astype(jnp.bfloat16)
        inner_two = lax.all_to_all(
            dealt_out.reshape(sequence_count, row_count // sequence_count, 1, inner_width),
            "seq",
            split_axis=0,
            concat_axis=2,
            tiled=True,
        ).reshape(row_count, inner_width)
        normed_three, back_three = jax.vjp(
            norm_act,
            inner_two.astype(jnp.float32),
            gain_three.astype(jnp.float32),
            shift_three.astype(jnp.float32),
        )
        act_three = normed_three.astype(jnp.bfloat16)
        branch = jnp.dot(
            act_three, weight_out, preferred_element_type=jnp.float32
        ) + bias_out.astype(jnp.float32)
        outputs.append((inputs + branch).astype(jnp.bfloat16))
        pulled = cotangent[micro_index].astype(jnp.float32) * row_scale[:, None]
        grad_branch = pulled.astype(jnp.bfloat16)
        sum_exit_weight = column_product(act_three, grad_branch)
        sum_exit_bias = jnp.sum(grad_branch.astype(jnp.float32), axis=0)
        grad_act_three = row_product(grad_branch, weight_out)
        grad_inner_two, sum_final_gain, sum_final_shift = back_three(grad_act_three)
        low_inner_two = grad_inner_two.astype(jnp.bfloat16)
        sum_conv_bias = jnp.sum(low_inner_two.astype(jnp.float32), axis=0)
        grad_dealt = lax.all_to_all(
            low_inner_two.reshape(row_count // sequence_count, sequence_count, inner_width),
            "seq",
            split_axis=1,
            concat_axis=0,
            tiled=True,
        ).reshape(row_count, inner_width)
        sum_conv_weight = column_product(shifted_tap_rows, grad_dealt)
        grad_ext = jnp.pad(grad_dealt, ((half_reach * tap_offset, half_reach * tap_offset), (0, 0)))
        dealt_back = jnp.dot(
            stacked(grad_ext, segment_extended, tap_offset, row_count, item_count),
            flip_conv,
            preferred_element_type=jnp.float32,
        )
        grad_act_two = lax.all_to_all(
            dealt_back.reshape(sequence_count, row_count // sequence_count, 1, inner_width),
            "seq",
            split_axis=0,
            concat_axis=2,
            tiled=True,
        ).reshape(row_count, inner_width)
        grad_inner_one, sum_middle_gain, sum_middle_shift = back_two(grad_act_two)
        low_inner_one = grad_inner_one.astype(jnp.bfloat16)
        sum_entry_weight = column_product(act_one, low_inner_one)
        sum_entry_bias = jnp.sum(low_inner_one.astype(jnp.float32), axis=0)
        grad_act_one = row_product(low_inner_one, weight_in)
        grad_inputs, sum_first_gain, sum_first_shift = back_one(grad_act_one)
        input_grads.append((pulled + grad_inputs).astype(jnp.bfloat16))
        fresh = (
            sum_first_gain,
            sum_first_shift,
            sum_entry_weight,
            sum_entry_bias,
            sum_middle_gain,
            sum_middle_shift,
            sum_conv_weight.reshape(KERNEL_TAPS, inner_width, inner_width),
            sum_conv_bias,
            sum_final_gain,
            sum_final_shift,
            sum_exit_weight,
            sum_exit_bias,
        )
        totals = [left + right for left, right in zip(totals, fresh)]
    shares = (
        lax.psum_scatter(totals[0], "fsdp", scatter_dimension=0, tiled=True),
        lax.psum_scatter(totals[1], "fsdp", scatter_dimension=0, tiled=True),
        lax.psum_scatter(totals[2], "fsdp", scatter_dimension=0, tiled=True),
        lax.psum_scatter(totals[3], "fsdp", scatter_dimension=0, tiled=True),
        lax.psum_scatter(totals[4], "fsdp", scatter_dimension=0, tiled=True),
        lax.psum_scatter(totals[5], "fsdp", scatter_dimension=0, tiled=True),
        lax.psum_scatter(totals[6], "fsdp", scatter_dimension=1, tiled=True),
        lax.psum_scatter(totals[7], "fsdp", scatter_dimension=0, tiled=True),
        lax.psum_scatter(totals[8], "fsdp", scatter_dimension=0, tiled=True),
        lax.psum_scatter(totals[9], "fsdp", scatter_dimension=0, tiled=True),
        lax.psum_scatter(totals[10], "fsdp", scatter_dimension=1, tiled=True),
        lax.psum_scatter(totals[11], "fsdp", scatter_dimension=0, tiled=True),
    )
    result = lax.psum(
        (
            shares[0],
            shares[1],
            shares[2],
            shares[3],
            shares[4],
            shares[5],
            shares[6],
            shares[7],
            shares[8],
            shares[9],
            shares[10],
            shares[11],
        ),
        "seq",
    )
    return (
        jnp.stack(outputs),
        jnp.stack(input_grads),
        result[0],
        result[1],
        result[2],
        result[3],
        result[4],
        result[5],
        result[6],
        result[7],
        result[8],
        result[9],
        result[10],
        result[11],
    )


def solution(mesh):
    in_specs = (
        P(None, ("fsdp", "seq"), None),
        P(None, ("fsdp", "seq"), None),
        P(None, "fsdp", None),
        P(None, "fsdp", None),
        P("fsdp"),
        P("fsdp"),
        P("fsdp", None),
        P("fsdp"),
        P("fsdp"),
        P("fsdp"),
        P(None, "fsdp", None),
        P("fsdp"),
        P("fsdp"),
        P("fsdp"),
        P(None, "fsdp"),
        P("fsdp"),
    )
    out_specs = (
        P(None, ("fsdp", "seq"), None),
        P(None, ("fsdp", "seq"), None),
        P("fsdp"),
        P("fsdp"),
        P("fsdp", None),
        P("fsdp"),
        P("fsdp"),
        P("fsdp"),
        P(None, "fsdp", None),
        P("fsdp"),
        P("fsdp"),
        P("fsdp"),
        P(None, "fsdp"),
        P("fsdp"),
    )
    body = kernels_on_device if fits(mesh) else on_device
    return jax.shard_map(
        body, mesh=mesh, in_specs=in_specs, out_specs=out_specs, check_vma=False
    )
```

```python
import functools
import math

import jax
import jax.numpy as jnp
from jax import lax
from jax.experimental import pallas as pl
from jax.experimental.pallas import tpu as pltpu
from jax.sharding import PartitionSpec as P

KERNEL_TAPS = 5
DILATION_STEP = 128


eps_norm = 1e-05

MESH = pl.DeviceIdType.MESH
BF = jnp.bfloat16
F32 = jnp.float32
LANES = 128
VMEM_MOST = 60 << 20
NN = (((1,), (0,)), ((), ()))
NT = (((1,), (1,)), ((), ()))
TN = (((0,), (0,)), ((), ()))
ROOT_HALF = math.sqrt(0.5)
PHI_SCALE = 1.0 / math.sqrt(2.0 * math.pi)
EXP2_SCALE = -0.5 * math.log2(math.e)
G1, S1, BE, G2, S2, BC, G3, S3, BX = range(9)
VECTORS = 16


def mm(left, right, dims):
    return lax.dot_general(left, right, dims, preferred_element_type=F32)


def normed(v):
    centred = v - jnp.mean(v, axis=-1, keepdims=True)
    inverse = lax.rsqrt(jnp.mean(centred * centred, axis=-1, keepdims=True) + eps_norm)
    return centred * inverse, inverse


def phi(u):
    return 0.5 + 0.5 * lax.erf(u * ROOT_HALF)


def slope(u, big_phi):
    return big_phi + u * (PHI_SCALE * jnp.exp2(u * u * EXP2_SCALE))


def fold(tile):
    return jnp.sum(tile.reshape(tile.shape[0] // 8, 8, tile.shape[1]), axis=0)


def pull_back(t, n, inverse, gain):
    at = t * gain
    return (
        at - jnp.mean(at, axis=-1, keepdims=True) - n * jnp.mean(at * n, axis=-1, keepdims=True)
    ) * inverse


def span(i, size):
    return pl.ds(pl.multiple_of(i * size, size), size)


def for_each(count, step):
    lax.fori_loop(0, count, lambda i, carry: (step(i), carry)[1], 0)


def wide(mask, width):
    return jnp.concatenate([mask] * (width // LANES), axis=1)


class Place:
    def __init__(self):
        self.z = lax.axis_index("fsdp")
        self.s = lax.axis_index("seq")
        self.nz = lax.axis_size("fsdp")
        self.ns = lax.axis_size("seq")
        s = self.s
        self.c = lax.rem(s, 2)
        self.x = lax.rem(s // 2, 2)
        self.y = s // 4
        self.q = s // 2
        self.core = (self.z, s + 1 - 2 * self.c)
        self.px = (self.z, s + 2 - 4 * self.x)
        self.py = (self.z, s + 4 - 8 * self.y)
        self.across = (self.z, s + 3 - 4 * self.x - 2 * self.c)
        self.left = (self.z, lax.rem(s + self.ns - 1, self.ns))
        self.right = (self.z, lax.rem(s + 1, self.ns))

    def up(self, j):
        return lax.rem(self.z + j, self.nz)

    def down(self, j):
        return lax.rem(self.z + self.nz - j, self.nz)

    def above(self, j):
        return (self.up(j), self.s)

    def peers(self, turn):
        along_x, along_y = 2 - 4 * self.x, 4 - 8 * self.y
        return (
            (self.z, self.s + (1 - turn) * along_x + turn * along_y),
            (self.z, self.s + turn * along_x + (1 - turn) * along_y),
        )

    def partner(self, turn):
        return self.q + (1 - turn) * (1 - 2 * self.x) + turn * (2 - 4 * self.y)

    def greet(self):
        peers = [self.core, self.px, self.py, self.across, self.left, self.right]
        peers += [self.above(j) for j in range(1, self.nz)]
        barrier = pltpu.get_barrier_semaphore()
        for peer in peers:
            pl.semaphore_signal(barrier, inc=1, device_id=peer, device_id_type=MESH)
        pl.semaphore_wait(barrier, len(peers))


def send(src, dst, send_sem, recv_sem, peer):
    return pltpu.make_async_remote_copy(
        src_ref=src,
        dst_ref=dst,
        send_sem=send_sem,
        recv_sem=recv_sem,
        device_id=peer,
        device_id_type=MESH,
    )


def load_tap(place, own, gathered, dst, sems):
    shard = own.shape[0]
    copies = []
    for j in range(place.nz):
        rows = pl.ds(pl.multiple_of(place.down(j) * shard, 16), shard)
        src = own if j == 0 else gathered.at[rows]
        copies.append(pltpu.make_async_copy(src, dst.at[rows], sems.at[j]))
    for copy in copies:
        copy.start()
    return copies


def wait_all(copies):
    for copy in copies:
        copy.wait()


def wait_all_recv(copies):
    for copy in copies:
        copy.wait_recv()


def find_items(place, lengths, item, micro, rows, halo):
    extent = rows + 2 * halo
    count = lengths.shape[2]
    for m in range(micro):
        position = lax.broadcasted_iota(jnp.int32, (extent, LANES), 0) + (place.s * rows - halo)
        found = jnp.zeros((extent, LANES), jnp.int32)
        end = jnp.int32(0)
        for j in range(count):
            end = end + lengths[m, 0, j]
            found = found + jnp.where(position >= end, 1, 0)
        inside = (position >= 0) & (position < place.ns * rows) & (found < count)
        item[m] = jnp.where(inside, found, -1)


def row_scale(item, weights, m, first, size):
    own = item[m, pl.ds(first, size)]
    total = jnp.zeros((size, LANES), jnp.int32)
    for j in range(weights.shape[2]):
        total = total + jnp.where(own == j, weights[m, 0, j], 0)
    return total.astype(F32)


def keep(item, m, tap, first, size):
    own = item[m, pl.ds(first, size)]
    there = pl.multiple_of(first + (tap - KERNEL_TAPS // 2) * DILATION_STEP, DILATION_STEP)
    other = item[m, pl.ds(there, size)]
    return jnp.where((own == other) & (own >= 0), 1.0, 0.0).astype(F32)


TAP_ORDER = (2, 1, 3, 0, 4)
WHOLE = ()
BLOCK_RELAY, GRAD_RELAY = 2, 0
DEPTH = 3


def block_kernel(
    block_in, cotangent, lengths, weights, vectors, entry, conv, exit_t,
    block_out, input_grad, shares, vec_out, gathered, act_one, inner_one, act_three, grad_three, grad_branch, relay,
    held, total, grads, buf, chunk, item, params, parts, sums,
    out_core, own, in_core, in_a, out_a, keep_a, in_b, out_b, keep_b, in_z, out_z, keep_z, final, in_w, out_w, keep_w, out_p, in_p, keep_p, vec_part, vec_in,
    pv_send, pv_recv, zg_send, zg_recv, ag_send, ag_recv, bg_send, bg_recv, cg_send, cg_recv, halo_send, halo_recv, hop_send, hop_recv, pass_send,
    core_send, core_recv, a_send, a_recv, b_send, b_recv, z_send, z_recv, f_own, f_send, f_recv, g_send, g_recv, h_send, h_recv, w_send, w_recv,
    vec_send, vec_recv, load_sem, store_sem, tap_sem, chunk_sem, ready, credit,
):
    place = Place()
    micro, rows, width = block_in.shape
    halo = (KERNEL_TAPS // 2) * DILATION_STEP
    extent = rows + 2 * halo
    z, c, q, x, y, nz = place.z, place.c, place.q, place.x, place.y, place.nz
    taps, shard, _ = shares.shape
    piece = shard // 4
    half = width // 2
    tile_a = 256
    tile_m = half
    tile_r = 128
    down = rows // tile_a
    part = chunk.shape[1]
    per_block = rows // part
    others = range(1, nz)
    at_start, at_end = place.s == 0, place.s == place.ns - 1
    low, high = pl.ds(0, micro * rows), pl.ds(micro * rows, micro * rows)
    tap_rows = pl.ds(micro * rows, width)
    cols = pl.ds(pl.multiple_of(c * half, LANES), half)
    core_cols = pl.ds(pl.multiple_of(half - c * half, LANES), half)
    shards = [entry, exit_t] + [conv.at[k] for k in range(taps - 2)]

    def vec(r):
        return params[r : r + 1, :]

    def at_rows(m, first, count):
        return pl.ds(pl.multiple_of(m * extent + first, 16), count)

    def load(src, dst, n):
        copy = pltpu.make_async_copy(src, dst, load_sem.at[n])
        copy.start()
        return copy

    def store(src, dst, n):
        copy = pltpu.make_async_copy(src, dst, store_sem.at[n])
        copy.start()
        return copy

    def with_left(step):
        pl.when(jnp.logical_not(at_start))(step)

    def with_right(step):
        pl.when(jnp.logical_not(at_end))(step)

    block_load = [load(block_in.at[m], buf.at[at_rows(m, halo, rows)], m) for m in range(micro)]
    pull_load = [load(cotangent.at[m], held.at[m, pl.ds(0, rows)], micro + m) for m in range(micro)]
    place.greet()

    order = [0, 1] + [2 + k for k in TAP_ORDER]
    zg, ag, bg, cg, tap_loads = {}, {}, {}, {}, {}

    def at(t, zz, first, count):
        start = pl.multiple_of(zz * shard + first * piece, 16)
        return gathered.at[t, pl.ds(start, count * piece), cols]

    def spread_z(i):
        t = order[i]
        first, count = (0, 4) if i in WHOLE else (q, 1)
        start = pl.multiple_of(first * piece, 16)
        for j in others:
            copy = send(shards[t].at[pl.ds(start, count * piece), cols], at(t, z, first, count), zg_send.at[t, j - 1], zg_recv.at[t, j - 1], place.above(j))
            copy.start()
            zg[t, j] = copy

    def spread_a(i):
        t = order[i]
        for j in others:
            if i in WHOLE:
                continue
            zg[t, j].wait_recv()
            block = at(t, place.down(j), q, 1)
            copy = send(block, block, ag_send.at[t, j - 1], ag_recv.at[t, j - 1], place.peers(c)[0])
            copy.start()
            ag[t, j] = copy

    def spread_b(i):
        t = order[i]
        for j in others:
            if i in WHOLE:
                bg[t, j] = [zg[t, j]]
                continue
            ag[t, j].wait_recv()
            copies = []
            for n, which in enumerate((q, place.partner(c))):
                block = at(t, place.down(j), which, 1)
                copy = send(block, block, bg_send.at[t, j - 1, n], bg_recv.at[t, j - 1, n], place.peers(c)[1])
                copy.start()
                copies.append(copy)
            bg[t, j] = copies

    def spread_c(i):
        t = order[i]
        for j in others:
            wait_all_recv(bg[t, j])
            block = at(t, place.down(j), 0, 4)
            copy = send(block, block, cg_send.at[t, j - 1], cg_recv.at[t, j - 1], place.core)
            copy.start()
            cg[t, j] = copy

    def slot_rows(i):
        return pl.ds((i % 2) * width, width)

    def arrived(i):
        t = order[i]
        for j in others:
            cg[t, j].wait_recv()
        tap_loads[i] = load_tap(place, shards[t], gathered.at[t], grads.at[slot_rows(i)], tap_sem.at[i % 2])

    def tick(i):
        for back, stage in ((-3, spread_z), (0, spread_a), (1, spread_b), (2, spread_c)):
            if 0 <= i - back < taps:
                stage(i - back)

    spread_z(0)
    pv = [
        send(vectors, parts.at[z], pv_send.at[j - 1], pv_recv.at[j - 1], place.above(j))
        for j in others
    ]
    for copy in pv:
        copy.start()
    parts[z] = vectors[...]

    def block_right(m):
        return send(block_in.at[m, pl.ds(rows - halo, halo)], buf.at[at_rows(m, 0, halo)], halo_send.at[0, m], halo_recv.at[0, m], place.right)

    def block_left(m):
        return send(block_in.at[m, pl.ds(0, halo)], buf.at[at_rows(m, rows + halo, halo)], halo_send.at[1, m], halo_recv.at[1, m], place.left)

    turns_right = (lax.rem(place.s, 4) == 3) & jnp.logical_not(at_end)
    turns_left = (lax.rem(place.s, 4) == 0) & jnp.logical_not(at_start)
    straight_right = jnp.logical_not(at_end | turns_right)
    straight_left = jnp.logical_not(at_start | turns_left)

    def hop(n, src):
        return send(src, relay.at[n], hop_send.at[n], hop_recv.at[n], place.py)

    def pass_on(n, m, dst):
        return send(relay.at[n], dst, pass_send.at[n], halo_recv.at[n, m], place.across)

    def block_hop(side):
        first = rows - halo if side == 0 else 0
        return hop(side, block_in.at[BLOCK_RELAY, pl.ds(first, halo)])

    def block_pass(side):
        first = 0 if side == 0 else rows + halo
        return pass_on(side, BLOCK_RELAY, buf.at[at_rows(BLOCK_RELAY, first, halo)])

    def sides(relayed, right, left, hop_of, act):
        if relayed:
            pl.when(straight_right)(lambda: act(right))
            pl.when(straight_left)(lambda: act(left))
            pl.when(turns_right)(lambda: act(hop_of(0)))
            pl.when(turns_left)(lambda: act(hop_of(1)))
        else:
            with_right(lambda: act(right))
            with_left(lambda: act(left))

    def forward_sides(hop_of, pass_of):
        for side, here in ((0, at_end), (1, at_start)):

            @pl.when(here)
            def _(side=side):
                hop_of(side).wait_recv()
                pass_of(side).start()

    def block_sides(m):
        sides(m == BLOCK_RELAY, block_right(m), block_left(m), block_hop, lambda copy: copy.start())

    block_sides(0)

    def edges(array):
        for m in range(micro):

            @pl.when(at_start)
            def _(m=m):
                array[at_rows(m, 0, halo), :] = jnp.zeros((halo, width), BF)

            @pl.when(at_end)
            def _(m=m):
                array[at_rows(m, rows + halo, halo), :] = jnp.zeros((halo, width), BF)

    edges(buf)
    spread_z(1)
    find_items(place, lengths, item, micro, rows, halo)
    sums[...] = jnp.zeros_like(sums)
    wait_all_recv(pv)
    params[...] = jnp.concatenate([parts[zz].astype(F32)[:, :shard] for zz in range(nz)], axis=1)
    spread_z(2)

    def norm_one(first, count):
        def step(i):
            rs = pl.ds(pl.multiple_of(first + i * tile_r, tile_r), tile_r)
            n, _ = normed(buf[rs, :].astype(F32))
            u = n * vec(G1) + vec(S1)
            buf[rs, :] = (u * phi(u)).astype(BF)

        for_each(count // tile_r, step)

    one_out = []
    for m in range(micro):
        block_load[m].wait()
        norm_one(m * extent + halo, rows)
        one_out.append(store(buf.at[at_rows(m, halo, rows)], act_one.at[m], m))

    branch_out = []
    for m in range(micro):
        pull_load[m].wait()

        def pull(i, m=m):
            rs = span(i, tile_r)
            weight = row_scale(item, weights, m, pl.multiple_of(halo + i * tile_r, tile_r), tile_r)
            value = (held[m, rs, :].astype(F32) * wide(weight, width)).astype(BF)
            held[m, rs, :] = value
            sums[BX] += fold(value.astype(F32))

        for_each(rows // tile_r, pull)
        branch_out.append(store(held.at[m, pl.ds(0, rows)], grad_branch.at[m], micro + m))
    tick(0)

    def norm_sides(m):
        with_left(lambda: block_right(m).wait_recv())
        with_right(lambda: block_left(m).wait_recv())
        norm_one(m * extent, halo)
        norm_one(m * extent + halo + rows, halo)

    norm_sides(0)
    tick(1)
    for m in range(1, micro):
        block_sides(m)
    tick(2)
    norm_sides(1)
    forward_sides(block_hop, block_pass)
    tick(3)
    arrived(0)

    wait_all(tap_loads[0])
    wait_all(branch_out)
    inner_out = []

    def norm_two(m, source, first, count):
        def step(i):
            n, _ = normed(total[m, pl.ds(pl.multiple_of(source + i * tile_r, tile_r), tile_r), :])
            u = n * vec(G2) + vec(S2)
            rs = pl.ds(pl.multiple_of(first + i * tile_r, tile_r), tile_r)
            held[m, rs, :] = (u * phi(u)).astype(BF)

        for_each(count // tile_r, step)

    def entry_tile(m, i, first):
        got = mm(buf[at_rows(m, first, tile_a), :], grads[pl.ds(0, width), :], NN)
        total[m, span(i, tile_a), :] = got + vec(BE)

    for m in range(micro):
        for_each(down, lambda i, m=m: entry_tile(m, i, halo + i * tile_a))
        inner_out.append(store(total.at[m], inner_one.at[m], 2 * micro + m))
        norm_two(m, 0, halo, rows)
        if m == 1:
            tick(4)
            arrived(1)
    norm_sides(2)
    for m in range(micro):
        inner_out[m].wait()
        for_each(halo // tile_a, lambda i, m=m: entry_tile(m, i, i * tile_a))
        for_each(halo // tile_a, lambda i, m=m: entry_tile(m, halo // tile_a + i, halo + rows + i * tile_a))
        norm_two(m, 0, 0, halo)
        norm_two(m, halo, halo + rows, halo)
        if m == 1:
            tick(5)
    arrived(2)
    wait_all(one_out)
    branch_in = [load(grad_branch.at[m], buf.at[pl.ds(m * rows, rows)], m) for m in range(micro)]

    wait_all(tap_loads[1])
    three_out = []
    for m in range(micro):
        branch_in[m].wait()

        def exit_back(i, m=m):
            left = buf[pl.ds(pl.multiple_of(m * rows + i * tile_a, tile_a), tile_a), :]
            total[m, span(i, tile_a), :] = mm(left, grads[pl.ds(width, width), :], NN)

        for_each(down, exit_back)
        three_out.append(store(total.at[m], grad_three.at[m], 2 * micro + m))
    tick(6)
    arrived(3)
    wait_all(three_out)

    def conv_tap(i):
        tap = TAP_ORDER[i - 2]
        wait_all(tap_loads[i])
        offset = (tap - KERNEL_TAPS // 2) * DILATION_STEP

        def step(n):
            m, r = n // down, pl.multiple_of(lax.rem(n, down) * tile_a, tile_a)
            rs = pl.ds(r, tile_a)
            left = held[m, pl.ds(pl.multiple_of(halo + offset + r, DILATION_STEP), tile_a), :]
            got = mm(left, grads[slot_rows(i), :], NN)
            got = got * wide(keep(item, m, tap, halo + r, tile_a), width)
            if i == 2:
                total[m, rs, :] = got
            else:
                total[m, rs, :] += got

        for_each(micro * down, step)

    for i in range(2, taps):
        conv_tap(i)
        if i == 2:
            tick(taps)
        if i == taps - 2:
            tick(taps + 1)
            arrived(taps - 1)
        elif i + 2 < taps - 1:
            arrived(i + 2)

    with_left(lambda: pl.semaphore_signal(ready.at[1], inc=1, device_id=place.left, device_id_type=MESH))
    with_right(lambda: pl.semaphore_signal(ready.at[0], inc=1, device_id=place.right, device_id_type=MESH))
    edges(grads)

    def fetch(source, n):
        m, r = n // per_block, lax.rem(n, per_block)
        slot = lax.rem(n, 2)
        return pltpu.make_async_copy(source.at[m, span(r, part)], chunk.at[slot], chunk_sem.at[slot])

    def chunked(source, m, work):
        def step(n, carry):
            @pl.when(n + 1 < micro * per_block)
            def _():
                fetch(source, n + 1).start()

            fetch(source, n).wait()
            for p in range(part // tile_r):
                r = pl.multiple_of((n - m * per_block) * part + p * tile_r, tile_r)
                work(m, r, chunk[lax.rem(n, 2), p * tile_r : (p + 1) * tile_r, :])
            return carry

        lax.fori_loop(m * per_block, (m + 1) * per_block, step, 0)

    def norm_three(m, r, grad_in):
        v = (total[m, pl.ds(r, tile_r), :] + vec(BC)).astype(BF).astype(F32)
        n, inverse = normed(v)
        u = n * vec(G3) + vec(S3)
        big_phi = phi(u)
        buf[pl.ds(pl.multiple_of((micro + m) * rows + r, tile_r), tile_r), :] = (u * big_phi).astype(BF)
        t = grad_in * slope(u, big_phi)
        sums[G3] += fold(t * n)
        sums[S3] += fold(t)
        grad = pull_back(t, n, inverse, vec(G3)).astype(BF)
        grads[at_rows(m, halo + r, tile_r), :] = grad
        sums[BC] += fold(grad.astype(F32))

    def grad_right(m):
        return send(grads.at[at_rows(m, rows, halo)], grads.at[at_rows(m, 0, halo)], halo_send.at[2, m], halo_recv.at[2, m], place.right)

    def grad_left(m):
        return send(grads.at[at_rows(m, halo, halo)], grads.at[at_rows(m, rows + halo, halo)], halo_send.at[3, m], halo_recv.at[3, m], place.left)

    def grad_hop(side):
        first = rows if side == 0 else halo
        return hop(2 + side, grads.at[at_rows(GRAD_RELAY, first, halo)])

    def grad_pass(side):
        first = 0 if side == 0 else rows + halo
        return pass_on(2 + side, GRAD_RELAY, grads.at[at_rows(GRAD_RELAY, first, halo)])

    fetch(grad_three, 0).start()
    act_out = []
    for m in range(micro):
        chunked(grad_three, m, norm_three)
        if m == 0:
            with_left(lambda: pl.semaphore_wait(ready.at[0], 1))
            with_right(lambda: pl.semaphore_wait(ready.at[1], 1))
        sides(m == GRAD_RELAY, grad_right(m), grad_left(m), grad_hop, lambda copy: copy.start())
        act_out.append(store(buf.at[pl.ds((micro + m) * rows, rows)], act_three.at[m], m))

    forward_sides(grad_hop, grad_pass)

    back = [1] + [2 + k for k in TAP_ORDER] + [0]
    last = taps - 1
    mine_a, mine_b = (1 - c) * x + c * y, c * x + (1 - c) * y
    sent = {}

    def block_at(other, mine):
        return (other * (2 - c) + mine * (1 + c)) * piece

    def stage_core(i):
        copy = send(out_core, in_core, core_send.at[i], core_recv.at[i], place.core)
        if i > 0:
            pl.semaphore_wait(credit.at[0], 1)
        copy.start()
        sent["core", i] = copy

    def used_core(i):
        if i < last:
            pl.semaphore_signal(credit.at[0], inc=1, device_id=place.core, device_id_type=MESH)

    def stage_w():
        sent["core", 0].wait_recv()
        for j in range(nz):
            rs = pl.ds(pl.multiple_of(place.up(j) * shard, 16), shard)
            value = own[rs, :].astype(F32) + in_core[rs, :].astype(F32)
            if j == 0:
                keep_w[...] = value
                continue
            out_w[j - 1] = value.astype(BF)
            copy = send(out_w.at[j - 1], in_w.at[j - 1], w_send.at[j - 1], w_recv.at[j - 1], place.above(j))
            copy.start()
            sent["w", j] = copy
        used_core(0)

    def stage_wa():
        value = keep_w[...]
        for j in others:
            sent["w", j].wait_recv()
            value = value + in_w[j - 1].astype(F32)
        keep_w[...] = value
        for other in range(2):
            gone = pl.ds(pl.multiple_of(block_at(other, 1 - mine_a), 16), piece)
            out_p[other] = keep_w[gone, :].astype(BF)
        copy = send(out_p.at[pl.ds(0, 2)], in_p.at[pl.ds(0, 2)], a_send.at[0], a_recv.at[0], place.peers(c)[0])
        copy.start()
        sent["a", 0] = copy

    def stage_wb():
        sent["a", 0].wait_recv()

        def total_of(other):
            rs = pl.ds(pl.multiple_of(block_at(other, mine_a), 16), piece)
            return keep_w[rs, :] + in_p[other].astype(F32)

        out_p[2] = total_of(1 - mine_b).astype(BF)
        keep_p[...] = total_of(mine_b)
        copy = send(out_p.at[2], in_p.at[2], b_send.at[0], b_recv.at[0], place.peers(c)[1])
        copy.start()
        sent["b", 0] = copy

    def stage_a(i):
        slot = i % 2
        sent["core", i].wait_recv()
        if i >= 3:
            sent["a", i - 2].wait_send()

        def step(n):
            base, other = (n // 2) * shard, lax.rem(n, 2)
            kept = pl.ds(pl.multiple_of(base + block_at(other, mine_a), 16), piece)
            gone = pl.ds(pl.multiple_of(base + block_at(other, 1 - mine_a), 16), piece)
            out_a[slot, n] = (own[gone, :].astype(F32) + in_core[gone, :].astype(F32)).astype(BF)
            keep_a[slot, n] = (own[kept, :].astype(F32) + in_core[kept, :].astype(F32)).astype(keep_a.dtype)

        for_each(2 * nz, step)
        if i > DEPTH:
            pl.semaphore_wait(credit.at[1], 1)
        copy = send(out_a.at[slot], in_a.at[i % DEPTH], a_send.at[i], a_recv.at[i], place.peers(c)[0])
        copy.start()
        sent["a", i] = copy
        used_core(i)

    def stage_b(i):
        slot = i % 2
        sent["a", i].wait_recv()
        if i >= 3:
            sent["b", i - 2].wait_send()

        def step(zz):
            kept, gone = 2 * zz + mine_b, 2 * zz + 1 - mine_b
            out_b[slot, zz] = (keep_a[slot, gone].astype(F32) + in_a[i % DEPTH, gone].astype(F32)).astype(BF)
            keep_b[slot, zz] = (keep_a[slot, kept].astype(F32) + in_a[i % DEPTH, kept].astype(F32)).astype(keep_b.dtype)

        for_each(nz, step)
        if i + DEPTH <= last:
            pl.semaphore_signal(credit.at[1], inc=1, device_id=place.peers(c)[0], device_id_type=MESH)
        if i > DEPTH:
            pl.semaphore_wait(credit.at[2], 1)
        copy = send(out_b.at[slot], in_b.at[i % DEPTH], b_send.at[i], b_recv.at[i], place.peers(c)[1])
        copy.start()
        sent["b", i] = copy

    def stage_z(i):
        slot = i % 2
        sent["b", i].wait_recv()
        for j in range(nz):
            if j > 0 and i >= 3:
                sent["z", i - 2, j].wait_send()
            zz = place.up(j)
            value = keep_b[slot, zz].astype(F32) + in_b[i % DEPTH, zz].astype(F32)
            if j == 0:
                keep_z[slot] = value
                continue
            out_z[slot, j - 1] = value.astype(BF)
            copy = send(out_z.at[slot, j - 1], in_z.at[i - 1, j - 1], z_send.at[i, j - 1], z_recv.at[i, j - 1], place.above(j))
            copy.start()
            sent["z", i, j] = copy
        used_b(i)

    def used_b(i):
        if i + DEPTH <= last:
            pl.semaphore_signal(credit.at[2], inc=1, device_id=place.peers(c)[1], device_id_type=MESH)

    def share_at(i, first, count):
        return shares.at[back[i], pl.ds(pl.multiple_of(first * piece, 16), count * piece), cols]

    def stage_f(i):
        slot = i % 2
        if i == 0:
            sent["b", 0].wait_recv()
            value = keep_p[...] + in_p[2].astype(F32)
        else:
            value = keep_z[slot]
            for j in others:
                sent["z", i, j].wait_recv()
                value = value + in_z[i - 1, j - 1].astype(F32)
        if i >= 2:
            sent["f", i - 2].wait_send()
        final[slot] = value.astype(BF)
        here = pltpu.make_async_copy(final.at[slot], share_at(i, q, 1), f_own.at[i])
        here.start()
        copy = send(final.at[slot], share_at(i, q, 1), f_send.at[i], f_recv.at[i], place.peers(c)[0])
        copy.start()
        sent["f", i] = copy
        sent["own", i] = here

    def stage_g(i):
        sent["own", i].wait()
        sent["f", i].wait_recv()
        for n, which in enumerate((q, place.partner(c))):
            block = share_at(i, which, 1)
            copy = send(block, block, g_send.at[i, n], g_recv.at[i, n], place.peers(c)[1])
            copy.start()
            sent["g", i, n] = copy

    def stage_h(i):
        for n in range(2):
            sent["g", i, n].wait_recv()
        block = share_at(i, 0, 4)
        copy = send(block, block, h_send.at[i], h_recv.at[i], place.core)
        copy.start()
        sent["h", i] = copy

    def weight_grad(i, product):
        if i > 0:
            sent["core", i - 1].wait_send()

        def far(n):
            ms = span(n, tile_m)
            out_core[ms, :] = product(ms, core_cols).astype(BF)

        for_each(width // tile_m, far)
        stage_core(i)

        def near(n):
            ms = span(n, tile_m)
            own[ms, :] = product(ms, cols).astype(own.dtype)

        for_each(width // tile_m, near)
        if i == 0:
            stage_w()
        else:
            stage_a(i)

    weight_grad(0, lambda ms, ns: mm(buf[low, ms], buf[high, ns], TN))
    wait_all(act_out)

    def fetch_tap(t):
        return load_tap(place, shards[t], gathered.at[t], buf.at[tap_rows], tap_sem.at[0])

    def back_tap(n, k):
        offset = (k - KERNEL_TAPS // 2) * DILATION_STEP

        def step(i):
            m, r = i // down, pl.multiple_of(lax.rem(i, down) * tile_a, tile_a)
            rs = pl.ds(r, tile_a)
            first = pl.multiple_of(m * extent + halo - offset + r, DILATION_STEP)
            got = mm(grads[pl.ds(first, tile_a), :], buf[tap_rows, :], NT)
            got = got * wide(keep(item, m, KERNEL_TAPS - 1 - k, halo + r, tile_a), width)
            if n == 0:
                total[m, rs, :] = got
            else:
                total[m, rs, :] += got

        for_each(micro * down, step)

    tap_in = fetch_tap(2 + TAP_ORDER[0])
    for n, k in enumerate(TAP_ORDER):

        def masked(i, k=k):
            m, r = i // (rows // 128), lax.rem(i, rows // 128)
            first = pl.multiple_of(halo + r * 128, 128)
            mask = keep(item, m, k, first, 128)
            value = grads[at_rows(m, first, 128), :].astype(F32) * wide(mask, width)
            buf[span(i, 128), :] = value.astype(BF)

        for_each(micro * rows // 128, masked)
        start = halo + (k - KERNEL_TAPS // 2) * DILATION_STEP

        def product(ms, ns, start=start):
            got = None
            for m in range(micro):
                one = mm(held[m, pl.ds(start, rows), ms], buf[pl.ds(m * rows, rows), ns], TN)
                got = one if got is None else got + one
            return got

        weight_grad(n + 1, product)
        if n == 1:
            for m in range(micro):
                with_left(lambda m=m: grad_right(m).wait_recv())
                with_right(lambda m=m: grad_left(m).wait_recv())
        if n == 2:
            stage_wa()
        elif n == 3:
            stage_wb()
        elif n == 4:
            stage_f(0)
        wait_all(tap_in)
        back_tap(n, k)
        if n + 1 < len(TAP_ORDER):
            tap_in = fetch_tap(2 + TAP_ORDER[n + 1])
        if n == 3:
            stage_f(1)
        elif n == 4:
            stage_g(0)
            stage_g(1)
            stage_f(2)
        if n >= 2:
            stage_z(n - 1)
        if n >= 1:
            stage_b(n)

    entry_in = fetch_tap(0)
    one_in = [load(act_one.at[m], held.at[m, pl.ds(0, rows)], m) for m in range(micro)]
    block_load = [load(block_in.at[m], held.at[m, pl.ds(rows, rows)], micro + m) for m in range(micro)]
    for m in range(micro):
        sides(m == GRAD_RELAY, grad_right(m), grad_left(m), grad_hop, lambda copy: copy.wait_send())
    pull_in = [load(cotangent.at[m], grads.at[at_rows(m, 0, rows)], 2 * micro + m) for m in range(micro)]

    def norm_two_back(m, r, inner):
        n, inverse = normed(inner)
        u = n * vec(G2) + vec(S2)
        t = total[m, pl.ds(r, tile_r), :] * slope(u, phi(u))
        sums[G2] += fold(t * n)
        sums[S2] += fold(t)
        grad = pull_back(t, n, inverse, vec(G2)).astype(BF)
        buf[pl.ds(pl.multiple_of(m * rows + r, tile_r), tile_r), :] = grad
        sums[BE] += fold(grad.astype(F32))

    fetch(inner_one, 0).start()
    for m in range(micro):
        chunked(inner_one, m, norm_two_back)
        if m == 0:
            stage_z(4)
            stage_b(5)
        elif m == 1:
            stage_h(0)
            stage_h(1)
            stage_g(2)
            stage_f(3)
        else:
            stage_f(4)

    wait_all(one_in)

    def entry_product(ms, ns):
        got = None
        for m in range(micro):
            one = mm(held[m, pl.ds(0, rows), ms], buf[pl.ds(m * rows, rows), ns], TN)
            got = one if got is None else got + one
        return got

    weight_grad(last, entry_product)
    stage_h(2)
    stage_g(3)
    stage_z(5)
    three_again = [load(act_three.at[m], held.at[m, pl.ds(0, rows)], m) for m in range(micro)]

    wait_all(entry_in)

    def entry_back(i):
        m, r = i // down, lax.rem(i, down)
        total[m, span(r, tile_a), :] = mm(buf[span(i, tile_a), :], buf[tap_rows, :], NT)

    for_each(micro * down, entry_back)
    exit_in = fetch_tap(1)
    stage_h(3)
    stage_g(4)
    stage_f(5)
    stage_b(6)
    stores = []
    for m in range(micro):
        block_load[m].wait()
        pull_in[m].wait()

        def norm_one_back(i, m=m):
            rs = span(i, tile_r)
            n, inverse = normed(held[m, pl.ds(pl.multiple_of(rows + i * tile_r, tile_r), tile_r), :].astype(F32))
            u = n * vec(G1) + vec(S1)
            t = total[m, rs, :] * slope(u, phi(u))
            sums[G1] += fold(t * n)
            sums[S1] += fold(t)
            grad = pull_back(t, n, inverse, vec(G1))
            there = at_rows(m, i * tile_r, tile_r)
            weight = row_scale(item, weights, m, pl.multiple_of(halo + i * tile_r, tile_r), tile_r)
            pulled = grads[there, :].astype(F32) * wide(weight, width)
            grads[there, :] = (pulled + grad).astype(BF)

        for_each(rows // tile_r, norm_one_back)
        stores.append(store(grads.at[at_rows(m, 0, rows)], input_grad.at[m], micro + m))
        if m == 0:
            stage_h(4)
            stage_g(5)
            stage_z(6)
    stage_h(5)
    stage_f(6)

    vec_part[0] = jnp.zeros_like(vec_part[0])
    for r in range(sums.shape[0]):
        vec_part[0, r : r + 1, :] = jnp.sum(sums[r], axis=0, keepdims=True)

    def vec_stage(n, peer):
        copy = send(vec_part.at[n], vec_in.at[n], vec_send.at[n], vec_recv.at[n], peer)
        copy.start()
        sent["v", n] = copy

    def vec_add(n):
        sent["v", n].wait_recv()
        vec_part[n + 1] = vec_part[n] + vec_in[n]

    vec_stage(0, place.core)

    wait_all(exit_in)
    for m in range(micro):
        three_again[m].wait()

        def exit_step(i, m=m):
            got = mm(held[m, span(i, tile_a), :], buf[tap_rows, :], NT) + vec(BX)
            rs = pl.ds(pl.multiple_of(rows + i * tile_a, tile_a), tile_a)
            held[m, rs, :] = (held[m, rs, :].astype(F32) + got).astype(BF)

        for_each(down, exit_step)
        stores.append(store(held.at[m, pl.ds(rows, rows)], block_out.at[m], 2 * micro + m))
        vec_add(m)
        if m == 0:
            vec_stage(1, place.px)
        elif m == 1:
            vec_stage(2, place.py)
    stage_g(6)
    for j in others:
        copy = send(vec_part.at[3], vec_in.at[2 + j], vec_send.at[2 + j], vec_recv.at[2 + j], place.above(j))
        copy.start()
        sent["v", 2 + j] = copy
    stage_h(6)
    value = vec_part[3]
    for j in others:
        sent["v", 2 + j].wait_recv()
        value = value + vec_in[2 + j]
    vec_out[...] = value
    for i in range(taps):
        sent["h", i].wait_recv()
    wait_all(stores)

    for m in range(micro):
        sides(m == BLOCK_RELAY, block_right(m), block_left(m), block_hop, lambda copy: copy.wait_send())
    for side, here in ((0, at_end), (1, at_start)):

        @pl.when(here)
        def _(side=side):
            block_pass(side).wait_send()
            grad_pass(side).wait_send()

    for copy in pv + list(zg.values()) + list(ag.values()) + list(cg.values()):
        copy.wait_send()
    for (t, j), copies in bg.items():
        for copy in copies:
            if copy is not zg[t, j]:
                copy.wait_send()
    sent["core", last].wait_send()
    for key, copy in sent.items():
        late = key[0] in ("a", "b", "z", "f") and key[1] >= last - 1
        if late or key in (("a", 0), ("b", 0)) or key[0] in ("g", "h", "v", "w"):
            copy.wait_send()


def run_block(block_in, cotangent, lengths, weights, vectors, entry, conv, exit_t):
    micro, rows, width = block_in.shape
    halo = (KERNEL_TAPS // 2) * DILATION_STEP
    taps = conv.shape[0] + 2
    nz = lax.axis_size("fsdp")
    extent = rows + 2 * halo
    shard = entry.shape[0]
    piece = shard // 4
    half = width // 2
    shape = jax.ShapeDtypeStruct
    anywhere = pl.BlockSpec(memory_space=pl.ANY)
    near = pl.BlockSpec(memory_space=pltpu.VMEM)
    scalars = pl.BlockSpec(memory_space=pltpu.SMEM)
    dma = pltpu.SemaphoreType.DMA
    vmem = pltpu.VMEM
    flops = 2 * micro * rows * width * width * (3 * taps)
    return pl.pallas_call(
        block_kernel,
        out_shape=(
            shape((micro, rows, width), BF),
            shape((micro, rows, width), BF),
            shape((taps, shard, width), BF),
            shape((VECTORS, width), F32),
            shape((taps, width, width), BF),
            shape((micro, rows, width), BF),
            shape((micro, rows, width), F32),
            shape((micro, rows, width), BF),
            shape((micro, rows, width), F32),
            shape((micro, rows, width), BF),
            shape((4, halo, width), BF),
        ),
        in_specs=[anywhere, anywhere, scalars, scalars, near, anywhere, anywhere, anywhere],
        out_specs=(anywhere, anywhere, anywhere, near) + (anywhere,) * 7,
        scratch_shapes=[
            vmem((micro, extent, width), BF),
            vmem((micro, rows, width), F32),
            vmem((micro * extent, width), BF),
            vmem((micro * extent, width), BF),
            vmem((2, 128, width), F32),
            vmem((micro, extent, LANES), jnp.int32),
            vmem((VECTORS, width), F32),
            vmem((nz,) + vectors.shape, BF),
            vmem((9, 8, width), F32),
            vmem((width, half), BF),
            vmem((width, half), BF),
            vmem((width, half), BF),
            vmem((DEPTH, 2 * nz, piece, half), BF),
            vmem((2, 2 * nz, piece, half), BF),
            vmem((2, 2 * nz, piece, half), BF),
            vmem((DEPTH, nz, piece, half), BF),
            vmem((2, nz, piece, half), BF),
            vmem((2, nz, piece, half), BF),
            vmem((taps - 1, nz - 1, piece, half), BF),
            vmem((2, nz - 1, piece, half), BF),
            vmem((2, piece, half), F32),
            vmem((2, piece, half), BF),
            vmem((nz - 1, shard, half), BF),
            vmem((nz - 1, shard, half), BF),
            vmem((shard, half), F32),
            vmem((3, piece, half), BF),
            vmem((3, piece, half), BF),
            vmem((piece, half), F32),
            vmem((4, VECTORS, width), F32),
            vmem((2 + nz, VECTORS, width), F32),
            dma((nz - 1,)),
            dma((nz - 1,)),
            dma((taps, nz - 1)),
            dma((taps, nz - 1)),
            dma((taps, nz - 1)),
            dma((taps, nz - 1)),
            dma((taps, nz - 1, 2)),
            dma((taps, nz - 1, 2)),
            dma((taps, nz - 1)),
            dma((taps, nz - 1)),
            dma((4, micro)),
            dma((4, micro)),
            dma((4,)),
            dma((4,)),
            dma((4,)),
            dma((taps,)),
            dma((taps,)),
            dma((taps,)),
            dma((taps,)),
            dma((taps,)),
            dma((taps,)),
            dma((taps, nz - 1)),
            dma((taps, nz - 1)),
            dma((taps,)),
            dma((taps,)),
            dma((taps,)),
            dma((taps, 2)),
            dma((taps, 2)),
            dma((taps,)),
            dma((taps,)),
            dma((nz - 1,)),
            dma((nz - 1,)),
            dma((2 + nz,)),
            dma((2 + nz,)),
            dma((3 * micro,)),
            dma((3 * micro,)),
            dma((2, nz)),
            dma((2,)),
            pltpu.SemaphoreType.REGULAR((2,)),
            pltpu.SemaphoreType.REGULAR((3,)),
        ],
        compiler_params=pltpu.CompilerParams(
            collective_id=1, has_side_effects=True, vmem_limit_bytes=VMEM_MOST
        ),
        cost_estimate=pl.CostEstimate(flops=flops, bytes_accessed=160 << 20, transcendentals=0),
        name="residual_block",
    )(block_in, cotangent, lengths, weights, vectors, entry, conv, exit_t)


def kernels_on_device(
    block_in,
    cotangent,
    lengths,
    item_weights,
    first_gain,
    first_shift,
    entry_weight,
    entry_bias,
    middle_gain,
    middle_shift,
    conv_weight,
    conv_bias,
    final_gain,
    final_shift,
    exit_weight,
    exit_bias,
):
    shard = entry_weight.shape[0]
    rows = [
        first_gain,
        first_shift,
        entry_bias,
        middle_gain,
        middle_shift,
        conv_bias,
        final_gain,
        final_shift,
        exit_bias,
    ]
    padded = -(-shard // LANES) * LANES
    place = lax.broadcasted_iota(jnp.int32, (VECTORS, padded), 0)
    vectors = jnp.zeros((VECTORS, padded), BF)
    for r, row in enumerate(rows):
        vectors = jnp.where(place == r, jnp.pad(row, (0, padded - shard))[None, :], vectors)
    outputs, input_grads, shares, sums = run_block(
        block_in, cotangent, lengths, item_weights, vectors, entry_weight, conv_weight, exit_weight.T
    )[:4]
    own_sums = lax.dynamic_slice_in_dim(sums, lax.axis_index("fsdp") * shard, shard, axis=1)
    vec = [own_sums[r] for r in range(len(rows))]
    return (
        outputs,
        input_grads,
        vec[G1],
        vec[S1],
        shares[0].astype(F32),
        vec[BE],
        vec[G2],
        vec[S2],
        shares[2:].astype(F32),
        vec[BC],
        vec[G3],
        vec[S3],
        shares[1].astype(F32).T,
        vec[BX],
    )


def fits(mesh):
    return mesh.shape["seq"] == 8


def norm_act(values, scale_vec, shift_vec):
    row_mean = jnp.mean(values, axis=-1, keepdims=True)
    centred = values - row_mean
    spread = jnp.mean(centred * centred, axis=-1, keepdims=True)
    return jax.nn.gelu(
        centred * lax.rsqrt(spread + eps_norm) * scale_vec + shift_vec, approximate=False
    )


def column_product(left, right):
    return lax.dot_general(
        left, right, (((0,), (0,)), ((), ())), preferred_element_type=jnp.float32
    )


def row_product(left, right):
    return lax.dot_general(
        left, right, (((1,), (1,)), ((), ())), preferred_element_type=jnp.float32
    )


def items_at(residue_position, item_lengths, stream_len):
    item_places = jnp.arange(item_lengths.shape[0], dtype=jnp.int32)
    ends = jnp.sum(
        jnp.where(item_places[:, None] <= item_places[None, :], item_lengths[:, None], 0), axis=0
    )
    inside = (residue_position >= 0) & (residue_position < stream_len)
    seg_all = jnp.sum((residue_position[:, None] >= ends[None, :]).astype(jnp.int32), axis=1)
    return jnp.where(inside, seg_all, -1)


def stacked(extended, segment_extended, tap_offset, row_count, item_count):
    half_reach = KERNEL_TAPS // 2
    middle_tap = segment_extended[half_reach * tap_offset : half_reach * tap_offset + row_count]
    tap_parts = []
    for kernel_tap_index in range(KERNEL_TAPS):
        segment_tapped = segment_extended[
            kernel_tap_index * tap_offset : kernel_tap_index * tap_offset + row_count
        ]
        keep_mask = (
            (segment_tapped == middle_tap) & (segment_tapped >= 0) & (segment_tapped < item_count)
        )
        tap_parts.append(
            extended[kernel_tap_index * tap_offset : kernel_tap_index * tap_offset + row_count]
            * keep_mask[:, None].astype(extended.dtype)
        )
    return jnp.concatenate(tap_parts, axis=1)


def on_device(
    block_in,
    cotangent,
    lengths,
    item_weights,
    first_gain,
    first_shift,
    entry_weight,
    entry_bias,
    middle_gain,
    middle_shift,
    conv_weight,
    conv_bias,
    final_gain,
    final_shift,
    exit_weight,
    exit_bias,
):
    micro_count = block_in.shape[0]
    row_count = block_in.shape[1]
    model_width = block_in.shape[2]
    inner_width = entry_weight.shape[1]
    item_count = lengths.shape[2]
    sequence_count = lax.axis_size("seq")
    seq_place = lax.axis_index("seq")
    stream_len = row_count * sequence_count
    half_reach = KERNEL_TAPS // 2
    totals = [
        jnp.zeros((model_width,), jnp.float32),
        jnp.zeros((model_width,), jnp.float32),
        jnp.zeros((model_width, inner_width), jnp.float32),
        jnp.zeros((inner_width,), jnp.float32),
        jnp.zeros((inner_width,), jnp.float32),
        jnp.zeros((inner_width,), jnp.float32),
        jnp.zeros((KERNEL_TAPS, inner_width, inner_width), jnp.float32),
        jnp.zeros((inner_width,), jnp.float32),
        jnp.zeros((inner_width,), jnp.float32),
        jnp.zeros((inner_width,), jnp.float32),
        jnp.zeros((inner_width, model_width), jnp.float32),
        jnp.zeros((model_width,), jnp.float32),
    ]
    outputs = []
    input_grads = []
    for micro_index in range(micro_count):
        params = (
            lax.all_gather(first_gain, "fsdp", axis=0, tiled=True),
            lax.all_gather(first_shift, "fsdp", axis=0, tiled=True),
            lax.all_gather(entry_weight, "fsdp", axis=0, tiled=True),
            lax.all_gather(entry_bias, "fsdp", axis=0, tiled=True),
            lax.all_gather(middle_gain, "fsdp", axis=0, tiled=True),
            lax.all_gather(middle_shift, "fsdp", axis=0, tiled=True),
            lax.all_gather(conv_weight, "fsdp", axis=1, tiled=True),
            lax.all_gather(conv_bias, "fsdp", axis=0, tiled=True),
            lax.all_gather(final_gain, "fsdp", axis=0, tiled=True),
            lax.all_gather(final_shift, "fsdp", axis=0, tiled=True),
            lax.all_gather(exit_weight, "fsdp", axis=1, tiled=True),
            lax.all_gather(exit_bias, "fsdp", axis=0, tiled=True),
        )
        (
            gain_one,
            shift_one,
            weight_in,
            bias_in,
            gain_two,
            shift_two,
            weight_conv,
            bias_conv,
            gain_three,
            shift_three,
            weight_out,
            bias_out,
        ) = params
        item_lengths = lengths[micro_index, 0]
        weight_row = item_weights[micro_index, 0]
        own_position = seq_place * row_count + jnp.arange(row_count, dtype=jnp.int32)
        seg_own = items_at(own_position, item_lengths, stream_len)
        match = seg_own[:, None] == jnp.arange(item_count, dtype=jnp.int32)[None, :]
        row_scale = jnp.sum(jnp.where(match, weight_row[None, :], 0), axis=1).astype(jnp.float32)
        inputs = block_in[micro_index].astype(jnp.float32)
        normed_one, back_one = jax.vjp(
            norm_act, inputs, gain_one.astype(jnp.float32), shift_one.astype(jnp.float32)
        )
        act_one = normed_one.astype(jnp.bfloat16)
        inner_one = jnp.dot(
            act_one, weight_in, preferred_element_type=jnp.float32
        ) + bias_in.astype(jnp.float32)
        normed_two, back_two = jax.vjp(
            norm_act, inner_one, gain_two.astype(jnp.float32), shift_two.astype(jnp.float32)
        )
        second_activation = normed_two.astype(jnp.bfloat16)
        flat_conv = weight_conv.reshape(KERNEL_TAPS * inner_width, inner_width)
        flip_conv = (
            jnp.flip(weight_conv, 0)
            .transpose(0, 2, 1)
            .reshape(KERNEL_TAPS * inner_width, inner_width)
        )
        tap_offset = DILATION_STEP // sequence_count
        residue_position = (
            sequence_count
            * (
                jnp.arange(row_count + 2 * half_reach * tap_offset, dtype=jnp.int32)
                - half_reach * tap_offset
            )
            + seq_place
        )
        segment_extended = items_at(residue_position, item_lengths, stream_len)
        dealt = lax.all_to_all(
            second_activation.reshape(row_count // sequence_count, sequence_count, inner_width),
            "seq",
            split_axis=1,
            concat_axis=0,
            tiled=True,
        ).reshape(row_count, inner_width)
        extended = jnp.pad(dealt, ((half_reach * tap_offset, half_reach * tap_offset), (0, 0)))
        shifted_tap_rows = stacked(extended, segment_extended, tap_offset, row_count, item_count)
        dealt_out = (
            jnp.dot(shifted_tap_rows, flat_conv, preferred_element_type=jnp.float32)
            + bias_conv.astype(jnp.float32)
        ).astype(jnp.bfloat16)
        inner_two = lax.all_to_all(
            dealt_out.reshape(sequence_count, row_count // sequence_count, 1, inner_width),
            "seq",
            split_axis=0,
            concat_axis=2,
            tiled=True,
        ).reshape(row_count, inner_width)
        normed_three, back_three = jax.vjp(
            norm_act,
            inner_two.astype(jnp.float32),
            gain_three.astype(jnp.float32),
            shift_three.astype(jnp.float32),
        )
        act_three = normed_three.astype(jnp.bfloat16)
        branch = jnp.dot(
            act_three, weight_out, preferred_element_type=jnp.float32
        ) + bias_out.astype(jnp.float32)
        outputs.append((inputs + branch).astype(jnp.bfloat16))
        pulled = cotangent[micro_index].astype(jnp.float32) * row_scale[:, None]
        grad_branch = pulled.astype(jnp.bfloat16)
        sum_exit_weight = column_product(act_three, grad_branch)
        sum_exit_bias = jnp.sum(grad_branch.astype(jnp.float32), axis=0)
        grad_act_three = row_product(grad_branch, weight_out)
        grad_inner_two, sum_final_gain, sum_final_shift = back_three(grad_act_three)
        low_inner_two = grad_inner_two.astype(jnp.bfloat16)
        sum_conv_bias = jnp.sum(low_inner_two.astype(jnp.float32), axis=0)
        grad_dealt = lax.all_to_all(
            low_inner_two.reshape(row_count // sequence_count, sequence_count, inner_width),
            "seq",
            split_axis=1,
            concat_axis=0,
            tiled=True,
        ).reshape(row_count, inner_width)
        sum_conv_weight = column_product(shifted_tap_rows, grad_dealt)
        grad_ext = jnp.pad(grad_dealt, ((half_reach * tap_offset, half_reach * tap_offset), (0, 0)))
        dealt_back = jnp.dot(
            stacked(grad_ext, segment_extended, tap_offset, row_count, item_count),
            flip_conv,
            preferred_element_type=jnp.float32,
        )
        grad_act_two = lax.all_to_all(
            dealt_back.reshape(sequence_count, row_count // sequence_count, 1, inner_width),
            "seq",
            split_axis=0,
            concat_axis=2,
            tiled=True,
        ).reshape(row_count, inner_width)
        grad_inner_one, sum_middle_gain, sum_middle_shift = back_two(grad_act_two)
        low_inner_one = grad_inner_one.astype(jnp.bfloat16)
        sum_entry_weight = column_product(act_one, low_inner_one)
        sum_entry_bias = jnp.sum(low_inner_one.astype(jnp.float32), axis=0)
        grad_act_one = row_product(low_inner_one, weight_in)
        grad_inputs, sum_first_gain, sum_first_shift = back_one(grad_act_one)
        input_grads.append((pulled + grad_inputs).astype(jnp.bfloat16))
        fresh = (
            sum_first_gain,
            sum_first_shift,
            sum_entry_weight,
            sum_entry_bias,
            sum_middle_gain,
            sum_middle_shift,
            sum_conv_weight.reshape(KERNEL_TAPS, inner_width, inner_width),
            sum_conv_bias,
            sum_final_gain,
            sum_final_shift,
            sum_exit_weight,
            sum_exit_bias,
        )
        totals = [left + right for left, right in zip(totals, fresh)]
    shares = (
        lax.psum_scatter(totals[0], "fsdp", scatter_dimension=0, tiled=True),
        lax.psum_scatter(totals[1], "fsdp", scatter_dimension=0, tiled=True),
        lax.psum_scatter(totals[2], "fsdp", scatter_dimension=0, tiled=True),
        lax.psum_scatter(totals[3], "fsdp", scatter_dimension=0, tiled=True),
        lax.psum_scatter(totals[4], "fsdp", scatter_dimension=0, tiled=True),
        lax.psum_scatter(totals[5], "fsdp", scatter_dimension=0, tiled=True),
        lax.psum_scatter(totals[6], "fsdp", scatter_dimension=1, tiled=True),
        lax.psum_scatter(totals[7], "fsdp", scatter_dimension=0, tiled=True),
        lax.psum_scatter(totals[8], "fsdp", scatter_dimension=0, tiled=True),
        lax.psum_scatter(totals[9], "fsdp", scatter_dimension=0, tiled=True),
        lax.psum_scatter(totals[10], "fsdp", scatter_dimension=1, tiled=True),
        lax.psum_scatter(totals[11], "fsdp", scatter_dimension=0, tiled=True),
    )
    result = lax.psum(
        (
            shares[0],
            shares[1],
            shares[2],
            shares[3],
            shares[4],
            shares[5],
            shares[6],
            shares[7],
            shares[8],
            shares[9],
            shares[10],
            shares[11],
        ),
        "seq",
    )
    return (
        jnp.stack(outputs),
        jnp.stack(input_grads),
        result[0],
        result[1],
        result[2],
        result[3],
        result[4],
        result[5],
        result[6],
        result[7],
        result[8],
        result[9],
        result[10],
        result[11],
    )


def solution(mesh):
    in_specs = (
        P(None, ("fsdp", "seq"), None),
        P(None, ("fsdp", "seq"), None),
        P(None, "fsdp", None),
        P(None, "fsdp", None),
        P("fsdp"),
        P("fsdp"),
        P("fsdp", None),
        P("fsdp"),
        P("fsdp"),
        P("fsdp"),
        P(None, "fsdp", None),
        P("fsdp"),
        P("fsdp"),
        P("fsdp"),
        P(None, "fsdp"),
        P("fsdp"),
    )
    out_specs = (
        P(None, ("fsdp", "seq"), None),
        P(None, ("fsdp", "seq"), None),
        P("fsdp"),
        P("fsdp"),
        P("fsdp", None),
        P("fsdp"),
        P("fsdp"),
        P("fsdp"),
        P(None, "fsdp", None),
        P("fsdp"),
        P("fsdp"),
        P("fsdp"),
        P(None, "fsdp"),
        P("fsdp"),
    )
    body = kernels_on_device if fits(mesh) else on_device
    return jax.shard_map(
        body, mesh=mesh, in_specs=in_specs, out_specs=out_specs, check_vma=False
    )
```

```python
import functools
import math

import jax
import jax.numpy as jnp
from jax import lax
from jax.experimental import pallas as pl
from jax.experimental.pallas import tpu as pltpu
from jax.sharding import PartitionSpec as P

KERNEL_TAPS = 5
DILATION_STEP = 128


eps_norm = 1e-05

MESH = pl.DeviceIdType.MESH
BF = jnp.bfloat16
F32 = jnp.float32
LANES = 128
VMEM_MOST = 60 << 20
NN = (((1,), (0,)), ((), ()))
NT = (((1,), (1,)), ((), ()))
TN = (((0,), (0,)), ((), ()))
ROOT_HALF = math.sqrt(0.5)
PHI_SCALE = 1.0 / math.sqrt(2.0 * math.pi)
EXP2_SCALE = -0.5 * math.log2(math.e)
G1, S1, BE, G2, S2, BC, G3, S3, BX = range(9)
VECTORS = 16


def mm(left, right, dims):
    return lax.dot_general(left, right, dims, preferred_element_type=F32)


def normed(v):
    centred = v - jnp.mean(v, axis=-1, keepdims=True)
    inverse = lax.rsqrt(jnp.mean(centred * centred, axis=-1, keepdims=True) + eps_norm)
    return centred * inverse, inverse


def phi(u):
    return 0.5 + 0.5 * lax.erf(u * ROOT_HALF)


def slope(u, big_phi):
    return big_phi + u * (PHI_SCALE * jnp.exp2(u * u * EXP2_SCALE))


def fold(tile):
    return jnp.sum(tile.reshape(tile.shape[0] // 8, 8, tile.shape[1]), axis=0)


def pull_back(t, n, inverse, gain):
    at = t * gain
    return (
        at - jnp.mean(at, axis=-1, keepdims=True) - n * jnp.mean(at * n, axis=-1, keepdims=True)
    ) * inverse


def span(i, size):
    return pl.ds(pl.multiple_of(i * size, size), size)


def for_each(count, step):
    lax.fori_loop(0, count, lambda i, carry: (step(i), carry)[1], 0)


def wide(mask, width):
    return jnp.concatenate([mask] * (width // LANES), axis=1)


class Place:
    def __init__(self):
        self.z = lax.axis_index("fsdp")
        self.s = lax.axis_index("seq")
        self.nz = lax.axis_size("fsdp")
        self.ns = lax.axis_size("seq")
        s = self.s
        self.c = lax.rem(s, 2)
        self.x = lax.rem(s // 2, 2)
        self.y = s // 4
        self.q = s // 2
        self.core = (self.z, s + 1 - 2 * self.c)
        self.px = (self.z, s + 2 - 4 * self.x)
        self.py = (self.z, s + 4 - 8 * self.y)
        self.across = (self.z, s + 3 - 4 * self.x - 2 * self.c)
        self.left = (self.z, lax.rem(s + self.ns - 1, self.ns))
        self.right = (self.z, lax.rem(s + 1, self.ns))

    def up(self, j):
        return lax.rem(self.z + j, self.nz)

    def down(self, j):
        return lax.rem(self.z + self.nz - j, self.nz)

    def above(self, j):
        return (self.up(j), self.s)

    def peers(self, turn):
        along_x, along_y = 2 - 4 * self.x, 4 - 8 * self.y
        return (
            (self.z, self.s + (1 - turn) * along_x + turn * along_y),
            (self.z, self.s + turn * along_x + (1 - turn) * along_y),
        )

    def partner(self, turn):
        return self.q + (1 - turn) * (1 - 2 * self.x) + turn * (2 - 4 * self.y)

    def greet(self):
        peers = [self.core, self.px, self.py, self.across, self.left, self.right]
        peers += [self.above(j) for j in range(1, self.nz)]
        barrier = pltpu.get_barrier_semaphore()
        for peer in peers:
            pl.semaphore_signal(barrier, inc=1, device_id=peer, device_id_type=MESH)
        pl.semaphore_wait(barrier, len(peers))


def send(src, dst, send_sem, recv_sem, peer):
    return pltpu.make_async_remote_copy(
        src_ref=src,
        dst_ref=dst,
        send_sem=send_sem,
        recv_sem=recv_sem,
        device_id=peer,
        device_id_type=MESH,
    )


def load_tap(place, own, gathered, dst, sems):
    shard = own.shape[0]
    copies = []
    for j in range(place.nz):
        rows = pl.ds(pl.multiple_of(place.down(j) * shard, 16), shard)
        src = own if j == 0 else gathered.at[rows]
        copies.append(pltpu.make_async_copy(src, dst.at[rows], sems.at[j]))
    for copy in copies:
        copy.start()
    return copies


def wait_all(copies):
    for copy in copies:
        copy.wait()


def wait_all_recv(copies):
    for copy in copies:
        copy.wait_recv()


def find_items(place, lengths, item, micro, rows, halo):
    extent = rows + 2 * halo
    count = lengths.shape[2]
    for m in range(micro):
        position = lax.broadcasted_iota(jnp.int32, (extent, LANES), 0) + (place.s * rows - halo)
        found = jnp.zeros((extent, LANES), jnp.int32)
        end = jnp.int32(0)
        for j in range(count):
            end = end + lengths[m, 0, j]
            found = found + jnp.where(position >= end, 1, 0)
        inside = (position >= 0) & (position < place.ns * rows) & (found < count)
        item[m] = jnp.where(inside, found, -1)


def row_scale(item, weights, m, first, size):
    own = item[m, pl.ds(first, size)]
    total = jnp.zeros((size, LANES), jnp.int32)
    for j in range(weights.shape[2]):
        total = total + jnp.where(own == j, weights[m, 0, j], 0)
    return total.astype(F32)


def keep(item, m, tap, first, size):
    own = item[m, pl.ds(first, size)]
    there = pl.multiple_of(first + (tap - KERNEL_TAPS // 2) * DILATION_STEP, DILATION_STEP)
    other = item[m, pl.ds(there, size)]
    return jnp.where((own == other) & (own >= 0), 1.0, 0.0).astype(F32)


TAP_ORDER = (2, 1, 3, 0, 4)
WHOLE = (6,)
BLOCK_RELAY, GRAD_RELAY = 2, 0
DEPTH = 3


def block_kernel(
    block_in, cotangent, lengths, weights, vectors, entry, conv, exit_t,
    block_out, input_grad, shares, vec_out, gathered, act_one, inner_one, act_three, grad_three, grad_branch, relay,
    held, total, grads, buf, chunk, item, params, parts, sums,
    out_core, own, in_core, in_a, out_a, keep_a, in_b, out_b, keep_b, in_z, out_z, keep_z, final, in_w, out_w, keep_w, out_p, in_p, keep_p, vec_part, vec_in,
    pv_send, pv_recv, zg_send, zg_recv, ag_send, ag_recv, bg_send, bg_recv, cg_send, cg_recv, halo_send, halo_recv, hop_send, hop_recv, pass_send,
    core_send, core_recv, a_send, a_recv, b_send, b_recv, z_send, z_recv, f_own, f_send, f_recv, g_send, g_recv, h_send, h_recv, w_send, w_recv,
    vec_send, vec_recv, load_sem, store_sem, tap_sem, chunk_sem, ready, credit,
):
    place = Place()
    micro, rows, width = block_in.shape
    halo = (KERNEL_TAPS // 2) * DILATION_STEP
    extent = rows + 2 * halo
    z, c, q, x, y, nz = place.z, place.c, place.q, place.x, place.y, place.nz
    taps, shard, _ = shares.shape
    piece = shard // 4
    half = width // 2
    tile_a = 256
    tile_m = half
    tile_r = 128
    down = rows // tile_a
    part = chunk.shape[1]
    per_block = rows // part
    others = range(1, nz)
    at_start, at_end = place.s == 0, place.s == place.ns - 1
    low, high = pl.ds(0, micro * rows), pl.ds(micro * rows, micro * rows)
    tap_rows = pl.ds(micro * rows, width)
    cols = pl.ds(pl.multiple_of(c * half, LANES), half)
    core_cols = pl.ds(pl.multiple_of(half - c * half, LANES), half)
    shards = [entry, exit_t] + [conv.at[k] for k in range(taps - 2)]

    def vec(r):
        return params[r : r + 1, :]

    def at_rows(m, first, count):
        return pl.ds(pl.multiple_of(m * extent + first, 16), count)

    def load(src, dst, n):
        copy = pltpu.make_async_copy(src, dst, load_sem.at[n])
        copy.start()
        return copy

    def store(src, dst, n):
        copy = pltpu.make_async_copy(src, dst, store_sem.at[n])
        copy.start()
        return copy

    def with_left(step):
        pl.when(jnp.logical_not(at_start))(step)

    def with_right(step):
        pl.when(jnp.logical_not(at_end))(step)

    block_load = [load(block_in.at[m], buf.at[at_rows(m, halo, rows)], m) for m in range(micro)]
    pull_load = [load(cotangent.at[m], held.at[m, pl.ds(0, rows)], micro + m) for m in range(micro)]
    place.greet()

    order = [0, 1] + [2 + k for k in TAP_ORDER]
    zg, ag, bg, cg, tap_loads = {}, {}, {}, {}, {}

    def at(t, zz, first, count):
        start = pl.multiple_of(zz * shard + first * piece, 16)
        return gathered.at[t, pl.ds(start, count * piece), cols]

    def spread_z(i):
        t = order[i]
        first, count = (0, 4) if i in WHOLE else (q, 1)
        start = pl.multiple_of(first * piece, 16)
        for j in others:
            copy = send(shards[t].at[pl.ds(start, count * piece), cols], at(t, z, first, count), zg_send.at[t, j - 1], zg_recv.at[t, j - 1], place.above(j))
            copy.start()
            zg[t, j] = copy

    def spread_a(i):
        t = order[i]
        for j in others:
            if i in WHOLE:
                continue
            zg[t, j].wait_recv()
            block = at(t, place.down(j), q, 1)
            copy = send(block, block, ag_send.at[t, j - 1], ag_recv.at[t, j - 1], place.peers(c)[0])
            copy.start()
            ag[t, j] = copy

    def spread_b(i):
        t = order[i]
        for j in others:
            if i in WHOLE:
                bg[t, j] = [zg[t, j]]
                continue
            ag[t, j].wait_recv()
            copies = []
            for n, which in enumerate((q, place.partner(c))):
                block = at(t, place.down(j), which, 1)
                copy = send(block, block, bg_send.at[t, j - 1, n], bg_recv.at[t, j - 1, n], place.peers(c)[1])
                copy.start()
                copies.append(copy)
            bg[t, j] = copies

    def spread_c(i):
        t = order[i]
        for j in others:
            wait_all_recv(bg[t, j])
            block = at(t, place.down(j), 0, 4)
            copy = send(block, block, cg_send.at[t, j - 1], cg_recv.at[t, j - 1], place.core)
            copy.start()
            cg[t, j] = copy

    def slot_rows(i):
        return pl.ds((i % 2) * width, width)

    def arrived(i):
        t = order[i]
        for j in others:
            cg[t, j].wait_recv()
        tap_loads[i] = load_tap(place, shards[t], gathered.at[t], grads.at[slot_rows(i)], tap_sem.at[i % 2])

    def tick(i):
        for back, stage in ((-3, spread_z), (0, spread_a), (1, spread_b), (2, spread_c)):
            if 0 <= i - back < taps:
                stage(i - back)

    spread_z(0)
    pv = [
        send(vectors, parts.at[z], pv_send.at[j - 1], pv_recv.at[j - 1], place.above(j))
        for j in others
    ]
    for copy in pv:
        copy.start()
    parts[z] = vectors[...]

    def block_right(m):
        return send(block_in.at[m, pl.ds(rows - halo, halo)], buf.at[at_rows(m, 0, halo)], halo_send.at[0, m], halo_recv.at[0, m], place.right)

    def block_left(m):
        return send(block_in.at[m, pl.ds(0, halo)], buf.at[at_rows(m, rows + halo, halo)], halo_send.at[1, m], halo_recv.at[1, m], place.left)

    turns_right = (lax.rem(place.s, 4) == 3) & jnp.logical_not(at_end)
    turns_left = (lax.rem(place.s, 4) == 0) & jnp.logical_not(at_start)
    straight_right = jnp.logical_not(at_end | turns_right)
    straight_left = jnp.logical_not(at_start | turns_left)

    def hop(n, src):
        return send(src, relay.at[n], hop_send.at[n], hop_recv.at[n], place.py)

    def pass_on(n, m, dst):
        return send(relay.at[n], dst, pass_send.at[n], halo_recv.at[n, m], place.across)

    def block_hop(side):
        first = rows - halo if side == 0 else 0
        return hop(side, block_in.at[BLOCK_RELAY, pl.ds(first, halo)])

    def block_pass(side):
        first = 0 if side == 0 else rows + halo
        return pass_on(side, BLOCK_RELAY, buf.at[at_rows(BLOCK_RELAY, first, halo)])

    def sides(relayed, right, left, hop_of, act):
        if relayed:
            pl.when(straight_right)(lambda: act(right))
            pl.when(straight_left)(lambda: act(left))
            pl.when(turns_right)(lambda: act(hop_of(0)))
            pl.when(turns_left)(lambda: act(hop_of(1)))
        else:
            with_right(lambda: act(right))
            with_left(lambda: act(left))

    def forward_sides(hop_of, pass_of):
        for side, here in ((0, at_end), (1, at_start)):

            @pl.when(here)
            def _(side=side):
                hop_of(side).wait_recv()
                pass_of(side).start()

    def block_sides(m):
        sides(m == BLOCK_RELAY, block_right(m), block_left(m), block_hop, lambda copy: copy.start())

    block_sides(0)

    def edges(array):
        for m in range(micro):

            @pl.when(at_start)
            def _(m=m):
                array[at_rows(m, 0, halo), :] = jnp.zeros((halo, width), BF)

            @pl.when(at_end)
            def _(m=m):
                array[at_rows(m, rows + halo, halo), :] = jnp.zeros((halo, width), BF)

    edges(buf)
    spread_z(1)
    find_items(place, lengths, item, micro, rows, halo)
    sums[...] = jnp.zeros_like(sums)
    wait_all_recv(pv)
    params[...] = jnp.concatenate([parts[zz].astype(F32)[:, :shard] for zz in range(nz)], axis=1)
    spread_z(2)

    def norm_one(first, count):
        def step(i):
            rs = pl.ds(pl.multiple_of(first + i * tile_r, tile_r), tile_r)
            n, _ = normed(buf[rs, :].astype(F32))
            u = n * vec(G1) + vec(S1)
            buf[rs, :] = (u * phi(u)).astype(BF)

        for_each(count // tile_r, step)

    one_out = []
    for m in range(micro):
        block_load[m].wait()
        norm_one(m * extent + halo, rows)
        one_out.append(store(buf.at[at_rows(m, halo, rows)], act_one.at[m], m))

    branch_out = []
    for m in range(micro):
        pull_load[m].wait()

        def pull(i, m=m):
            rs = span(i, tile_r)
            weight = row_scale(item, weights, m, pl.multiple_of(halo + i * tile_r, tile_r), tile_r)
            value = (held[m, rs, :].astype(F32) * wide(weight, width)).astype(BF)
            held[m, rs, :] = value
            sums[BX] += fold(value.astype(F32))

        for_each(rows // tile_r, pull)
        branch_out.append(store(held.at[m, pl.ds(0, rows)], grad_branch.at[m], micro + m))
    tick(0)

    def norm_sides(m):
        with_left(lambda: block_right(m).wait_recv())
        with_right(lambda: block_left(m).wait_recv())
        norm_one(m * extent, halo)
        norm_one(m * extent + halo + rows, halo)

    norm_sides(0)
    tick(1)
    for m in range(1, micro):
        block_sides(m)
    tick(2)
    norm_sides(1)
    forward_sides(block_hop, block_pass)
    tick(3)
    arrived(0)

    wait_all(tap_loads[0])
    wait_all(branch_out)
    inner_out = []

    def norm_two(m, source, first, count):
        def step(i):
            n, _ = normed(total[m, pl.ds(pl.multiple_of(source + i * tile_r, tile_r), tile_r), :])
            u = n * vec(G2) + vec(S2)
            rs = pl.ds(pl.multiple_of(first + i * tile_r, tile_r), tile_r)
            held[m, rs, :] = (u * phi(u)).astype(BF)

        for_each(count // tile_r, step)

    def entry_tile(m, i, first):
        got = mm(buf[at_rows(m, first, tile_a), :], grads[pl.ds(0, width), :], NN)
        total[m, span(i, tile_a), :] = got + vec(BE)

    for m in range(micro):
        for_each(down, lambda i, m=m: entry_tile(m, i, halo + i * tile_a))
        inner_out.append(store(total.at[m], inner_one.at[m], 2 * micro + m))
        norm_two(m, 0, halo, rows)
        if m == 1:
            tick(4)
            arrived(1)
    norm_sides(2)
    for m in range(micro):
        inner_out[m].wait()
        for_each(halo // tile_a, lambda i, m=m: entry_tile(m, i, i * tile_a))
        for_each(halo // tile_a, lambda i, m=m: entry_tile(m, halo // tile_a + i, halo + rows + i * tile_a))
        norm_two(m, 0, 0, halo)
        norm_two(m, halo, halo + rows, halo)
        if m == 1:
            tick(5)
    arrived(2)
    wait_all(one_out)
    branch_in = [load(grad_branch.at[m], buf.at[pl.ds(m * rows, rows)], m) for m in range(micro)]

    wait_all(tap_loads[1])
    three_out = []
    for m in range(micro):
        branch_in[m].wait()

        def exit_back(i, m=m):
            left = buf[pl.ds(pl.multiple_of(m * rows + i * tile_a, tile_a), tile_a), :]
            total[m, span(i, tile_a), :] = mm(left, grads[pl.ds(width, width), :], NN)

        for_each(down, exit_back)
        three_out.append(store(total.at[m], grad_three.at[m], 2 * micro + m))
    tick(6)
    arrived(3)
    wait_all(three_out)

    def conv_tap(i):
        tap = TAP_ORDER[i - 2]
        wait_all(tap_loads[i])
        offset = (tap - KERNEL_TAPS // 2) * DILATION_STEP

        def step(n):
            m, r = n // down, pl.multiple_of(lax.rem(n, down) * tile_a, tile_a)
            rs = pl.ds(r, tile_a)
            left = held[m, pl.ds(pl.multiple_of(halo + offset + r, DILATION_STEP), tile_a), :]
            got = mm(left, grads[slot_rows(i), :], NN)
            got = got * wide(keep(item, m, tap, halo + r, tile_a), width)
            if i == 2:
                total[m, rs, :] = got
            else:
                total[m, rs, :] += got

        for_each(micro * down, step)

    for i in range(2, taps):
        conv_tap(i)
        if i == 2:
            tick(taps)
        if i == taps - 2:
            tick(taps + 1)
            arrived(taps - 1)
        elif i + 2 < taps - 1:
            arrived(i + 2)

    with_left(lambda: pl.semaphore_signal(ready.at[1], inc=1, device_id=place.left, device_id_type=MESH))
    with_right(lambda: pl.semaphore_signal(ready.at[0], inc=1, device_id=place.right, device_id_type=MESH))
    edges(grads)

    def fetch(source, n):
        m, r = n // per_block, lax.rem(n, per_block)
        slot = lax.rem(n, 2)
        return pltpu.make_async_copy(source.at[m, span(r, part)], chunk.at[slot], chunk_sem.at[slot])

    def chunked(source, m, work):
        def step(n, carry):
            @pl.when(n + 1 < micro * per_block)
            def _():
                fetch(source, n + 1).start()

            fetch(source, n).wait()
            for p in range(part // tile_r):
                r = pl.multiple_of((n - m * per_block) * part + p * tile_r, tile_r)
                work(m, r, chunk[lax.rem(n, 2), p * tile_r : (p + 1) * tile_r, :])
            return carry

        lax.fori_loop(m * per_block, (m + 1) * per_block, step, 0)

    def norm_three(m, r, grad_in):
        v = (total[m, pl.ds(r, tile_r), :] + vec(BC)).astype(BF).astype(F32)
        n, inverse = normed(v)
        u = n * vec(G3) + vec(S3)
        big_phi = phi(u)
        buf[pl.ds(pl.multiple_of((micro + m) * rows + r, tile_r), tile_r), :] = (u * big_phi).astype(BF)
        t = grad_in * slope(u, big_phi)
        sums[G3] += fold(t * n)
        sums[S3] += fold(t)
        grad = pull_back(t, n, inverse, vec(G3)).astype(BF)
        grads[at_rows(m, halo + r, tile_r), :] = grad
        sums[BC] += fold(grad.astype(F32))

    def grad_right(m):
        return send(grads.at[at_rows(m, rows, halo)], grads.at[at_rows(m, 0, halo)], halo_send.at[2, m], halo_recv.at[2, m], place.right)

    def grad_left(m):
        return send(grads.at[at_rows(m, halo, halo)], grads.at[at_rows(m, rows + halo, halo)], halo_send.at[3, m], halo_recv.at[3, m], place.left)

    def grad_hop(side):
        first = rows if side == 0 else halo
        return hop(2 + side, grads.at[at_rows(GRAD_RELAY, first, halo)])

    def grad_pass(side):
        first = 0 if side == 0 else rows + halo
        return pass_on(2 + side, GRAD_RELAY, grads.at[at_rows(GRAD_RELAY, first, halo)])

    fetch(grad_three, 0).start()
    act_out = []
    for m in range(micro):
        chunked(grad_three, m, norm_three)
        if m == 0:
            with_left(lambda: pl.semaphore_wait(ready.at[0], 1))
            with_right(lambda: pl.semaphore_wait(ready.at[1], 1))
        sides(m == GRAD_RELAY, grad_right(m), grad_left(m), grad_hop, lambda copy: copy.start())
        act_out.append(store(buf.at[pl.ds((micro + m) * rows, rows)], act_three.at[m], m))

    forward_sides(grad_hop, grad_pass)

    back = [1] + [2 + k for k in TAP_ORDER] + [0]
    last = taps - 1
    mine_a, mine_b = (1 - c) * x + c * y, c * x + (1 - c) * y
    sent = {}

    def block_at(other, mine):
        return (other * (2 - c) + mine * (1 + c)) * piece

    def stage_core(i):
        copy = send(out_core, in_core, core_send.at[i], core_recv.at[i], place.core)
        if i > 0:
            pl.semaphore_wait(credit.at[0], 1)
        copy.start()
        sent["core", i] = copy

    def used_core(i):
        if i < last:
            pl.semaphore_signal(credit.at[0], inc=1, device_id=place.core, device_id_type=MESH)

    def stage_w():
        sent["core", 0].wait_recv()
        for j in range(nz):
            rs = pl.ds(pl.multiple_of(place.up(j) * shard, 16), shard)
            value = own[rs, :].astype(F32) + in_core[rs, :].astype(F32)
            if j == 0:
                keep_w[...] = value
                continue
            out_w[j - 1] = value.astype(BF)
            copy = send(out_w.at[j - 1], in_w.at[j - 1], w_send.at[j - 1], w_recv.at[j - 1], place.above(j))
            copy.start()
            sent["w", j] = copy
        used_core(0)

    def stage_wa():
        value = keep_w[...]
        for j in others:
            sent["w", j].wait_recv()
            value = value + in_w[j - 1].astype(F32)
        keep_w[...] = value
        for other in range(2):
            gone = pl.ds(pl.multiple_of(block_at(other, 1 - mine_a), 16), piece)
            out_p[other] = keep_w[gone, :].astype(BF)
        copy = send(out_p.at[pl.ds(0, 2)], in_p.at[pl.ds(0, 2)], a_send.at[0], a_recv.at[0], place.peers(c)[0])
        copy.start()
        sent["a", 0] = copy

    def stage_wb():
        sent["a", 0].wait_recv()

        def total_of(other):
            rs = pl.ds(pl.multiple_of(block_at(other, mine_a), 16), piece)
            return keep_w[rs, :] + in_p[other].astype(F32)

        out_p[2] = total_of(1 - mine_b).astype(BF)
        keep_p[...] = total_of(mine_b)
        copy = send(out_p.at[2], in_p.at[2], b_send.at[0], b_recv.at[0], place.peers(c)[1])
        copy.start()
        sent["b", 0] = copy

    def stage_a(i):
        slot = i % 2
        sent["core", i].wait_recv()
        if i >= 3:
            sent["a", i - 2].wait_send()

        def step(n):
            base, other = (n // 2) * shard, lax.rem(n, 2)
            kept = pl.ds(pl.multiple_of(base + block_at(other, mine_a), 16), piece)
            gone = pl.ds(pl.multiple_of(base + block_at(other, 1 - mine_a), 16), piece)
            out_a[slot, n] = (own[gone, :].astype(F32) + in_core[gone, :].astype(F32)).astype(BF)
            keep_a[slot, n] = (own[kept, :].astype(F32) + in_core[kept, :].astype(F32)).astype(keep_a.dtype)

        for_each(2 * nz, step)
        if i > DEPTH:
            pl.semaphore_wait(credit.at[1], 1)
        copy = send(out_a.at[slot], in_a.at[i % DEPTH], a_send.at[i], a_recv.at[i], place.peers(c)[0])
        copy.start()
        sent["a", i] = copy
        used_core(i)

    def stage_b(i):
        slot = i % 2
        sent["a", i].wait_recv()
        if i >= 3:
            sent["b", i - 2].wait_send()

        def step(zz):
            kept, gone = 2 * zz + mine_b, 2 * zz + 1 - mine_b
            out_b[slot, zz] = (keep_a[slot, gone].astype(F32) + in_a[i % DEPTH, gone].astype(F32)).astype(BF)
            keep_b[slot, zz] = (keep_a[slot, kept].astype(F32) + in_a[i % DEPTH, kept].astype(F32)).astype(keep_b.dtype)

        for_each(nz, step)
        if i + DEPTH <= last:
            pl.semaphore_signal(credit.at[1], inc=1, device_id=place.peers(c)[0], device_id_type=MESH)
        if i > DEPTH:
            pl.semaphore_wait(credit.at[2], 1)
        copy = send(out_b.at[slot], in_b.at[i % DEPTH], b_send.at[i], b_recv.at[i], place.peers(c)[1])
        copy.start()
        sent["b", i] = copy

    def stage_z(i):
        slot = i % 2
        sent["b", i].wait_recv()
        for j in range(nz):
            if j > 0 and i >= 3:
                sent["z", i - 2, j].wait_send()
            zz = place.up(j)
            value = keep_b[slot, zz].astype(F32) + in_b[i % DEPTH, zz].astype(F32)
            if j == 0:
                keep_z[slot] = value
                continue
            out_z[slot, j - 1] = value.astype(BF)
            copy = send(out_z.at[slot, j - 1], in_z.at[i - 1, j - 1], z_send.at[i, j - 1], z_recv.at[i, j - 1], place.above(j))
            copy.start()
            sent["z", i, j] = copy
        used_b(i)

    def used_b(i):
        if i + DEPTH <= last:
            pl.semaphore_signal(credit.at[2], inc=1, device_id=place.peers(c)[1], device_id_type=MESH)

    def share_at(i, first, count):
        return shares.at[back[i], pl.ds(pl.multiple_of(first * piece, 16), count * piece), cols]

    def stage_f(i):
        slot = i % 2
        if i == 0:
            sent["b", 0].wait_recv()
            value = keep_p[...] + in_p[2].astype(F32)
        else:
            value = keep_z[slot]
            for j in others:
                sent["z", i, j].wait_recv()
                value = value + in_z[i - 1, j - 1].astype(F32)
        if i >= 2:
            sent["f", i - 2].wait_send()
        final[slot] = value.astype(BF)
        here = pltpu.make_async_copy(final.at[slot], share_at(i, q, 1), f_own.at[i])
        here.start()
        copy = send(final.at[slot], share_at(i, q, 1), f_send.at[i], f_recv.at[i], place.peers(c)[0])
        copy.start()
        sent["f", i] = copy
        sent["own", i] = here

    def stage_g(i):
        sent["own", i].wait()
        sent["f", i].wait_recv()
        for n, which in enumerate((q, place.partner(c))):
            block = share_at(i, which, 1)
            copy = send(block, block, g_send.at[i, n], g_recv.at[i, n], place.peers(c)[1])
            copy.start()
            sent["g", i, n] = copy

    def stage_h(i):
        for n in range(2):
            sent["g", i, n].wait_recv()
        block = share_at(i, 0, 4)
        copy = send(block, block, h_send.at[i], h_recv.at[i], place.core)
        copy.start()
        sent["h", i] = copy

    def weight_grad(i, product):
        if i > 0:
            sent["core", i - 1].wait_send()

        def far(n):
            ms = span(n, tile_m)
            out_core[ms, :] = product(ms, core_cols).astype(BF)

        for_each(width // tile_m, far)
        stage_core(i)

        def near(n):
            ms = span(n, tile_m)
            own[ms, :] = product(ms, cols).astype(own.dtype)

        for_each(width // tile_m, near)
        if i == 0:
            stage_w()
        else:
            stage_a(i)

    weight_grad(0, lambda ms, ns: mm(buf[low, ms], buf[high, ns], TN))
    wait_all(act_out)

    def fetch_tap(t):
        return load_tap(place, shards[t], gathered.at[t], buf.at[tap_rows], tap_sem.at[0])

    def back_tap(n, k):
        offset = (k - KERNEL_TAPS // 2) * DILATION_STEP

        def step(i):
            m, r = i // down, pl.multiple_of(lax.rem(i, down) * tile_a, tile_a)
            rs = pl.ds(r, tile_a)
            first = pl.multiple_of(m * extent + halo - offset + r, DILATION_STEP)
            got = mm(grads[pl.ds(first, tile_a), :], buf[tap_rows, :], NT)
            got = got * wide(keep(item, m, KERNEL_TAPS - 1 - k, halo + r, tile_a), width)
            if n == 0:
                total[m, rs, :] = got
            else:
                total[m, rs, :] += got

        for_each(micro * down, step)

    tap_in = fetch_tap(2 + TAP_ORDER[0])
    for n, k in enumerate(TAP_ORDER):

        def masked(i, k=k):
            m, r = i // (rows // 128), lax.rem(i, rows // 128)
            first = pl.multiple_of(halo + r * 128, 128)
            mask = keep(item, m, k, first, 128)
            value = grads[at_rows(m, first, 128), :].astype(F32) * wide(mask, width)
            buf[span(i, 128), :] = value.astype(BF)

        for_each(micro * rows // 128, masked)
        start = halo + (k - KERNEL_TAPS // 2) * DILATION_STEP

        def product(ms, ns, start=start):
            got = None
            for m in range(micro):
                one = mm(held[m, pl.ds(start, rows), ms], buf[pl.ds(m * rows, rows), ns], TN)
                got = one if got is None else got + one
            return got

        weight_grad(n + 1, product)
        if n == 1:
            for m in range(micro):
                with_left(lambda m=m: grad_right(m).wait_recv())
                with_right(lambda m=m: grad_left(m).wait_recv())
        if n == 2:
            stage_wa()
        elif n == 3:
            stage_wb()
        elif n == 4:
            stage_f(0)
        wait_all(tap_in)
        back_tap(n, k)
        if n + 1 < len(TAP_ORDER):
            tap_in = fetch_tap(2 + TAP_ORDER[n + 1])
        if n == 3:
            stage_f(1)
        elif n == 4:
            stage_g(0)
            stage_g(1)
            stage_f(2)
        if n >= 2:
            stage_z(n - 1)
        if n >= 1:
            stage_b(n)

    entry_in = fetch_tap(0)
    one_in = [load(act_one.at[m], held.at[m, pl.ds(0, rows)], m) for m in range(micro)]
    block_load = [load(block_in.at[m], held.at[m, pl.ds(rows, rows)], micro + m) for m in range(micro)]
    for m in range(micro):
        sides(m == GRAD_RELAY, grad_right(m), grad_left(m), grad_hop, lambda copy: copy.wait_send())
    pull_in = [load(cotangent.at[m], grads.at[at_rows(m, 0, rows)], 2 * micro + m) for m in range(micro)]

    def norm_two_back(m, r, inner):
        n, inverse = normed(inner)
        u = n * vec(G2) + vec(S2)
        t = total[m, pl.ds(r, tile_r), :] * slope(u, phi(u))
        sums[G2] += fold(t * n)
        sums[S2] += fold(t)
        grad = pull_back(t, n, inverse, vec(G2)).astype(BF)
        buf[pl.ds(pl.multiple_of(m * rows + r, tile_r), tile_r), :] = grad
        sums[BE] += fold(grad.astype(F32))

    fetch(inner_one, 0).start()
    for m in range(micro):
        chunked(inner_one, m, norm_two_back)
        if m == 0:
            stage_z(4)
            stage_b(5)
        elif m == 1:
            stage_h(0)
            stage_h(1)
            stage_g(2)
            stage_f(3)
        else:
            stage_f(4)

    wait_all(one_in)

    def entry_product(ms, ns):
        got = None
        for m in range(micro):
            one = mm(held[m, pl.ds(0, rows), ms], buf[pl.ds(m * rows, rows), ns], TN)
            got = one if got is None else got + one
        return got

    weight_grad(last, entry_product)
    stage_h(2)
    stage_g(3)
    stage_z(5)
    three_again = [load(act_three.at[m], held.at[m, pl.ds(0, rows)], m) for m in range(micro)]

    wait_all(entry_in)

    def entry_back(i):
        m, r = i // down, lax.rem(i, down)
        total[m, span(r, tile_a), :] = mm(buf[span(i, tile_a), :], buf[tap_rows, :], NT)

    for_each(micro * down, entry_back)
    exit_in = fetch_tap(1)
    stage_h(3)
    stage_g(4)
    stage_f(5)
    stage_b(6)
    stores = []
    for m in range(micro):
        block_load[m].wait()
        pull_in[m].wait()

        def norm_one_back(i, m=m):
            rs = span(i, tile_r)
            n, inverse = normed(held[m, pl.ds(pl.multiple_of(rows + i * tile_r, tile_r), tile_r), :].astype(F32))
            u = n * vec(G1) + vec(S1)
            t = total[m, rs, :] * slope(u, phi(u))
            sums[G1] += fold(t * n)
            sums[S1] += fold(t)
            grad = pull_back(t, n, inverse, vec(G1))
            there = at_rows(m, i * tile_r, tile_r)
            weight = row_scale(item, weights, m, pl.multiple_of(halo + i * tile_r, tile_r), tile_r)
            pulled = grads[there, :].astype(F32) * wide(weight, width)
            grads[there, :] = (pulled + grad).astype(BF)

        for_each(rows // tile_r, norm_one_back)
        stores.append(store(grads.at[at_rows(m, 0, rows)], input_grad.at[m], micro + m))
        if m == 0:
            stage_h(4)
            stage_g(5)
            stage_z(6)
    stage_h(5)
    stage_f(6)

    vec_part[0] = jnp.zeros_like(vec_part[0])
    for r in range(sums.shape[0]):
        vec_part[0, r : r + 1, :] = jnp.sum(sums[r], axis=0, keepdims=True)

    def vec_stage(n, peer):
        copy = send(vec_part.at[n], vec_in.at[n], vec_send.at[n], vec_recv.at[n], peer)
        copy.start()
        sent["v", n] = copy

    def vec_add(n):
        sent["v", n].wait_recv()
        vec_part[n + 1] = vec_part[n] + vec_in[n]

    vec_stage(0, place.core)

    wait_all(exit_in)
    for m in range(micro):
        three_again[m].wait()

        def exit_step(i, m=m):
            got = mm(held[m, span(i, tile_a), :], buf[tap_rows, :], NT) + vec(BX)
            rs = pl.ds(pl.multiple_of(rows + i * tile_a, tile_a), tile_a)
            held[m, rs, :] = (held[m, rs, :].astype(F32) + got).astype(BF)

        for_each(down, exit_step)
        stores.append(store(held.at[m, pl.ds(rows, rows)], block_out.at[m], 2 * micro + m))
        vec_add(m)
        if m == 0:
            vec_stage(1, place.px)
            stage_g(6)
        elif m == 1:
            vec_stage(2, place.py)
            stage_h(6)
    for j in others:
        copy = send(vec_part.at[3], vec_in.at[2 + j], vec_send.at[2 + j], vec_recv.at[2 + j], place.above(j))
        copy.start()
        sent["v", 2 + j] = copy
    value = vec_part[3]
    for j in others:
        sent["v", 2 + j].wait_recv()
        value = value + vec_in[2 + j]
    vec_out[...] = value
    for i in range(taps):
        sent["h", i].wait_recv()
    wait_all(stores)

    for m in range(micro):
        sides(m == BLOCK_RELAY, block_right(m), block_left(m), block_hop, lambda copy: copy.wait_send())
    for side, here in ((0, at_end), (1, at_start)):

        @pl.when(here)
        def _(side=side):
            block_pass(side).wait_send()
            grad_pass(side).wait_send()

    for copy in pv + list(zg.values()) + list(ag.values()) + list(cg.values()):
        copy.wait_send()
    for (t, j), copies in bg.items():
        for copy in copies:
            if copy is not zg[t, j]:
                copy.wait_send()
    sent["core", last].wait_send()
    for key, copy in sent.items():
        late = key[0] in ("a", "b", "z", "f") and key[1] >= last - 1
        if late or key in (("a", 0), ("b", 0)) or key[0] in ("g", "h", "v", "w"):
            copy.wait_send()


def run_block(block_in, cotangent, lengths, weights, vectors, entry, conv, exit_t):
    micro, rows, width = block_in.shape
    halo = (KERNEL_TAPS // 2) * DILATION_STEP
    taps = conv.shape[0] + 2
    nz = lax.axis_size("fsdp")
    extent = rows + 2 * halo
    shard = entry.shape[0]
    piece = shard // 4
    half = width // 2
    shape = jax.ShapeDtypeStruct
    anywhere = pl.BlockSpec(memory_space=pl.ANY)
    near = pl.BlockSpec(memory_space=pltpu.VMEM)
    scalars = pl.BlockSpec(memory_space=pltpu.SMEM)
    dma = pltpu.SemaphoreType.DMA
    vmem = pltpu.VMEM
    flops = 2 * micro * rows * width * width * (3 * taps)
    return pl.pallas_call(
        block_kernel,
        out_shape=(
            shape((micro, rows, width), BF),
            shape((micro, rows, width), BF),
            shape((taps, shard, width), BF),
            shape((VECTORS, width), F32),
            shape((taps, width, width), BF),
            shape((micro, rows, width), BF),
            shape((micro, rows, width), F32),
            shape((micro, rows, width), BF),
            shape((micro, rows, width), F32),
            shape((micro, rows, width), BF),
            shape((4, halo, width), BF),
        ),
        in_specs=[anywhere, anywhere, scalars, scalars, near, anywhere, anywhere, anywhere],
        out_specs=(anywhere, anywhere, anywhere, near) + (anywhere,) * 7,
        scratch_shapes=[
            vmem((micro, extent, width), BF),
            vmem((micro, rows, width), F32),
            vmem((micro * extent, width), BF),
            vmem((micro * extent, width), BF),
            vmem((2, 128, width), F32),
            vmem((micro, extent, LANES), jnp.int32),
            vmem((VECTORS, width), F32),
            vmem((nz,) + vectors.shape, BF),
            vmem((9, 8, width), F32),
            vmem((width, half), BF),
            vmem((width, half), BF),
            vmem((width, half), BF),
            vmem((DEPTH, 2 * nz, piece, half), BF),
            vmem((2, 2 * nz, piece, half), BF),
            vmem((2, 2 * nz, piece, half), BF),
            vmem((DEPTH, nz, piece, half), BF),
            vmem((2, nz, piece, half), BF),
            vmem((2, nz, piece, half), BF),
            vmem((taps - 1, nz - 1, piece, half), BF),
            vmem((2, nz - 1, piece, half), BF),
            vmem((2, piece, half), F32),
            vmem((2, piece, half), BF),
            vmem((nz - 1, shard, half), BF),
            vmem((nz - 1, shard, half), BF),
            vmem((shard, half), F32),
            vmem((3, piece, half), BF),
            vmem((3, piece, half), BF),
            vmem((piece, half), F32),
            vmem((4, VECTORS, width), F32),
            vmem((2 + nz, VECTORS, width), F32),
            dma((nz - 1,)),
            dma((nz - 1,)),
            dma((taps, nz - 1)),
            dma((taps, nz - 1)),
            dma((taps, nz - 1)),
            dma((taps, nz - 1)),
            dma((taps, nz - 1, 2)),
            dma((taps, nz - 1, 2)),
            dma((taps, nz - 1)),
            dma((taps, nz - 1)),
            dma((4, micro)),
            dma((4, micro)),
            dma((4,)),
            dma((4,)),
            dma((4,)),
            dma((taps,)),
            dma((taps,)),
            dma((taps,)),
            dma((taps,)),
            dma((taps,)),
            dma((taps,)),
            dma((taps, nz - 1)),
            dma((taps, nz - 1)),
            dma((taps,)),
            dma((taps,)),
            dma((taps,)),
            dma((taps, 2)),
            dma((taps, 2)),
            dma((taps,)),
            dma((taps,)),
            dma((nz - 1,)),
            dma((nz - 1,)),
            dma((2 + nz,)),
            dma((2 + nz,)),
            dma((3 * micro,)),
            dma((3 * micro,)),
            dma((2, nz)),
            dma((2,)),
            pltpu.SemaphoreType.REGULAR((2,)),
            pltpu.SemaphoreType.REGULAR((3,)),
        ],
        compiler_params=pltpu.CompilerParams(
            collective_id=1, has_side_effects=True, vmem_limit_bytes=VMEM_MOST
        ),
        cost_estimate=pl.CostEstimate(flops=flops, bytes_accessed=160 << 20, transcendentals=0),
        name="residual_block",
    )(block_in, cotangent, lengths, weights, vectors, entry, conv, exit_t)


def kernels_on_device(
    block_in,
    cotangent,
    lengths,
    item_weights,
    first_gain,
    first_shift,
    entry_weight,
    entry_bias,
    middle_gain,
    middle_shift,
    conv_weight,
    conv_bias,
    final_gain,
    final_shift,
    exit_weight,
    exit_bias,
):
    shard = entry_weight.shape[0]
    rows = [
        first_gain,
        first_shift,
        entry_bias,
        middle_gain,
        middle_shift,
        conv_bias,
        final_gain,
        final_shift,
        exit_bias,
    ]
    padded = -(-shard // LANES) * LANES
    place = lax.broadcasted_iota(jnp.int32, (VECTORS, padded), 0)
    vectors = jnp.zeros((VECTORS, padded), BF)
    for r, row in enumerate(rows):
        vectors = jnp.where(place == r, jnp.pad(row, (0, padded - shard))[None, :], vectors)
    outputs, input_grads, shares, sums = run_block(
        block_in, cotangent, lengths, item_weights, vectors, entry_weight, conv_weight, exit_weight.T
    )[:4]
    own_sums = lax.dynamic_slice_in_dim(sums, lax.axis_index("fsdp") * shard, shard, axis=1)
    vec = [own_sums[r] for r in range(len(rows))]
    return (
        outputs,
        input_grads,
        vec[G1],
        vec[S1],
        shares[0].astype(F32),
        vec[BE],
        vec[G2],
        vec[S2],
        shares[2:].astype(F32),
        vec[BC],
        vec[G3],
        vec[S3],
        shares[1].astype(F32).T,
        vec[BX],
    )


def fits(mesh):
    return mesh.shape["seq"] == 8


def norm_act(values, scale_vec, shift_vec):
    row_mean = jnp.mean(values, axis=-1, keepdims=True)
    centred = values - row_mean
    spread = jnp.mean(centred * centred, axis=-1, keepdims=True)
    return jax.nn.gelu(
        centred * lax.rsqrt(spread + eps_norm) * scale_vec + shift_vec, approximate=False
    )


def column_product(left, right):
    return lax.dot_general(
        left, right, (((0,), (0,)), ((), ())), preferred_element_type=jnp.float32
    )


def row_product(left, right):
    return lax.dot_general(
        left, right, (((1,), (1,)), ((), ())), preferred_element_type=jnp.float32
    )


def items_at(residue_position, item_lengths, stream_len):
    item_places = jnp.arange(item_lengths.shape[0], dtype=jnp.int32)
    ends = jnp.sum(
        jnp.where(item_places[:, None] <= item_places[None, :], item_lengths[:, None], 0), axis=0
    )
    inside = (residue_position >= 0) & (residue_position < stream_len)
    seg_all = jnp.sum((residue_position[:, None] >= ends[None, :]).astype(jnp.int32), axis=1)
    return jnp.where(inside, seg_all, -1)


def stacked(extended, segment_extended, tap_offset, row_count, item_count):
    half_reach = KERNEL_TAPS // 2
    middle_tap = segment_extended[half_reach * tap_offset : half_reach * tap_offset + row_count]
    tap_parts = []
    for kernel_tap_index in range(KERNEL_TAPS):
        segment_tapped = segment_extended[
            kernel_tap_index * tap_offset : kernel_tap_index * tap_offset + row_count
        ]
        keep_mask = (
            (segment_tapped == middle_tap) & (segment_tapped >= 0) & (segment_tapped < item_count)
        )
        tap_parts.append(
            extended[kernel_tap_index * tap_offset : kernel_tap_index * tap_offset + row_count]
            * keep_mask[:, None].astype(extended.dtype)
        )
    return jnp.concatenate(tap_parts, axis=1)


def on_device(
    block_in,
    cotangent,
    lengths,
    item_weights,
    first_gain,
    first_shift,
    entry_weight,
    entry_bias,
    middle_gain,
    middle_shift,
    conv_weight,
    conv_bias,
    final_gain,
    final_shift,
    exit_weight,
    exit_bias,
):
    micro_count = block_in.shape[0]
    row_count = block_in.shape[1]
    model_width = block_in.shape[2]
    inner_width = entry_weight.shape[1]
    item_count = lengths.shape[2]
    sequence_count = lax.axis_size("seq")
    seq_place = lax.axis_index("seq")
    stream_len = row_count * sequence_count
    half_reach = KERNEL_TAPS // 2
    totals = [
        jnp.zeros((model_width,), jnp.float32),
        jnp.zeros((model_width,), jnp.float32),
        jnp.zeros((model_width, inner_width), jnp.float32),
        jnp.zeros((inner_width,), jnp.float32),
        jnp.zeros((inner_width,), jnp.float32),
        jnp.zeros((inner_width,), jnp.float32),
        jnp.zeros((KERNEL_TAPS, inner_width, inner_width), jnp.float32),
        jnp.zeros((inner_width,), jnp.float32),
        jnp.zeros((inner_width,), jnp.float32),
        jnp.zeros((inner_width,), jnp.float32),
        jnp.zeros((inner_width, model_width), jnp.float32),
        jnp.zeros((model_width,), jnp.float32),
    ]
    outputs = []
    input_grads = []
    for micro_index in range(micro_count):
        params = (
            lax.all_gather(first_gain, "fsdp", axis=0, tiled=True),
            lax.all_gather(first_shift, "fsdp", axis=0, tiled=True),
            lax.all_gather(entry_weight, "fsdp", axis=0, tiled=True),
            lax.all_gather(entry_bias, "fsdp", axis=0, tiled=True),
            lax.all_gather(middle_gain, "fsdp", axis=0, tiled=True),
            lax.all_gather(middle_shift, "fsdp", axis=0, tiled=True),
            lax.all_gather(conv_weight, "fsdp", axis=1, tiled=True),
            lax.all_gather(conv_bias, "fsdp", axis=0, tiled=True),
            lax.all_gather(final_gain, "fsdp", axis=0, tiled=True),
            lax.all_gather(final_shift, "fsdp", axis=0, tiled=True),
            lax.all_gather(exit_weight, "fsdp", axis=1, tiled=True),
            lax.all_gather(exit_bias, "fsdp", axis=0, tiled=True),
        )
        (
            gain_one,
            shift_one,
            weight_in,
            bias_in,
            gain_two,
            shift_two,
            weight_conv,
            bias_conv,
            gain_three,
            shift_three,
            weight_out,
            bias_out,
        ) = params
        item_lengths = lengths[micro_index, 0]
        weight_row = item_weights[micro_index, 0]
        own_position = seq_place * row_count + jnp.arange(row_count, dtype=jnp.int32)
        seg_own = items_at(own_position, item_lengths, stream_len)
        match = seg_own[:, None] == jnp.arange(item_count, dtype=jnp.int32)[None, :]
        row_scale = jnp.sum(jnp.where(match, weight_row[None, :], 0), axis=1).astype(jnp.float32)
        inputs = block_in[micro_index].astype(jnp.float32)
        normed_one, back_one = jax.vjp(
            norm_act, inputs, gain_one.astype(jnp.float32), shift_one.astype(jnp.float32)
        )
        act_one = normed_one.astype(jnp.bfloat16)
        inner_one = jnp.dot(
            act_one, weight_in, preferred_element_type=jnp.float32
        ) + bias_in.astype(jnp.float32)
        normed_two, back_two = jax.vjp(
            norm_act, inner_one, gain_two.astype(jnp.float32), shift_two.astype(jnp.float32)
        )
        second_activation = normed_two.astype(jnp.bfloat16)
        flat_conv = weight_conv.reshape(KERNEL_TAPS * inner_width, inner_width)
        flip_conv = (
            jnp.flip(weight_conv, 0)
            .transpose(0, 2, 1)
            .reshape(KERNEL_TAPS * inner_width, inner_width)
        )
        tap_offset = DILATION_STEP // sequence_count
        residue_position = (
            sequence_count
            * (
                jnp.arange(row_count + 2 * half_reach * tap_offset, dtype=jnp.int32)
                - half_reach * tap_offset
            )
            + seq_place
        )
        segment_extended = items_at(residue_position, item_lengths, stream_len)
        dealt = lax.all_to_all(
            second_activation.reshape(row_count // sequence_count, sequence_count, inner_width),
            "seq",
            split_axis=1,
            concat_axis=0,
            tiled=True,
        ).reshape(row_count, inner_width)
        extended = jnp.pad(dealt, ((half_reach * tap_offset, half_reach * tap_offset), (0, 0)))
        shifted_tap_rows = stacked(extended, segment_extended, tap_offset, row_count, item_count)
        dealt_out = (
            jnp.dot(shifted_tap_rows, flat_conv, preferred_element_type=jnp.float32)
            + bias_conv.astype(jnp.float32)
        ).astype(jnp.bfloat16)
        inner_two = lax.all_to_all(
            dealt_out.reshape(sequence_count, row_count // sequence_count, 1, inner_width),
            "seq",
            split_axis=0,
            concat_axis=2,
            tiled=True,
        ).reshape(row_count, inner_width)
        normed_three, back_three = jax.vjp(
            norm_act,
            inner_two.astype(jnp.float32),
            gain_three.astype(jnp.float32),
            shift_three.astype(jnp.float32),
        )
        act_three = normed_three.astype(jnp.bfloat16)
        branch = jnp.dot(
            act_three, weight_out, preferred_element_type=jnp.float32
        ) + bias_out.astype(jnp.float32)
        outputs.append((inputs + branch).astype(jnp.bfloat16))
        pulled = cotangent[micro_index].astype(jnp.float32) * row_scale[:, None]
        grad_branch = pulled.astype(jnp.bfloat16)
        sum_exit_weight = column_product(act_three, grad_branch)
        sum_exit_bias = jnp.sum(grad_branch.astype(jnp.float32), axis=0)
        grad_act_three = row_product(grad_branch, weight_out)
        grad_inner_two, sum_final_gain, sum_final_shift = back_three(grad_act_three)
        low_inner_two = grad_inner_two.astype(jnp.bfloat16)
        sum_conv_bias = jnp.sum(low_inner_two.astype(jnp.float32), axis=0)
        grad_dealt = lax.all_to_all(
            low_inner_two.reshape(row_count // sequence_count, sequence_count, inner_width),
            "seq",
            split_axis=1,
            concat_axis=0,
            tiled=True,
        ).reshape(row_count, inner_width)
        sum_conv_weight = column_product(shifted_tap_rows, grad_dealt)
        grad_ext = jnp.pad(grad_dealt, ((half_reach * tap_offset, half_reach * tap_offset), (0, 0)))
        dealt_back = jnp.dot(
            stacked(grad_ext, segment_extended, tap_offset, row_count, item_count),
            flip_conv,
            preferred_element_type=jnp.float32,
        )
        grad_act_two = lax.all_to_all(
            dealt_back.reshape(sequence_count, row_count // sequence_count, 1, inner_width),
            "seq",
            split_axis=0,
            concat_axis=2,
            tiled=True,
        ).reshape(row_count, inner_width)
        grad_inner_one, sum_middle_gain, sum_middle_shift = back_two(grad_act_two)
        low_inner_one = grad_inner_one.astype(jnp.bfloat16)
        sum_entry_weight = column_product(act_one, low_inner_one)
        sum_entry_bias = jnp.sum(low_inner_one.astype(jnp.float32), axis=0)
        grad_act_one = row_product(low_inner_one, weight_in)
        grad_inputs, sum_first_gain, sum_first_shift = back_one(grad_act_one)
        input_grads.append((pulled + grad_inputs).astype(jnp.bfloat16))
        fresh = (
            sum_first_gain,
            sum_first_shift,
            sum_entry_weight,
            sum_entry_bias,
            sum_middle_gain,
            sum_middle_shift,
            sum_conv_weight.reshape(KERNEL_TAPS, inner_width, inner_width),
            sum_conv_bias,
            sum_final_gain,
            sum_final_shift,
            sum_exit_weight,
            sum_exit_bias,
        )
        totals = [left + right for left, right in zip(totals, fresh)]
    shares = (
        lax.psum_scatter(totals[0], "fsdp", scatter_dimension=0, tiled=True),
        lax.psum_scatter(totals[1], "fsdp", scatter_dimension=0, tiled=True),
        lax.psum_scatter(totals[2], "fsdp", scatter_dimension=0, tiled=True),
        lax.psum_scatter(totals[3], "fsdp", scatter_dimension=0, tiled=True),
        lax.psum_scatter(totals[4], "fsdp", scatter_dimension=0, tiled=True),
        lax.psum_scatter(totals[5], "fsdp", scatter_dimension=0, tiled=True),
        lax.psum_scatter(totals[6], "fsdp", scatter_dimension=1, tiled=True),
        lax.psum_scatter(totals[7], "fsdp", scatter_dimension=0, tiled=True),
        lax.psum_scatter(totals[8], "fsdp", scatter_dimension=0, tiled=True),
        lax.psum_scatter(totals[9], "fsdp", scatter_dimension=0, tiled=True),
        lax.psum_scatter(totals[10], "fsdp", scatter_dimension=1, tiled=True),
        lax.psum_scatter(totals[11], "fsdp", scatter_dimension=0, tiled=True),
    )
    result = lax.psum(
        (
            shares[0],
            shares[1],
            shares[2],
            shares[3],
            shares[4],
            shares[5],
            shares[6],
            shares[7],
            shares[8],
            shares[9],
            shares[10],
            shares[11],
        ),
        "seq",
    )
    return (
        jnp.stack(outputs),
        jnp.stack(input_grads),
        result[0],
        result[1],
        result[2],
        result[3],
        result[4],
        result[5],
        result[6],
        result[7],
        result[8],
        result[9],
        result[10],
        result[11],
    )


def solution(mesh):
    in_specs = (
        P(None, ("fsdp", "seq"), None),
        P(None, ("fsdp", "seq"), None),
        P(None, "fsdp", None),
        P(None, "fsdp", None),
        P("fsdp"),
        P("fsdp"),
        P("fsdp", None),
        P("fsdp"),
        P("fsdp"),
        P("fsdp"),
        P(None, "fsdp", None),
        P("fsdp"),
        P("fsdp"),
        P("fsdp"),
        P(None, "fsdp"),
        P("fsdp"),
    )
    out_specs = (
        P(None, ("fsdp", "seq"), None),
        P(None, ("fsdp", "seq"), None),
        P("fsdp"),
        P("fsdp"),
        P("fsdp", None),
        P("fsdp"),
        P("fsdp"),
        P("fsdp"),
        P(None, "fsdp", None),
        P("fsdp"),
        P("fsdp"),
        P("fsdp"),
        P(None, "fsdp"),
        P("fsdp"),
    )
    body = kernels_on_device if fits(mesh) else on_device
    return jax.shard_map(
        body, mesh=mesh, in_specs=in_specs, out_specs=out_specs, check_vma=False
    )
```
